128 devices in a mesh: expert: 32 (over y, z, core), shard: 4 (over x).
Axes of the slice: x: 4, y: 4, z: 4, core: 2. Of those that a mesh axis runs over, the one named last changes fastest.
Arguments:
- tokens: bfloat16 [16384, 768], P(('expert', 'shard')), may hold values from -6 to 6
- seq_lengths: int32 [128, 4], P(('expert', 'shard')), may hold values from 1 to 96, 128 in all within a row
- routes: int32 [16384, 2], P(('expert', 'shard')), may hold values from 0 to 63, all different within a row; in each aligned block of 128 rows (0 to 127, 128 to 255, ...) at most 6 rows name the same one
- gain_attn: bfloat16 [768], P('shard'), may hold values from 0.25 to 1.75
- w_query: bfloat16 [768, 768], P('shard'), may hold values from -0.21875 to 0.21875
- w_key: bfloat16 [768, 768], P('shard'), may hold values from -0.21875 to 0.21875
- w_value: bfloat16 [768, 768], P('shard'), may hold values from -0.21875 to 0.21875
- w_output: bfloat16 [768, 768], P('shard'), may hold values from -0.875 to 0.875
- rel_bias: bfloat16 [12, 32], P('shard'), may hold values from -3 to 3
- gain_moe: bfloat16 [768], P('shard'), may hold values from 0.25 to 1.75
- w_router: bfloat16 [768, 64], P('shard'), may hold values from -0.21875 to 0.21875
- w_in: bfloat16 [64, 768, 3072], P('expert', None, 'shard'), may hold values from -0.21875 to 0.21875
- w_out: bfloat16 [64, 3072, 768], P('expert', 'shard'), may hold values from -0.109375 to 0.109375
- cotangent: bfloat16 [16384, 768], P(('expert', 'shard')), may hold values from -6 to 6
Outputs:
- result: bfloat16 [16384, 768], P(('expert', 'shard'))
- grad_tokens: float32 [16384, 768], P(('expert', 'shard'))
- grad_gain_attn: float32 [768], P('shard')
- grad_w_query: float32 [768, 768], P('shard')
- grad_w_key: float32 [768, 768], P('shard')
- grad_w_value: float32 [768, 768], P('shard')
- grad_w_output: float32 [768, 768], P('shard')
- grad_rel_bias: float32 [12, 32], P('shard')
- grad_gain_moe: float32 [768], P('shard')
- grad_w_router: float32 [768, 64], P('shard')
- grad_w_in: float32 [64, 768, 3072], P('expert', None, 'shard')
- grad_w_out: float32 [64, 3072, 768], P('expert', 'shard')
The draws below stay inside these ranges and needn't reach their ends.
Inputs may be any that keep to these rules, and one draw needn't show every extreme that they name: `seq_lengths`: each rank's 4 lengths sum to 128; its sequences lie one after another in its rows; the largest length is exactly 96. `routes`: each row names two different experts. Among the rows of one rank no expert is named more than 6 times, a bound that some block reaches.
All inputs are finite; a program needn't handle non-finite values.
Results may differ from the reference program's by a relative error of at most 0.025.
Values may be sent and summed in bfloat16 or wider, within the bound.
No kernel may reach another device: no remote copies, remote signals or barrier semaphores. Data moves between devices by JAX's collectives and lax.ppermute only.
A program may use at most 128 MiB of HBM per device.

```python
import math
import jax
import jax.numpy as jnp
import numpy as np
from jax import lax

D = 768
HEADS = 12
HEAD_DIM = 64
FF = 3072
BUCKETS = 32
TOK_DEV = 128
SEQ_DEV = 4
MAXLEN = 96
EXPERTS = 64
CAP = 6
RANKS = 128
TOKENS = 16384


def block_levels(stream_key, dims, pieces, low, top_value):
    loudness = 1.0
    for dim, shards_of in pieces:
        steps = jax.random.uniform(jax.random.fold_in(jax.random.fold_in(stream_key, 6), dim), (shards_of,), jnp.float32, low / len(pieces), top_value / len(pieces))
        loudness = loudness * jnp.repeat(jnp.exp(steps), dims[dim] // shards_of).reshape((-1,) + (1,) * (len(dims) - 1 - dim))
    return loudness


def split_up(amount, total, reach, lean):
    weights = [(1 << 20) // math.isqrt(standing ** lean) + 1 for standing in range(2, amount + 1)]
    spare, holding = total - reach - (amount - 1), [1] * (amount - 1)
    while spare > 0:
        movable = [i for i in range(amount - 1) if holding[i] < reach]
        whole, remaining = sum([weights[i] for i in movable]), spare
        for i in movable:
            extra = min(reach - holding[i], max(1, remaining * weights[i] // whole), spare)
            holding[i] = holding[i] + extra
            spare = spare - extra
    return np.array([reach] + holding)


def ragged_sizes(key, count, total, bound, slope):
    if count == 2:
        one = jax.random.randint(key, (), max(1, total - bound), min(bound, total - 1) + 1)
        return jnp.stack([one, total - one])
    sizes = jnp.asarray(split_up(count, total, bound, slope), jnp.int32)
    pairs = (count - 1) // 2
    donor, receiver = sizes[1:1 + 2 * pairs:2], sizes[2:2 + 2 * pairs:2]
    margin = jnp.minimum(donor - 1, bound - receiver)
    moved = jax.random.randint(jax.random.fold_in(key, 1), (pairs,), 0, 1 << 20) % (margin + 1)
    sizes = sizes.at[1:1 + 2 * pairs:2].set(donor - moved).at[2:2 + 2 * pairs:2].set(receiver + moved)
    return sizes[jax.random.permutation(jax.random.fold_in(key, 2), count)]


def shared_out(rng, own, number, rows, count, top, reach, lean):
    ranking = jax.random.permutation(rng, count)
    heavy_load, common = shares(count, rows * top, reach, lean, True), shares(count, rows * top, reach, lean, False)
    places = jnp.arange(count)

    def named(tallies, rotation):
        used = int((tallies > 0).sum())
        fixed = max(1, used // 4)
        shifted = fixed + (places - fixed + rotation * (used - fixed)) % max(1, count - fixed)
        return jnp.zeros((count,), jnp.int32).at[ranking[jnp.where(places < fixed, places, shifted)]].set(jnp.asarray(tallies, jnp.int32))

    tallies = jnp.where(number % 4 == 0, named(heavy_load, number // 4), named(common, number - number // 4 - 1))
    mixed = jax.random.permutation(jax.random.fold_in(own, 3), count)
    source_of, receiver = mixed[0:count // 2 * 2:2], mixed[1:count // 2 * 2:2]
    room = jnp.minimum(tallies[source_of] - 1, reach - tallies[receiver]) // 2
    room = jnp.where((source_of == ranking[0]) | (receiver == ranking[0]) | (tallies[receiver] == 0), 0, jnp.maximum(room, 0))
    shifted = jax.random.randint(jax.random.fold_in(own, 4), (count // 2,), 0, 1 << 20) % (room + 1)
    tallies = tallies.at[source_of].add(-shifted).at[receiver].add(shifted)
    items = jnp.searchsorted(jnp.cumsum(tallies), jnp.arange(rows * top), side="right").astype(jnp.int32)
    grid = items.reshape(top, rows).T
    grid = grid[jax.random.permutation(jax.random.fold_in(own, 1), rows)]
    rotation = jax.random.randint(jax.random.fold_in(own, 2), (rows, 1), 0, top)
    return jnp.take_along_axis(grid, (jnp.arange(top)[None, :] + rotation) % top, axis=1)


def shares(amount, total, most, skew, full):
    weights = [(1 << 20) // math.isqrt(standing ** skew) + 1 for standing in range(1, amount + 1)]
    largest = most if full else min(most, max(-(-total // amount), total * weights[0] // sum(weights)))
    least = 1 if total - largest >= amount - 1 else 0
    given, rest = [largest] + [least] * (amount - 1), total - largest - least * (amount - 1)
    while rest > 0:
        movable = [i for i in range(1, amount) if given[i] < largest] or [i for i in range(1, amount) if given[i] < most]
        mass, budget = sum([weights[i] for i in movable]), rest
        for i in movable:
            extra = min(most - given[i], max(1, budget * weights[i] // mass), rest)
            given[i] = given[i] + extra
            rest = rest - extra
    return np.array(given)


def bell_draw(rng, dims, width, limit, split=(), kind=jnp.bfloat16):
    result = jax.random.normal(rng, dims, jnp.float32) * width
    if len(split) > 0:
        result = block_levels(rng, dims, split, -0.22, 0.18) * result
    return jnp.clip(result, min=-limit, max=limit).astype(kind)


def setup_inputs(seed: int = 0) -> dict:
    key_of = jax.random.split(jax.random.key(seed), 15)
    tokens = bell_draw(key_of[0], (TOKENS, D), 1.0, 6.0, ((0, 128),))
    seq_lengths = jax.vmap(lambda own: ragged_sizes(own, SEQ_DEV, TOK_DEV, MAXLEN, 2))(jax.random.split(key_of[1], RANKS)).reshape((RANKS, SEQ_DEV)).astype(jnp.int32)
    routes_keys = jax.random.split(jax.random.fold_in(key_of[2], 1), TOKENS // TOK_DEV)
    routes_turns = jax.random.permutation(jax.random.fold_in(key_of[2], 3), TOKENS // TOK_DEV)
    routes = jax.vmap(lambda own, number: shared_out(jax.random.fold_in(key_of[2], 2), own, number, TOK_DEV, EXPERTS, 2, CAP, 1))(routes_keys, routes_turns).reshape((TOKENS, 2))
    gain_attn = jnp.clip(1.0 + 0.15 * jax.random.normal(key_of[3], (D,), jnp.float32), 0.25, 1.75).astype(jnp.bfloat16)
    w_query = bell_draw(key_of[4], (D, D), D ** -0.5, 0.21875, ((0, 4),))
    w_key = bell_draw(key_of[5], (D, D), D ** -0.5, 0.21875, ((0, 4),))
    w_value = bell_draw(key_of[6], (D, D), D ** -0.5, 0.21875, ((0, 4),))
    w_output = bell_draw(key_of[7], (D, D), (D // 16) ** -0.5, 0.875, ((0, 4),))
    rel_bias = bell_draw(key_of[8], (HEADS, BUCKETS), 0.5, 3.0, ((0, 4),))
    gain_moe = jnp.clip(1.0 + 0.15 * jax.random.normal(key_of[9], (D,), jnp.float32), 0.25, 1.75).astype(jnp.bfloat16)
    w_router = bell_draw(key_of[10], (D, EXPERTS), D ** -0.5, 0.21875, ((0, 4),))
    w_in = bell_draw(key_of[11], (EXPERTS, D, FF), D ** -0.5, 0.21875, ((0, 32), (2, 4)))
    w_out = bell_draw(key_of[12], (EXPERTS, FF, D), FF ** -0.5, 0.109375, ((0, 32), (1, 4)))
    cotangent = bell_draw(key_of[13], (TOKENS, D), 1.0, 6.0, ((0, 128),))
    return {"tokens": tokens, "seq_lengths": seq_lengths, "routes": routes, "gain_attn": gain_attn, "w_query": w_query, "w_key": w_key, "w_value": w_value, "w_output": w_output, "rel_bias": rel_bias, "gain_moe": gain_moe, "w_router": w_router, "w_in": w_in, "w_out": w_out, "cotangent": cotangent}


@jax.custom_vjp
def low(v):
    return lax.optimization_barrier(v.astype(jnp.bfloat16)).astype(jnp.float32)

@jax.custom_vjp
def low_back(v):
    return v

def low_keep(v):
    return (low(v), None)

def low_pass(kept, grad):
    return (grad,)

def back_keep(v):
    return (v, None)

def back_low(kept, grad):
    return (low(grad),)
low.defvjp(low_keep, low_pass)
low_back.defvjp(back_keep, back_low)
epsilon = 1e-06
bucket_edges = list(range(1, 17)) + [int(math.ceil(16.0 * 8.0 ** ((bucket_level - 16) / 16.0))) for bucket_level in range(17, 32)]

def row_segments(lengths, row_count):
    sequence_ends = jnp.cumsum(lengths).astype(jnp.int32)
    positions = jnp.arange(row_count, dtype=jnp.int32)
    return lax.optimization_barrier(jnp.sum((positions[:, None] >= sequence_ends[None, :]).astype(jnp.int32), axis=1)).astype(jnp.int32)

def capacity_slots(route_block, expert_count):
    order_block = jnp.arange(route_block.shape[0], dtype=jnp.int32)
    named_rows = lax.optimization_barrier(jnp.sum((route_block[:, :, None] == jnp.arange(expert_count, dtype=jnp.int32)).astype(jnp.int32), axis=1)).astype(jnp.int32)
    earlier = (order_block[None, :] < order_block[:, None]).astype(jnp.int32)
    counts = lax.optimization_barrier(jnp.sum(earlier[:, :, None] * named_rows[None, :, :], axis=1)).astype(jnp.int32)
    return jnp.take_along_axis(counts, route_block, axis=1).astype(jnp.int32)

def rms_scale(values):
    return lax.rsqrt(lax.optimization_barrier(jnp.mean(values * values, axis=1, keepdims=True)) + epsilon)

def reference(tokens, seq_lengths, routes, gain_attn, w_query, w_key, w_value, w_output, rel_bias, gain_moe, w_router, w_in, w_out, cotangent):
    highest = lax.Precision.HIGHEST
    score_scale = 1.0 / math.sqrt(HEAD_DIM)
    segments = jax.vmap(lambda lengths: row_segments(lengths, TOK_DEV))(seq_lengths)
    positions = jnp.arange(TOK_DEV, dtype=jnp.int32)
    distance = positions[:, None] - positions[None, :]
    bucket = lax.optimization_barrier(jnp.sum((distance[:, :, None] >= jnp.array(bucket_edges, dtype=jnp.int32)).astype(jnp.int32), axis=2)).astype(jnp.int32)
    allowed = (segments[:, :, None] == segments[:, None, :]) & (distance >= 0)[None]
    slots = lax.map(lambda route_block: capacity_slots(route_block, EXPERTS), routes.reshape(RANKS, TOK_DEV, 2)).reshape(TOKENS, 2)
    rank_of_row = jnp.arange(TOKENS, dtype=jnp.int32) // TOK_DEV
    places = ((routes * RANKS + rank_of_row[:, None]) * CAP + slots).reshape(-1).astype(jnp.int32)

    def forward(inputs, gain_one, query_w, key_w, value_w, output_w, bias_table, gain_two, router_w, expert_in, expert_out):
        hidden_one = low(inputs * rms_scale(inputs) * gain_one)
        queries = low_back(low(jnp.dot(hidden_one, query_w, precision=highest)))
        key_rows = low_back(low(jnp.dot(hidden_one, key_w, precision=highest)))
        value_rows = low_back(low(jnp.dot(hidden_one, value_w, precision=highest)))
        bias_full = bias_table[:, bucket]

        def attend(block_args):
            query_blk, key_blk, value_blk, allowed_blk = block_args
            raw_scores = jnp.einsum('ihd,jhd->hij', query_blk, key_blk, precision=highest) * score_scale + bias_full
            scores = jnp.where(allowed_blk[None], low_back(raw_scores), -1000000000.0)
            attention = jax.nn.softmax(scores, axis=2)
            return jnp.einsum('hij,jhd->ihd', low(attention), value_blk, precision=highest)
        head_shape = (RANKS, TOK_DEV, HEADS, HEAD_DIM)
        attended = lax.map(jax.checkpoint(attend), (queries.reshape(head_shape), key_rows.reshape(head_shape), value_rows.reshape(head_shape), allowed))
        attended = low_back(low(attended.reshape(TOKENS, D)))
        middle = inputs + low_back(jnp.dot(attended, output_w, precision=highest))
        moe_in = low(middle * rms_scale(middle) * gain_two)
        logits = low_back(jnp.dot(moe_in, router_w, precision=highest))
        chosen = jnp.take_along_axis(logits, routes, axis=1)
        gate_weights = jax.nn.softmax(chosen, axis=1)
        outgoing = jnp.zeros((EXPERTS * RANKS * CAP, D), jnp.float32).at[places].set(jnp.repeat(moe_in, 2, axis=0))
        outgoing = low_back(outgoing)

        def expert_apply(block_args):
            row_block, weight_in, weight_out = block_args
            pre_active = low_back(jnp.dot(row_block, weight_in, precision=highest))
            active = low(jax.nn.gelu(pre_active, approximate=True))
            return low_back(low(jnp.dot(active, weight_out, precision=highest)))
        returned = lax.map(jax.checkpoint(expert_apply), (outgoing.reshape(EXPERTS, RANKS * CAP, D), expert_in, expert_out)).reshape(EXPERTS * RANKS * CAP, D)
        picked = returned[places].reshape(TOKENS, 2, D)
        return middle + lax.optimization_barrier(jnp.sum(gate_weights[:, :, None] * picked, axis=1))
    floats = tuple((argument.astype(jnp.float32) for argument in (tokens, gain_attn, w_query, w_key, w_value, w_output, rel_bias, gain_moe, w_router, w_in, w_out)))
    outputs, backward = jax.vjp(forward, *floats)
    grads = backward(cotangent.astype(jnp.float32))
    return (outputs.astype(jnp.bfloat16), grads[0], grads[1], grads[2], grads[3], grads[4], grads[5], grads[6], grads[7], grads[8], grads[9], grads[10])
```

```python
import math

import jax
import jax.numpy as jnp
from jax import lax
from jax.experimental import pallas as pl
from jax.experimental.pallas import tpu as pltpu
from jax.sharding import Mesh, PartitionSpec as P

epsilon = 1e-06
bucket_edges = list(range(1, 17)) + [
    int(math.ceil(16.0 * 8.0 ** ((bucket_level - 16) / 16.0))) for bucket_level in range(17, 32)
]


def row_segments(lengths, row_count):
    sequence_ends = jnp.cumsum(lengths)
    positions = jnp.arange(row_count, dtype=jnp.int32)
    return jnp.sum((positions[:, None] >= sequence_ends[None, :]).astype(jnp.int32), axis=1)


def position_tables(row_count, bucket_count):
    positions = jnp.arange(row_count, dtype=jnp.int32)
    distance = positions[:, None] - positions[None, :]
    edge_values = jnp.array(bucket_edges, dtype=jnp.int32)
    bucket = jnp.sum((distance[:, :, None] >= edge_values).astype(jnp.int32), axis=2)
    onehot = (bucket[:, :, None] == jnp.arange(bucket_count, dtype=jnp.int32)).astype(jnp.bfloat16)
    return (distance, onehot)


def capacity_slots(route_block, expert_count):
    order_block = jnp.arange(route_block.shape[0], dtype=jnp.int32)
    named_rows = jnp.sum(
        (route_block[:, :, None] == jnp.arange(expert_count, dtype=jnp.int32)).astype(jnp.bfloat16),
        axis=1,
    )
    earlier = (order_block[None, :] < order_block[:, None]).astype(jnp.bfloat16)
    counts = jnp.dot(earlier, named_rows, preferred_element_type=jnp.float32)
    match = route_block[:, :, None] == jnp.arange(expert_count, dtype=jnp.int32)
    return jnp.sum(jnp.where(match, counts[:, None, :], 0.0), axis=2).astype(jnp.int32)


def gelu_tanh(argument):
    return jax.nn.gelu(argument, approximate=True)


def rms_backward(grad_normed, normed, scale):
    return scale * (grad_normed - normed * jnp.mean(grad_normed * normed, axis=1, keepdims=True))


def shift_x(block, step):
    ranks = lax.axis_size("x")
    return lax.ppermute(block, "x", [(i, (i + step) % ranks) for i in range(ranks)])


def swap_core(block):
    return lax.ppermute(block, "c", [(0, 1), (1, 0)])


def along_x(block):
    return [block, shift_x(block, 1), shift_x(block, 2), shift_x(block, 3)]


def pack_kernel(core_ref, *refs):
    mats, out, sems = refs[:4], refs[4], refs[5]
    half = mats[0].shape[0] // 2
    start = pl.multiple_of(core_ref[0] * half, half)
    copies = [
        pltpu.make_async_copy(m.at[pl.ds(start, half)], out.at[pl.ds(k * half, half)], sems.at[k])
        for k, m in enumerate(mats)
    ]
    for c in copies:
        c.start()
    for c in copies:
        c.wait()


def assemble_kernel(place_ref, *refs):
    mats, near, far, outs, sems = refs[:4], refs[4:7], refs[7], refs[8:12], refs[12]
    shard, core = place_ref[0], place_ref[1]
    rows = mats[0].shape[0]
    half = rows // 2
    copies = []
    for k in range(4):
        begin = pl.multiple_of(shard * rows, rows)
        copies.append((mats[k], outs[k].at[pl.ds(begin, rows)]))
    for r in range(1, 4):
        begin = lax.rem(shard + (4 - r), 4) * rows
        mine = pl.multiple_of(begin + core * half, half)
        other = pl.multiple_of(begin + (1 - core) * half, half)
        for k in range(4):
            part = pl.ds(k * half, half)
            copies.append((near[r - 1].at[part], outs[k].at[pl.ds(mine, half)]))
            part = pl.ds(((r - 1) * 4 + k) * half, half)
            copies.append((far.at[part], outs[k].at[pl.ds(other, half)]))
    copies = [pltpu.make_async_copy(s, d, sems.at[i]) for i, (s, d) in enumerate(copies)]
    for c in copies:
        c.start()
    for c in copies:
        c.wait()


ANYWHERE = pl.BlockSpec(memory_space=pl.ANY)
SCALARS = pl.BlockSpec(memory_space=pltpu.SMEM)
WHOLE = pl.BlockSpec(memory_space=pltpu.VMEM)
ROOM = pltpu.CompilerParams(vmem_limit_bytes=56 * 1024 * 1024)


def gather_weights(mats):
    shard = lax.axis_index("x").astype(jnp.int32)
    core = lax.axis_index("c").astype(jnp.int32)
    rows, cols = mats[0].shape
    half = rows // 2
    sent = pl.pallas_call(
        pack_kernel,
        out_shape=jax.ShapeDtypeStruct((4 * half, cols), jnp.bfloat16),
        in_specs=[SCALARS] + [ANYWHERE] * 4,
        out_specs=ANYWHERE,
        scratch_shapes=[pltpu.SemaphoreType.DMA((4,))],
        name="pack",
    )(core[None], *mats)
    near = along_x(sent)[1:]
    far = swap_core(jnp.concatenate(near, axis=0))
    full = jax.ShapeDtypeStruct((4 * rows, cols), jnp.bfloat16)
    return pl.pallas_call(
        assemble_kernel,
        out_shape=[full] * 4,
        in_specs=[SCALARS] + [ANYWHERE] * 8,
        out_specs=[ANYWHERE] * 4,
        scratch_shapes=[pltpu.SemaphoreType.DMA((28,))],
        name="assemble",
    )(jnp.stack([shard, core]), *mats, *near, far)


def dispatch_kernel(places_ref, *refs):
    pieces, out_ref = refs[:4], refs[4]
    rows = out_ref.shape[0]
    features = 768
    wide = pieces[0].shape[1] > features
    tokens = pieces[0].shape[0]
    line = jnp.concatenate([p[...] for p in pieces], axis=0)
    places = places_ref[...]
    row = lax.broadcasted_iota(jnp.int32, (rows, 4 * tokens), 0)
    for e in range(2):
        at = row + e * rows
        pick = ((at == places[0:1]) | (at == places[1:2])).astype(jnp.float32).astype(jnp.bfloat16)
        out_ref[:, e * features : (e + 1) * features] = jnp.dot(
            pick, line[:, :features], preferred_element_type=jnp.float32
        ).astype(jnp.bfloat16)
        if wide:
            ids = jnp.dot(pick, line[:, features:], preferred_element_type=jnp.float32)
            if e == 0:
                extra = ids
            else:
                extra = extra + pltpu.roll(ids, 2, axis=1)
    if wide:
        out_ref[:, 2 * features :] = extra.astype(jnp.bfloat16)


def dispatch(places, pieces, rows):
    features = 768
    lanes = 2 * features + pieces[0].shape[1] - features
    return pl.pallas_call(
        dispatch_kernel,
        out_shape=jax.ShapeDtypeStruct((rows, lanes), jnp.bfloat16),
        in_specs=[WHOLE] * 5,
        out_specs=WHOLE,
        compiler_params=ROOM,
        name="dispatch",
    )(places, *pieces)


def chosen_logit(logits, ids):
    lanes = lax.broadcasted_iota(jnp.int32, logits.shape, 1)
    return jnp.sum(jnp.where(lanes == ids, logits, 0.0), axis=1, keepdims=True)


def gate_pair(first, second):
    top = jnp.maximum(first, second)
    one, two = jnp.exp(first - top), jnp.exp(second - top)
    total = one + two
    return one / total, two / total


def expert_kernel(
    own_ref, x_ref, g_ref, ids_ref, in_ref, out_ref, router_ref, ret_ref, act_ref, pre_ref, arr_ref
):
    f32, bf16 = jnp.float32, jnp.bfloat16
    e = pl.program_id(0)
    own = own_ref[0] + e
    features = x_ref.shape[1]
    step = 256
    slope = math.sqrt(2.0 / math.pi)
    last = (((1,), (1,)), ((), ()))

    def chunk(i, carry):
        at = pl.ds(pl.multiple_of(i * step, step), step)
        x = x_ref[at, :]
        ids = ids_ref[at, :].astype(f32)
        lanes = lax.broadcasted_iota(jnp.int32, ids.shape, 1)
        mine = (lanes == 2 * e) | (lanes == 2 * e + 1)
        other = jnp.sum(jnp.where(mine, ids, 0.0), axis=1, keepdims=True).astype(jnp.int32) - own
        logits = jnp.dot(x, router_ref[...], preferred_element_type=f32)
        gate, _ = gate_pair(chosen_logit(logits, own), chosen_logit(logits, other))
        pre = jnp.dot(x, in_ref[0], preferred_element_type=f32)
        tanh = jnp.tanh(slope * (pre + 0.044715 * (pre * pre * pre)))
        active = (0.5 * pre * (1.0 + tanh)).astype(bf16)
        act_ref[0, at, :] = active
        ret_ref[at, :features] = jnp.dot(active, out_ref[0], preferred_element_type=f32).astype(bf16)
        rows = (gate * g_ref[at, :].astype(f32)).astype(bf16)
        arr_ref[0, at, :] = rows
        back = lax.dot_general(rows, out_ref[0], last, preferred_element_type=f32)
        rise = 0.5 * (1.0 + tanh) + 0.5 * pre * (1.0 - tanh * tanh) * (
            slope * (1.0 + 3.0 * 0.044715 * (pre * pre))
        )
        grad = (back * rise).astype(bf16)
        pre_ref[0, at, :] = grad
        ret_ref[at, features:] = lax.dot_general(
            grad, in_ref[0], last, preferred_element_type=f32
        ).astype(bf16)
        return carry

    lax.fori_loop(0, x_ref.shape[0] // step, chunk, 0)


def experts(own, arrived, grad_wide, w_in, w_out, router_w):
    rows = arrived.shape[0]
    features = w_in.shape[1]
    hidden = w_in.shape[2]
    bf16 = jnp.bfloat16
    per = lambda n: pl.BlockSpec((rows, n), lambda e: (0, e))
    weights = lambda a, b: pl.BlockSpec((1, a, b), lambda e: (e, 0, 0))
    return pl.pallas_call(
        expert_kernel,
        grid=(2,),
        out_shape=[
            jax.ShapeDtypeStruct((rows, 4 * features), bf16),
            jax.ShapeDtypeStruct((2, rows, hidden), bf16),
            jax.ShapeDtypeStruct((2, rows, hidden), bf16),
            jax.ShapeDtypeStruct((2, rows, features), bf16),
        ],
        in_specs=[
            SCALARS,
            per(features),
            per(features),
            pl.BlockSpec((rows, 128), lambda e: (0, 2 * features // 128)),
            weights(features, hidden),
            weights(hidden, features),
            pl.BlockSpec(router_w.shape, lambda e: (0, 0)),
        ],
        out_specs=[
            per(2 * features),
            weights(rows, hidden),
            weights(rows, hidden),
            weights(rows, features),
        ],
        compiler_params=ROOM,
        name="experts",
    )(own[None], arrived, grad_wide, grad_wide, w_in, w_out, router_w)


def combine_kernel(places_ref, routes_ref, router_ref, ret_ref, *refs):
    f32, bf16 = jnp.float32, jnp.bfloat16
    grads, moes, outs = refs[:4], refs[4:8], refs[8:12]
    tokens = moes[0].shape[0]
    features = moes[0].shape[1]
    rows = ret_ref.shape[0]
    lane = lax.broadcasted_iota(jnp.int32, (tokens, rows), 1)
    tail_lane = lax.broadcasted_iota(jnp.int32, (tokens, 128), 1)
    for r in range(4):
        here = slice(r * tokens, (r + 1) * tokens)
        logits = jnp.dot(moes[r][...], router_ref[...], preferred_element_type=f32)
        gates = gate_pair(
            chosen_logit(logits, routes_ref[here, 0:1]), chosen_logit(logits, routes_ref[here, 1:2])
        )
        total = jnp.zeros((tokens, features), f32)
        back = jnp.zeros((tokens, features), f32)
        tail = jnp.zeros((tokens, 128), f32)
        grad = grads[r][:, :features].astype(f32)
        picks = [
            [
                (lane + e * rows == places_ref[here, k : k + 1]).astype(f32).astype(bf16)
                for e in range(2)
            ]
            for k in range(2)
        ]
        for k in range(2):
            got = jnp.zeros((tokens, features), f32)
            for e in range(2):
                at = 2 * e * features
                got = got + jnp.dot(
                    picks[k][e], ret_ref[:, at : at + features], preferred_element_type=f32
                )
            total = total + gates[k] * got
            dots = jnp.sum(grad * got, axis=1, keepdims=True)
            high = dots.astype(bf16).astype(f32)
            tail = jnp.where(tail_lane == k, high, tail)
            tail = jnp.where(tail_lane == 2 + k, dots - high, tail)
        for e in range(2):
            at = (2 * e + 1) * features
            back = back + jnp.dot(
                picks[0][e] + picks[1][e],
                ret_ref[:, at : at + features],
                preferred_element_type=f32,
            )
        outs[r][:, :features] = total.astype(bf16)
        outs[r][:, features : 2 * features] = back.astype(bf16)
        outs[r][:, 2 * features :] = tail.astype(bf16)


def combine(places, routes, router_w, returned, grads, moes):
    tokens, features = moes[0].shape
    return pl.pallas_call(
        combine_kernel,
        out_shape=[jax.ShapeDtypeStruct((tokens, 2 * features + 128), jnp.bfloat16)] * 4,
        in_specs=[WHOLE] * 12,
        out_specs=[WHOLE] * 4,
        compiler_params=ROOM,
        name="combine",
    )(places, routes, router_w, returned, *grads, *moes)


def layer(
    tokens,
    seq_lengths,
    routes,
    gain_attn,
    w_query,
    w_key,
    w_value,
    w_output,
    rel_bias,
    gain_moe,
    w_router,
    w_in,
    w_out,
    cotangent,
):
    row_count, features = tokens.shape
    shard_rows = w_query.shape[0]
    expert_count = w_router.shape[1]
    bucket_count = rel_bias.shape[1]
    head_count = 4 * rel_bias.shape[0]
    head_size = features // head_count
    capacity = 3 * row_count // expert_count
    score_scale = 1.0 / math.sqrt(head_size)
    head_shape = (row_count, head_count, head_size)
    bias_size = rel_bias.size
    f32 = jnp.float32
    bf16 = jnp.bfloat16

    small = jnp.concatenate(
        [
            w_router,
            gain_attn[:, None],
            gain_moe[:, None],
            jnp.pad(rel_bias.reshape(-1), (0, shard_rows - bias_size))[:, None],
            jnp.zeros((shard_rows, 128 - expert_count - 3), bf16),
        ],
        axis=1,
    )
    query_w, key_w, value_w, output_w = gather_weights((w_query, w_key, w_value, w_output))
    shard = lax.axis_index("x")
    rest = jnp.take(jnp.stack(along_x(small)), (shard - jnp.arange(4)) % 4, axis=0)
    router_w = rest[:, :, :expert_count].reshape(features, expert_count)
    gain_one = rest[:, :, expert_count].reshape(features)
    gain_two = rest[:, :, expert_count + 1].reshape(features)
    bias_table = rest[:, :bias_size, expert_count + 2].reshape(head_count, bucket_count)

    route_rows = jnp.pad(routes.astype(bf16), ((0, 0), (0, 126)))
    line_grads = along_x(jnp.concatenate([cotangent, route_rows], axis=1))
    line_routes = jnp.concatenate(
        [piece[:, features : features + 2] for piece in line_grads], axis=0
    ).astype(jnp.int32)
    line_slots = jnp.concatenate(
        [
            capacity_slots(line_routes[r * row_count : (r + 1) * row_count], expert_count)
            + r * capacity
            for r in range(4)
        ],
        axis=0,
    )
    owners = expert_count // 2
    group = 4 * capacity
    slot_rows = owners * group
    line_places = (line_routes % 2) * slot_rows + (line_routes // 2) * group + line_slots

    def to_owners(pieces):
        return lax.all_to_all(
            dispatch(line_places.T, pieces, slot_rows), ("y", "z", "c"), 0, 0, tiled=True
        )

    grad_wide = to_owners(line_grads)
    first_expert = 2 * lax.axis_index(("y", "z", "c")).astype(jnp.int32)

    inputs = tokens.astype(f32)
    scale_one = lax.rsqrt(jnp.mean(inputs * inputs, axis=1, keepdims=True) + epsilon)
    normed_one = inputs * scale_one
    gain_one_f = gain_one.astype(f32)
    hidden_one = (normed_one * gain_one_f).astype(bf16)
    queries = jnp.dot(hidden_one, query_w, preferred_element_type=f32).astype(bf16)
    key_rows = jnp.dot(hidden_one, key_w, preferred_element_type=f32).astype(bf16)
    value_rows = jnp.dot(hidden_one, value_w, preferred_element_type=f32).astype(bf16)
    query_heads = queries.reshape(head_shape)
    key_heads = key_rows.reshape(head_shape)
    value_heads = value_rows.reshape(head_shape)
    segments = row_segments(seq_lengths[0], row_count)
    distance, onehot = position_tables(row_count, bucket_count)
    allowed = (segments[:, None] == segments[None, :]) & (distance >= 0)
    position_bias = jnp.einsum("ijb,hb->hij", onehot, bias_table, preferred_element_type=f32)

    def scores_of():
        raw_scores = (
            jnp.einsum("ihd,jhd->hij", query_heads, key_heads, preferred_element_type=f32)
            * score_scale
            + position_bias
        )
        return jnp.where(allowed[None], raw_scores, -1000000000.0)

    scores = scores_of()
    row_max = jnp.max(scores, axis=2, keepdims=True)
    log_total = row_max + jnp.log(jnp.sum(jnp.exp(scores - row_max), axis=2, keepdims=True))
    attention = jnp.exp(scores - log_total)
    attended = (
        jnp.einsum("hij,jhd->ihd", attention.astype(bf16), value_heads, preferred_element_type=f32)
        .reshape(row_count, features)
        .astype(bf16)
    )
    middle = inputs + jnp.dot(attended, output_w, preferred_element_type=f32)
    scale_two = lax.rsqrt(jnp.mean(middle * middle, axis=1, keepdims=True) + epsilon)
    normed_two = middle * scale_two
    gain_two_f = gain_two.astype(f32)
    moe_in = (normed_two * gain_two_f).astype(bf16)

    line_moe = along_x(moe_in)
    arrived = to_owners(line_moe)
    ret, active, grad_pre, grad_arrived = experts(
        first_expert, arrived, grad_wide, w_in, w_out, router_w
    )
    returned = lax.all_to_all(ret, ("y", "z", "c"), 0, 0, tiled=True)
    grad_w_out = jnp.einsum("erf,erd->efd", active, grad_arrived, preferred_element_type=f32)
    grad_w_in = jnp.einsum(
        "red,erf->edf",
        arrived.reshape(slot_rows, 2, features),
        grad_pre,
        preferred_element_type=f32,
    )

    bundle = combine(line_places, line_routes, router_w, returned, line_grads, line_moe)
    home = bundle[0][:, : 2 * features + 4].astype(f32)
    for r in range(1, 4):
        home = home + shift_x(bundle[r], -r)[:, : 2 * features + 4].astype(f32)
    outputs = middle + home[:, :features]
    result = outputs.astype(bf16)
    grad_gates = home[:, 2 * features : 2 * features + 2] + home[:, 2 * features + 2 :]
    logits = jnp.dot(moe_in, router_w, preferred_element_type=f32)
    lanes = jnp.arange(expert_count, dtype=jnp.int32)
    gate_weights = jax.nn.softmax(
        jnp.sum(jnp.where(routes[:, :, None] == lanes, logits[:, None, :], 0.0), axis=2), axis=1
    )
    grad_out = cotangent.astype(f32)
    gate_mix = jnp.sum(gate_weights * grad_gates, axis=1, keepdims=True)
    grad_chosen = gate_weights * (grad_gates - gate_mix)
    expert_match = (routes[:, :, None] == jnp.arange(expert_count, dtype=jnp.int32)).astype(f32)
    grad_logits = jnp.sum(grad_chosen[:, :, None] * expert_match, axis=1).astype(bf16)
    grad_moe = home[:, features : 2 * features] + jnp.dot(
        grad_logits, router_w.T, preferred_element_type=f32
    )
    grad_router = jnp.dot(moe_in.T, grad_logits, preferred_element_type=f32)
    grad_gain_two = jnp.sum(grad_moe * normed_two, axis=0)
    grad_middle = grad_out + rms_backward(grad_moe * gain_two_f, normed_two, scale_two)
    grad_branch = grad_middle.astype(bf16)
    grad_output_w = jnp.dot(attended.T, grad_branch, preferred_element_type=f32)
    grad_attended = (
        jnp.dot(grad_branch, output_w.T, preferred_element_type=f32).astype(bf16).reshape(head_shape)
    )
    grad_values = (
        jnp.einsum(
            "hij,ihd->jhd", attention.astype(bf16), grad_attended, preferred_element_type=f32
        )
        .astype(bf16)
        .reshape(row_count, features)
    )
    grad_attention = jnp.einsum(
        "ihd,jhd->hij", grad_attended, value_heads, preferred_element_type=f32
    )
    grad_scores = (
        attention * (grad_attention - jnp.sum(attention * grad_attention, axis=2, keepdims=True))
    ).astype(bf16)
    grad_bias = jnp.einsum("hij,ijb->hb", grad_scores, onehot, preferred_element_type=f32)
    grad_queries = (
        (
            jnp.einsum("hij,jhd->ihd", grad_scores, key_heads, preferred_element_type=f32)
            * score_scale
        )
        .astype(bf16)
        .reshape(row_count, features)
    )
    grad_keys = (
        (
            jnp.einsum("hij,ihd->jhd", grad_scores, query_heads, preferred_element_type=f32)
            * score_scale
        )
        .astype(bf16)
        .reshape(row_count, features)
    )
    grad_query_w = jnp.dot(hidden_one.T, grad_queries, preferred_element_type=f32)
    grad_key_w = jnp.dot(hidden_one.T, grad_keys, preferred_element_type=f32)
    grad_value_w = jnp.dot(hidden_one.T, grad_values, preferred_element_type=f32)
    grad_hidden = jnp.dot(grad_queries, query_w.T, preferred_element_type=f32)
    grad_hidden = grad_hidden + jnp.dot(grad_keys, key_w.T, preferred_element_type=f32)
    grad_hidden = grad_hidden + jnp.dot(grad_values, value_w.T, preferred_element_type=f32)
    grad_gain_one = jnp.sum(grad_hidden * normed_one, axis=0)
    grad_tokens = grad_middle + rms_backward(grad_hidden * gain_one_f, normed_one, scale_one)

    core = lax.axis_index("c")
    piece = shard_rows // 8
    wide = features + 128
    bias_column = jnp.pad(grad_bias.reshape(4, bias_size), ((0, 0), (0, shard_rows - bias_size)))
    small_grads = jnp.concatenate(
        [
            grad_router,
            grad_gain_one[:, None],
            grad_gain_two[:, None],
            bias_column.reshape(-1, 1),
        ],
        axis=1,
    ).astype(bf16)
    small_grads = jnp.pad(small_grads, ((0, 0), (0, 128 - small_grads.shape[1])))
    none = jnp.zeros_like(small_grads)
    stacked = jnp.stack(
        [
            jnp.concatenate([g.astype(bf16), s], axis=1)
            for g, s in (
                (grad_query_w, small_grads),
                (grad_key_w, none),
                (grad_value_w, none),
                (grad_output_w, none),
            )
        ]
    ).reshape(4, 4, 4, 2, piece, wide)
    kept = lax.dynamic_index_in_dim(stacked, core, 3, keepdims=False)
    given = lax.dynamic_index_in_dim(stacked, 1 - core, 3, keepdims=False)
    paired = (kept.astype(f32) + swap_core(given).astype(f32)).astype(bf16)
    paired = paired.transpose(0, 2, 1, 3, 4).reshape(64 * piece, wide)
    spread = lax.all_to_all(paired, ("y", "z", "x"), 0, 0, tiled=True)
    mine = jnp.sum(spread.reshape(64, piece, wide).astype(f32), axis=0).astype(bf16)
    totals = lax.all_to_all(
        jnp.broadcast_to(mine[None], (32, piece, wide)).reshape(32 * piece, wide),
        ("y", "z", "c"),
        0,
        0,
        tiled=True,
    ).reshape(4, shard_rows, wide)
    small_totals = totals[0, :, features:].astype(f32)
    totals = totals[:, :, :features].astype(f32)
    router_total = small_totals[:, :expert_count]
    gain_one_total = small_totals[:, expert_count]
    gain_two_total = small_totals[:, expert_count + 1]
    bias_total = small_totals[:bias_size, expert_count + 2].reshape(rel_bias.shape)
    return (
        result,
        grad_tokens,
        gain_one_total,
        totals[0],
        totals[1],
        totals[2],
        totals[3],
        bias_total,
        gain_two_total,
        router_total,
        grad_w_in,
        grad_w_out,
    )


def solution(mesh):
    cube = Mesh(mesh.devices.reshape(4, 4, 2, 4), ("y", "z", "c", "x"))
    expert = ("y", "z", "c")
    everyone = ("y", "z", "c", "x")
    placed = (
        P(everyone, None),
        P(everyone, None),
        P(everyone, None),
        P("x"),
        P("x", None),
        P("x", None),
        P("x", None),
        P("x", None),
        P("x", None),
        P("x"),
        P("x", None),
        P(expert, None, "x"),
        P(expert, "x", None),
        P(everyone, None),
    )
    return jax.shard_map(
        layer,
        mesh=cube,
        in_specs=placed,
        out_specs=(
            P(everyone, None),
            P(everyone, None),
            P("x"),
            P("x", None),
            P("x", None),
            P("x", None),
            P("x", None),
            P("x", None),
            P("x"),
            P("x", None),
            P(expert, None, "x"),
            P(expert, "x", None),
        ),
        check_vma=False,
    )
```

```python
import functools
import math

import jax
import jax.numpy as jnp
from jax import lax
from jax.experimental import pallas as pl
from jax.experimental.pallas import tpu as pltpu
from jax.sharding import Mesh, PartitionSpec as P

epsilon = 1e-06
bucket_edges = list(range(1, 17)) + [
    int(math.ceil(16.0 * 8.0 ** ((bucket_level - 16) / 16.0))) for bucket_level in range(17, 32)
]


def row_segments(lengths, row_count):
    sequence_ends = jnp.cumsum(lengths)
    positions = jnp.arange(row_count, dtype=jnp.int32)
    return jnp.sum((positions[:, None] >= sequence_ends[None, :]).astype(jnp.int32), axis=1)


def position_tables(row_count, bucket_count):
    positions = jnp.arange(row_count, dtype=jnp.int32)
    distance = positions[:, None] - positions[None, :]
    edge_values = jnp.array(bucket_edges, dtype=jnp.int32)
    bucket = jnp.sum((distance[:, :, None] >= edge_values).astype(jnp.int32), axis=2)
    onehot = (bucket[:, :, None] == jnp.arange(bucket_count, dtype=jnp.int32)).astype(jnp.bfloat16)
    return (distance, onehot)


def capacity_slots(route_block, expert_count):
    order_block = jnp.arange(route_block.shape[0], dtype=jnp.int32)
    named_rows = jnp.sum(
        (route_block[:, :, None] == jnp.arange(expert_count, dtype=jnp.int32)).astype(jnp.bfloat16),
        axis=1,
    )
    earlier = (order_block[None, :] < order_block[:, None]).astype(jnp.bfloat16)
    counts = jnp.dot(earlier, named_rows, preferred_element_type=jnp.float32)
    match = route_block[:, :, None] == jnp.arange(expert_count, dtype=jnp.int32)
    return jnp.sum(jnp.where(match, counts[:, None, :], 0.0), axis=2).astype(jnp.int32)


def shift_x(block, step):
    ranks = lax.axis_size("x")
    return lax.ppermute(block, "x", [(i, (i + step) % ranks) for i in range(ranks)])


def swap_core(block):
    return lax.ppermute(block, "c", [(0, 1), (1, 0)])


def along_x(block):
    return [block, shift_x(block, 1), shift_x(block, 2), shift_x(block, 3)]


def pack_kernel(core_ref, *refs):
    mats, outs, sems = refs[:4], refs[4:6], refs[6]
    half = mats[0].shape[0] // 2
    start = pl.multiple_of(core_ref[0] * half, half)
    spots = [outs[0].at[pl.ds(k * half, half)] for k in range(3)] + [outs[1]]
    copies = [
        pltpu.make_async_copy(m.at[pl.ds(start, half)], spot, sems.at[k])
        for k, (m, spot) in enumerate(zip(mats, spots))
    ]
    for c in copies:
        c.start()
    for c in copies:
        c.wait()


def start_copies(pairs, sems):
    copies = [pltpu.make_async_copy(s, d, sems.at[i]) for i, (s, d) in enumerate(pairs)]
    for c in copies:
        c.start()
    return copies


def block_copies(shard, core, mats, near, far, outs):
    rows = mats[0].shape[0]
    half = rows // 2
    pairs = []
    for k, (mat, out) in enumerate(zip(mats, outs)):
        begin = pl.multiple_of(shard * rows, rows)
        pairs.append((mat, out.at[pl.ds(begin, rows)]))
        part = pl.ds(k * half, half)
        for r in range(1, 4):
            begin = lax.rem(shard + (4 - r), 4) * rows
            mine = pl.multiple_of(begin + core * half, half)
            other = pl.multiple_of(begin + (1 - core) * half, half)
            pairs.append((near[r - 1].at[part], out.at[pl.ds(mine, half)]))
            pairs.append((far[r - 1].at[part], out.at[pl.ds(other, half)]))
    return pairs


def norm_scale(x):
    return lax.rsqrt(jnp.mean(x * x, axis=1, keepdims=True) + epsilon)


def head_half(block, side):
    lanes = lax.broadcasted_iota(jnp.int32, block.shape, 1)
    keep = (lanes < 64) if side == 0 else (lanes >= 64)
    return jnp.where(keep, block, jnp.zeros_like(block))


LAST = (((1,), (1,)), ((), ()))
FIRST = (((0,), (0,)), ((), ()))


def attend_kernel(place_ref, tokens_ref, gain_ref, bias_ref, *refs):
    f32, bf16 = jnp.float32, jnp.bfloat16
    mats, near, far = refs[:3], refs[3:6], refs[6:9]
    weights = refs[10:13]
    hidden_ref, q_ref, k_ref, v_ref, probs_ref, attended_ref, sems = refs[13:20]
    copies = start_copies(
        block_copies(place_ref[0], place_ref[1], mats, near, far, weights), sems
    )
    x = tokens_ref[...].astype(f32)
    hidden = (x * norm_scale(x) * gain_ref[...].astype(f32)).astype(bf16)
    hidden_ref[...] = hidden
    for n, (w, out) in enumerate(zip(weights, (q_ref, k_ref, v_ref))):
        for c in copies[7 * n : 7 * n + 7]:
            c.wait()
        out[...] = jnp.dot(hidden, w[...], preferred_element_type=f32).astype(bf16)
    heads = bias_ref.shape[0]
    for pair in range(heads // 2):
        lanes = slice(pair * 128, pair * 128 + 128)
        q, k, v = q_ref[:, lanes], k_ref[:, lanes], v_ref[:, lanes]
        total = jnp.zeros(q.shape, f32)
        for side in range(2):
            h = 2 * pair + side
            scores = lax.dot_general(q, head_half(k, side), LAST, preferred_element_type=f32)
            scores = scores * 0.125 + bias_ref[h]
            top = jnp.max(scores, axis=1, keepdims=True)
            grown = jnp.exp(scores - top)
            probs = grown / jnp.sum(grown, axis=1, keepdims=True)
            probs_ref[h] = probs
            total = total + jnp.dot(
                probs.astype(bf16), head_half(v, side), preferred_element_type=f32
            )
        attended_ref[:, lanes] = total.astype(bf16)


def middle_kernel(place_ref, tokens_ref, gain_ref, attended_ref, *refs):
    f32 = jnp.float32
    mats, near, far = refs[:1], refs[1:4], refs[4:7]
    weight, middle_ref, moe_ref, sems = refs[8:12]
    copies = start_copies(
        block_copies(place_ref[0], place_ref[1], mats, near, far, [weight]), sems
    )
    for c in copies:
        c.wait()
    middle = tokens_ref[...].astype(f32) + jnp.dot(
        attended_ref[...], weight[...], preferred_element_type=f32
    )
    middle_ref[...] = middle
    moe_ref[...] = (middle * norm_scale(middle) * gain_ref[...].astype(f32)).astype(jnp.bfloat16)


def backward_kernel(
    core_ref,
    tokens_ref,
    cotangent_ref,
    gain_one_ref,
    gain_two_ref,
    routes_ref,
    router_ref,
    middle_ref,
    moe_ref,
    attended_ref,
    hidden_ref,
    q_ref,
    k_ref,
    v_ref,
    probs_ref,
    *refs,
):
    f32, bf16 = jnp.float32, jnp.bfloat16
    homes, weights = refs[:4], refs[4:8]
    result_ref, tokens_out, kept_ref, given_ref, scores_ref, router_out, gains_out = refs[8:15]
    held, grads_ref, sems = refs[15:18]
    copies = start_copies([(w, held.at[i]) for i, w in enumerate(weights)], sems)
    features = tokens_ref.shape[1]
    core = core_ref[0]

    def leave(mat, left, right):
        grad = lax.dot_general(left, right, FIRST, preferred_element_type=f32).astype(bf16)
        grads_ref[...] = grad
        for x in range(4):
            low = grads_ref[x * 192 : x * 192 + 96, :]
            high = grads_ref[x * 192 + 96 : x * 192 + 192, :]
            at = (mat * 4 + x) * 96
            kept_ref[at : at + 96, :features] = jnp.where(core == 0, low, high)
            given_ref[at : at + 96, :features] = jnp.where(core == 0, high, low)

    home = homes[0][...].astype(f32)
    for piece in homes[1:]:
        home = home + piece[...].astype(f32)
    middle = middle_ref[...]
    result_ref[...] = (middle + home[:, :features]).astype(bf16)
    tail = home[:, 2 * features :]
    lane = lax.broadcasted_iota(jnp.int32, tail.shape, 1)
    grad_gates = [
        jnp.sum(jnp.where((lane == k) | (lane == 2 + k), tail, 0.0), axis=1, keepdims=True)
        for k in range(2)
    ]
    moe = moe_ref[...]
    logits = jnp.dot(moe, router_ref[...], preferred_element_type=f32)
    ids = [routes_ref[:, k : k + 1] for k in range(2)]
    gates = gate_pair(chosen_logit(logits, ids[0]), chosen_logit(logits, ids[1]))
    mix = gates[0] * grad_gates[0] + gates[1] * grad_gates[1]
    spots = lax.broadcasted_iota(jnp.int32, logits.shape, 1)
    grad_logits = jnp.zeros(logits.shape, f32)
    for k in range(2):
        grad_logits = jnp.where(spots == ids[k], gates[k] * (grad_gates[k] - mix), grad_logits)
    grad_logits = grad_logits.astype(bf16)
    grad_moe = home[:, features : 2 * features] + lax.dot_general(
        grad_logits, router_ref[...], LAST, preferred_element_type=f32
    )
    router_out[...] = lax.dot_general(moe, grad_logits, FIRST, preferred_element_type=f32)
    scale = norm_scale(middle)
    normed = middle * scale
    gains_out[1:2, :] = jnp.sum(grad_moe * normed, axis=0, keepdims=True)
    inner = grad_moe * gain_two_ref[...].astype(f32)
    grad_middle = cotangent_ref[...].astype(f32) + scale * (
        inner - normed * jnp.mean(inner * normed, axis=1, keepdims=True)
    )
    branch = grad_middle.astype(bf16)
    leave(3, attended_ref[...], branch)
    copies[3].wait()
    grad_attended = lax.dot_general(branch, held[3], LAST, preferred_element_type=f32).astype(bf16)
    grad_q, grad_k, grad_v = [], [], []
    for pair in range(probs_ref.shape[0] // 2):
        lanes = slice(pair * 128, pair * 128 + 128)
        q, k, v = q_ref[:, lanes], k_ref[:, lanes], v_ref[:, lanes]
        grad = grad_attended[:, lanes]
        parts = [jnp.zeros(q.shape, f32) for _ in range(3)]
        for side in range(2):
            h = 2 * pair + side
            probs = probs_ref[h]
            grad_half = head_half(grad, side)
            parts[2] = parts[2] + lax.dot_general(
                probs.astype(bf16), grad_half, FIRST, preferred_element_type=f32
            )
            grad_probs = lax.dot_general(grad_half, v, LAST, preferred_element_type=f32)
            grad_scores = (
                probs * (grad_probs - jnp.sum(probs * grad_probs, axis=1, keepdims=True))
            ).astype(bf16)
            scores_ref[h] = grad_scores
            parts[0] = parts[0] + jnp.dot(
                grad_scores, head_half(k, side), preferred_element_type=f32
            )
            parts[1] = parts[1] + lax.dot_general(
                grad_scores, head_half(q, side), FIRST, preferred_element_type=f32
            )
        grad_q.append((parts[0] * 0.125).astype(bf16))
        grad_k.append((parts[1] * 0.125).astype(bf16))
        grad_v.append(parts[2].astype(bf16))
    hidden = hidden_ref[...]
    grad_hidden = jnp.zeros(hidden.shape, f32)
    for n, parts in enumerate((grad_q, grad_k, grad_v)):
        grad = jnp.concatenate(parts, axis=1)
        leave(n, hidden, grad)
        copies[n].wait()
        grad_hidden = grad_hidden + lax.dot_general(
            grad, held[n], LAST, preferred_element_type=f32
        )
    x = tokens_ref[...].astype(f32)
    scale = norm_scale(x)
    normed = x * scale
    gains_out[0:1, :] = jnp.sum(grad_hidden * normed, axis=0, keepdims=True)
    inner = grad_hidden * gain_one_ref[...].astype(f32)
    tokens_out[...] = grad_middle + scale * (
        inner - normed * jnp.mean(inner * normed, axis=1, keepdims=True)
    )


ANYWHERE = pl.BlockSpec(memory_space=pl.ANY)
SCALARS = pl.BlockSpec(memory_space=pltpu.SMEM)
WHOLE = pl.BlockSpec(memory_space=pltpu.VMEM)
ROOM = pltpu.CompilerParams(vmem_limit_bytes=56 * 1024 * 1024)


def send_weights(mats):
    core = lax.axis_index("c").astype(jnp.int32)
    rows, cols = mats[0].shape
    half = rows // 2
    sent = pl.pallas_call(
        pack_kernel,
        out_shape=[jax.ShapeDtypeStruct((n * half, cols), jnp.bfloat16) for n in (3, 1)],
        in_specs=[SCALARS] + [ANYWHERE] * 4,
        out_specs=[WHOLE] * 2,
        scratch_shapes=[pltpu.SemaphoreType.DMA((4,))],
        name="pack",
    )(core[None], *mats)
    return [along_x(part)[1:] for part in sent]


def attend(where, tokens, gain, bias, mats, near, far, after):
    rows, cols = mats[0].shape
    full = jax.ShapeDtypeStruct((4 * rows, cols), jnp.bfloat16)
    state = jax.ShapeDtypeStruct(tokens.shape, jnp.bfloat16)
    return pl.pallas_call(
        attend_kernel,
        out_shape=[full] * 3 + [state] * 4 + [jax.ShapeDtypeStruct(bias.shape, jnp.float32), state],
        in_specs=[SCALARS] + [WHOLE] * 3 + [ANYWHERE] * 10,
        out_specs=[WHOLE] * 9,
        scratch_shapes=[pltpu.SemaphoreType.DMA((21,))],
        compiler_params=ROOM,
        name="attend",
    )(where, tokens, gain, bias, *mats, *near, *far, after)


def to_middle(where, tokens, gain, attended, mat, near, far, after):
    rows, cols = mat.shape
    return pl.pallas_call(
        middle_kernel,
        out_shape=[
            jax.ShapeDtypeStruct((4 * rows, cols), jnp.bfloat16),
            jax.ShapeDtypeStruct(tokens.shape, jnp.float32),
            jax.ShapeDtypeStruct(tokens.shape, jnp.bfloat16),
        ],
        in_specs=[SCALARS] + [WHOLE] * 3 + [ANYWHERE] * 8,
        out_specs=[WHOLE] * 3,
        scratch_shapes=[pltpu.SemaphoreType.DMA((7,))],
        compiler_params=ROOM,
        name="middle",
    )(where, tokens, gain, attended, mat, *near, *far, after)


def backward(core, *arrays):
    tokens, router_w, probs = arrays[0], arrays[5], arrays[13]
    count, features = tokens.shape
    bf16, f32 = jnp.bfloat16, jnp.float32
    shape = jax.ShapeDtypeStruct
    return pl.pallas_call(
        backward_kernel,
        out_shape=[
            shape((count, features), bf16),
            shape((count, features), f32),
            shape((2 * features, features), bf16),
            shape((2 * features, features), bf16),
            shape(probs.shape, bf16),
            shape(router_w.shape, f32),
            shape((2, features), f32),
        ],
        in_specs=[SCALARS] + [WHOLE] * 18 + [ANYWHERE] * 4,
        out_specs=[WHOLE] * 7,
        scratch_shapes=[
            pltpu.VMEM((4, features, features), bf16),
            pltpu.VMEM((features, features), bf16),
            pltpu.SemaphoreType.DMA((4,)),
        ],
        compiler_params=ROOM,
        name="backward",
    )(core, *arrays)


def dispatch_kernel(places_ref, *refs):
    pieces, out_ref = refs[:4], refs[4]
    rows = out_ref.shape[0]
    features = 768
    wide = pieces[0].shape[1] > features
    tokens = pieces[0].shape[0]
    line = jnp.concatenate([p[...] for p in pieces], axis=0)
    places = places_ref[...]
    row = lax.broadcasted_iota(jnp.int32, (rows, 4 * tokens), 0)
    for e in range(2):
        at = row + e * rows
        pick = ((at == places[0:1]) | (at == places[1:2])).astype(jnp.float32).astype(jnp.bfloat16)
        out_ref[:, e * features : (e + 1) * features] = jnp.dot(
            pick, line[:, :features], preferred_element_type=jnp.float32
        ).astype(jnp.bfloat16)
        if wide:
            extra_lanes = line[:, features : features + 128]
            lanes = lax.broadcasted_iota(jnp.int32, extra_lanes.shape, 1)
            extra_lanes = jnp.where(lanes < 2, extra_lanes, jnp.zeros_like(extra_lanes))
            ids = jnp.dot(pick, extra_lanes, preferred_element_type=jnp.float32)
            if e == 0:
                extra = ids
            else:
                extra = extra + pltpu.roll(ids, 2, axis=1)
    if wide:
        out_ref[:, 2 * features :] = extra.astype(jnp.bfloat16)


def dispatch(places, pieces, rows):
    features = 768
    lanes = 2 * features + (128 if pieces[0].shape[1] > features else 0)
    return pl.pallas_call(
        dispatch_kernel,
        out_shape=jax.ShapeDtypeStruct((rows, lanes), jnp.bfloat16),
        in_specs=[WHOLE] * 5,
        out_specs=WHOLE,
        compiler_params=ROOM,
        name="dispatch",
    )(places, *pieces)


def chosen_logit(logits, ids):
    lanes = lax.broadcasted_iota(jnp.int32, logits.shape, 1)
    return jnp.sum(jnp.where(lanes == ids, logits, 0.0), axis=1, keepdims=True)


def gate_pair(first, second):
    top = jnp.maximum(first, second)
    one, two = jnp.exp(first - top), jnp.exp(second - top)
    total = one + two
    return one / total, two / total


def expert_kernel(
    own_ref, x_ref, g_ref, ids_ref, in_ref, out_ref, router_ref, ret_ref, act_ref, pre_ref, arr_ref
):
    f32, bf16 = jnp.float32, jnp.bfloat16
    e = pl.program_id(0)
    own = own_ref[0] + e
    features = x_ref.shape[1]
    step = 256
    slope = math.sqrt(2.0 / math.pi)
    last = (((1,), (1,)), ((), ()))

    def chunk(i, carry):
        at = pl.ds(pl.multiple_of(i * step, step), step)
        x = x_ref[at, :]
        ids = ids_ref[at, :].astype(f32)
        lanes = lax.broadcasted_iota(jnp.int32, ids.shape, 1)
        mine = (lanes == 2 * e) | (lanes == 2 * e + 1)
        other = jnp.sum(jnp.where(mine, ids, 0.0), axis=1, keepdims=True).astype(jnp.int32) - own
        logits = jnp.dot(x, router_ref[...], preferred_element_type=f32)
        gate, _ = gate_pair(chosen_logit(logits, own), chosen_logit(logits, other))
        pre = jnp.dot(x, in_ref[0], preferred_element_type=f32)
        tanh = jnp.tanh(slope * (pre + 0.044715 * (pre * pre * pre)))
        active = (0.5 * pre * (1.0 + tanh)).astype(bf16)
        act_ref[0, at, :] = active
        ret_ref[at, :features] = jnp.dot(active, out_ref[0], preferred_element_type=f32).astype(bf16)
        rows = (gate * g_ref[at, :].astype(f32)).astype(bf16)
        arr_ref[0, at, :] = rows
        back = lax.dot_general(rows, out_ref[0], last, preferred_element_type=f32)
        rise = 0.5 * (1.0 + tanh) + 0.5 * pre * (1.0 - tanh * tanh) * (
            slope * (1.0 + 3.0 * 0.044715 * (pre * pre))
        )
        grad = (back * rise).astype(bf16)
        pre_ref[0, at, :] = grad
        ret_ref[at, features:] = lax.dot_general(
            grad, in_ref[0], last, preferred_element_type=f32
        ).astype(bf16)
        return carry

    lax.fori_loop(0, x_ref.shape[0] // step, chunk, 0)


def experts(own, arrived, grad_wide, w_in, w_out, router_w):
    rows = arrived.shape[0]
    features = w_in.shape[1]
    hidden = w_in.shape[2]
    bf16 = jnp.bfloat16
    per = lambda n: pl.BlockSpec((rows, n), lambda e: (0, e))
    weights = lambda a, b: pl.BlockSpec((1, a, b), lambda e: (e, 0, 0))
    return pl.pallas_call(
        expert_kernel,
        grid=(2,),
        out_shape=[
            jax.ShapeDtypeStruct((rows, 4 * features), bf16),
            jax.ShapeDtypeStruct((2, rows, hidden), bf16),
            jax.ShapeDtypeStruct((2, rows, hidden), bf16),
            jax.ShapeDtypeStruct((2, rows, features), bf16),
        ],
        in_specs=[
            SCALARS,
            per(features),
            per(features),
            pl.BlockSpec((rows, 128), lambda e: (0, 2 * features // 128)),
            weights(features, hidden),
            weights(hidden, features),
            pl.BlockSpec(router_w.shape, lambda e: (0, 0)),
        ],
        out_specs=[
            per(2 * features),
            weights(rows, hidden),
            weights(rows, hidden),
            weights(rows, features),
        ],
        compiler_params=ROOM,
        name="experts",
    )(own[None], arrived, grad_wide, grad_wide, w_in, w_out, router_w)


def combine_kernel(places_ref, routes_ref, router_ref, ret_ref, *refs):
    f32, bf16 = jnp.float32, jnp.bfloat16
    grads, moes, outs = refs[:4], refs[4:8], refs[8:12]
    tokens = moes[0].shape[0]
    features = moes[0].shape[1]
    rows = ret_ref.shape[0]
    lane = lax.broadcasted_iota(jnp.int32, (tokens, rows), 1)
    tail_lane = lax.broadcasted_iota(jnp.int32, (tokens, 128), 1)
    for r in range(4):
        here = slice(r * tokens, (r + 1) * tokens)
        logits = jnp.dot(moes[r][...], router_ref[...], preferred_element_type=f32)
        gates = gate_pair(
            chosen_logit(logits, routes_ref[here, 0:1]), chosen_logit(logits, routes_ref[here, 1:2])
        )
        total = jnp.zeros((tokens, features), f32)
        back = jnp.zeros((tokens, features), f32)
        tail = jnp.zeros((tokens, 128), f32)
        grad = grads[r][:, :features].astype(f32)
        picks = [
            [
                (lane + e * rows == places_ref[here, k : k + 1]).astype(f32).astype(bf16)
                for e in range(2)
            ]
            for k in range(2)
        ]
        for k in range(2):
            got = jnp.zeros((tokens, features), f32)
            for e in range(2):
                at = 2 * e * features
                got = got + jnp.dot(
                    picks[k][e], ret_ref[:, at : at + features], preferred_element_type=f32
                )
            total = total + gates[k] * got
            dots = jnp.sum(grad * got, axis=1, keepdims=True)
            high = dots.astype(bf16).astype(f32)
            tail = jnp.where(tail_lane == k, high, tail)
            tail = jnp.where(tail_lane == 2 + k, dots - high, tail)
        for e in range(2):
            at = (2 * e + 1) * features
            back = back + jnp.dot(
                picks[0][e] + picks[1][e],
                ret_ref[:, at : at + features],
                preferred_element_type=f32,
            )
        outs[r][:, :features] = total.astype(bf16)
        outs[r][:, features : 2 * features] = back.astype(bf16)
        outs[r][:, 2 * features :] = tail.astype(bf16)


def combine(places, routes, router_w, returned, grads, moes):
    tokens, features = moes[0].shape
    return pl.pallas_call(
        combine_kernel,
        out_shape=[jax.ShapeDtypeStruct((tokens, 2 * features + 128), jnp.bfloat16)] * 4,
        in_specs=[WHOLE] * 12,
        out_specs=[WHOLE] * 4,
        compiler_params=ROOM,
        name="combine",
    )(places, routes, router_w, returned, *grads, *moes)


def layer(
    tokens,
    seq_lengths,
    routes,
    gain_attn,
    w_query,
    w_key,
    w_value,
    w_output,
    rel_bias,
    gain_moe,
    w_router,
    w_in,
    w_out,
    cotangent,
):
    row_count, features = tokens.shape
    shard_rows = w_query.shape[0]
    expert_count = w_router.shape[1]
    bucket_count = rel_bias.shape[1]
    head_count = 4 * rel_bias.shape[0]
    head_size = features // head_count
    capacity = 3 * row_count // expert_count
    score_scale = 1.0 / math.sqrt(head_size)
    head_shape = (row_count, head_count, head_size)
    bias_size = rel_bias.size
    f32 = jnp.float32
    bf16 = jnp.bfloat16

    extra = shard_rows - row_count
    column = lambda a: a.reshape(-1, 1)
    bias_column = column(jnp.pad(rel_bias.reshape(-1), (0, row_count - bias_size)))
    first = jnp.concatenate(
        [
            routes.astype(bf16),
            column(gain_attn[:row_count]),
            column(gain_moe[:row_count]),
            bias_column,
            jnp.zeros((row_count, 64 - 5), bf16),
            w_router[:row_count],
        ],
        axis=1,
    )
    second = jnp.concatenate(
        [
            column(gain_attn[row_count:]),
            column(gain_moe[row_count:]),
            jnp.zeros((extra, 64 - 2), bf16),
            w_router[row_count:],
        ],
        axis=1,
    )
    second = jnp.pad(second, ((0, row_count - extra), (0, 0)))
    line_grads = along_x(jnp.concatenate([cotangent, first, second], axis=1))
    near_qkv, near_out = send_weights((w_query, w_key, w_value, w_output))
    shard = lax.axis_index("x").astype(jnp.int32)
    core = lax.axis_index("c").astype(jnp.int32)
    where = jnp.stack([shard, core])
    first = jnp.stack([piece[:, features : features + 128] for piece in line_grads])
    second = jnp.stack([piece[:extra, features + 128 :] for piece in line_grads])
    order = (shard - jnp.arange(4)) % 4
    first, second = jnp.take(first, order, axis=0), jnp.take(second, order, axis=0)
    router_w = jnp.concatenate([first[:, :, 64:], second[:, :, 64:]], axis=1).reshape(
        features, expert_count
    )
    gain_one = jnp.concatenate([first[:, :, 2], second[:, :, 0]], axis=1).reshape(1, features)
    gain_two = jnp.concatenate([first[:, :, 3], second[:, :, 1]], axis=1).reshape(1, features)
    bias_table = first[:, :bias_size, 4].reshape(head_count, bucket_count)

    line_routes = jnp.concatenate(
        [piece[:, features : features + 2] for piece in line_grads], axis=0
    ).astype(jnp.int32)
    line_slots = jnp.concatenate(
        [
            capacity_slots(line_routes[r * row_count : (r + 1) * row_count], expert_count)
            + r * capacity
            for r in range(4)
        ],
        axis=0,
    )
    owners = expert_count // 2
    group = 4 * capacity
    slot_rows = owners * group
    line_places = (line_routes % 2) * slot_rows + (line_routes // 2) * group + line_slots

    def to_owners(outgoing):
        return lax.all_to_all(outgoing, ("y", "z", "c"), 0, 0, tiled=True)

    outgoing_grads = dispatch(line_places.T, line_grads, slot_rows)
    grad_wide = to_owners(outgoing_grads)
    first_expert = 2 * lax.axis_index(("y", "z", "c")).astype(jnp.int32)

    segments = row_segments(seq_lengths[0], row_count)
    distance, onehot = position_tables(row_count, bucket_count)
    allowed = (segments[:, None] == segments[None, :]) & (distance >= 0)
    position_bias = jnp.einsum("ijb,hb->hij", onehot, bias_table, preferred_element_type=f32)
    masked_bias = jnp.where(allowed[None], position_bias, -1000000000.0)
    far_qkv = [swap_core(part) for part in near_qkv]
    far_out = [swap_core(part) for part in near_out]
    query_w, key_w, value_w, hidden_one, queries, key_rows, value_rows, probs, attended = attend(
        where,
        tokens,
        gain_one,
        masked_bias,
        (w_query, w_key, w_value),
        near_qkv,
        far_qkv,
        outgoing_grads,
    )
    output_w, middle, moe_in = to_middle(
        where, tokens, gain_two, attended, w_output, near_out, far_out, outgoing_grads
    )

    line_moe = along_x(moe_in)
    arrived = to_owners(dispatch(line_places.T, line_moe, slot_rows))
    ret, active, grad_pre, grad_arrived = experts(
        first_expert, arrived, grad_wide, w_in, w_out, router_w
    )
    returned = lax.all_to_all(ret, ("y", "z", "c"), 0, 0, tiled=True)
    grad_w_out = jnp.einsum("erf,erd->efd", active, grad_arrived, preferred_element_type=f32)
    grad_w_in = jnp.einsum(
        "red,erf->edf",
        arrived.reshape(slot_rows, 2, features),
        grad_pre,
        preferred_element_type=f32,
    )

    bundle = combine(line_places, line_routes, router_w, returned, line_grads, line_moe)
    homes = [bundle[0]] + [shift_x(bundle[r], -r) for r in range(1, 4)]
    result, grad_tokens, kept, given, grad_scores, grad_router, grad_gains = backward(
        core[None],
        tokens,
        cotangent,
        gain_one,
        gain_two,
        routes,
        router_w,
        middle,
        moe_in,
        attended,
        hidden_one,
        queries,
        key_rows,
        value_rows,
        probs,
        *homes,
        query_w,
        key_w,
        value_w,
        output_w,
    )
    grad_bias = jnp.einsum("hij,ijb->hb", grad_scores, onehot, preferred_element_type=f32)

    piece = shard_rows // 8
    wide = features + 128
    bias_column = jnp.pad(grad_bias.reshape(4, bias_size), ((0, 0), (0, shard_rows - bias_size)))
    small_grads = jnp.concatenate(
        [grad_router, grad_gains.T, bias_column.reshape(-1, 1)], axis=1
    ).astype(bf16)
    small_grads = jnp.pad(small_grads, ((0, 0), (0, 128 - small_grads.shape[1])))
    small_grads = small_grads.reshape(4, 2, shard_rows // 2, 128)

    def with_small(main, side):
        part = lax.dynamic_index_in_dim(small_grads, side, 1, keepdims=False).reshape(-1, 128)
        return jnp.concatenate(
            [main, jnp.pad(part, ((0, main.shape[0] - part.shape[0]), (0, 0)))], axis=1
        )

    swapped = swap_core(with_small(given, 1 - core))
    paired = (with_small(kept, core).astype(f32) + swapped.astype(f32)).astype(bf16)
    spread = lax.all_to_all(paired, ("y", "x", "z"), 0, 0, tiled=True)
    mine = jnp.sum(spread.reshape(64, piece, wide).astype(f32), axis=0).astype(bf16)
    totals = lax.all_to_all(
        jnp.broadcast_to(mine[None], (32, piece, wide)).reshape(32 * piece, wide),
        ("y", "c", "z"),
        0,
        0,
        tiled=True,
    ).reshape(4, shard_rows, wide)
    small_totals = totals[0, :, features:].astype(f32)
    totals = totals[:, :, :features].astype(f32)
    router_total = small_totals[:, :expert_count]
    gain_one_total = small_totals[:, expert_count]
    gain_two_total = small_totals[:, expert_count + 1]
    bias_total = small_totals[:bias_size, expert_count + 2].reshape(rel_bias.shape)
    return (
        result,
        grad_tokens,
        gain_one_total,
        totals[0],
        totals[1],
        totals[2],
        totals[3],
        bias_total,
        gain_two_total,
        router_total,
        grad_w_in,
        grad_w_out,
    )


def solution(mesh):
    cube = Mesh(mesh.devices.reshape(4, 4, 2, 4), ("y", "z", "c", "x"))
    expert = ("y", "z", "c")
    everyone = ("y", "z", "c", "x")
    placed = (
        P(everyone, None),
        P(everyone, None),
        P(everyone, None),
        P("x"),
        P("x", None),
        P("x", None),
        P("x", None),
        P("x", None),
        P("x", None),
        P("x"),
        P("x", None),
        P(expert, None, "x"),
        P(expert, "x", None),
        P(everyone, None),
    )
    return jax.shard_map(
        layer,
        mesh=cube,
        in_specs=placed,
        out_specs=(
            P(everyone, None),
            P(everyone, None),
            P("x"),
            P("x", None),
            P("x", None),
            P("x", None),
            P("x", None),
            P("x", None),
            P("x"),
            P("x", None),
            P(expert, None, "x"),
            P(expert, "x", None),
        ),
        check_vma=False,
    )
```

```python
import functools
import math

import jax
import jax.numpy as jnp
from jax import lax
from jax.experimental import pallas as pl
from jax.experimental.pallas import tpu as pltpu
from jax.sharding import Mesh, PartitionSpec as P

epsilon = 1e-06
bucket_edges = list(range(1, 17)) + [
    int(math.ceil(16.0 * 8.0 ** ((bucket_level - 16) / 16.0))) for bucket_level in range(17, 32)
]


def row_segments(lengths, row_count):
    sequence_ends = jnp.cumsum(lengths)
    positions = jnp.arange(row_count, dtype=jnp.int32)
    return jnp.sum((positions[:, None] >= sequence_ends[None, :]).astype(jnp.int32), axis=1)


def position_tables(row_count, bucket_count):
    positions = jnp.arange(row_count, dtype=jnp.int32)
    distance = positions[:, None] - positions[None, :]
    edge_values = jnp.array(bucket_edges, dtype=jnp.int32)
    bucket = jnp.sum((distance[:, :, None] >= edge_values).astype(jnp.int32), axis=2)
    onehot = (bucket[:, :, None] == jnp.arange(bucket_count, dtype=jnp.int32)).astype(jnp.bfloat16)
    return (distance, onehot)


def shift_x(block, step):
    ranks = lax.axis_size("x")
    return lax.ppermute(block, "x", [(i, (i + step) % ranks) for i in range(ranks)])


def swap_core(block):
    return lax.ppermute(block, "c", [(0, 1), (1, 0)])


def along_x(block):
    return [block, shift_x(block, 1), shift_x(block, 2), shift_x(block, 3)]


def head_kernel(core_ref, routes_ref, one_ref, two_ref, bias_ref, router_ref, cotangent_ref, *refs):
    mats, line_ref, qkv_ref, out_ref, held, sems = refs[:4], *refs[4:9]
    f32 = jnp.float32
    tokens = cotangent_ref.shape[0]
    half = mats[0].shape[0] // 2
    start = pl.multiple_of(core_ref[0] * half, half)
    spots = [qkv_ref.at[pl.ds(k * half, half)] for k in range(3)] + [out_ref]
    copies = start_copies(
        [(cotangent_ref, line_ref.at[pl.ds(0, tokens)])]
        + [(m.at[pl.ds(start, half)], spot) for m, spot in zip(mats, spots)],
        sems,
    )
    held[...] = jnp.zeros_like(held)
    held[0:1, : one_ref.shape[1]] = one_ref[...].astype(f32)
    held[1:2, : two_ref.shape[1]] = two_ref[...].astype(f32)
    held[2:5, : bias_ref.shape[1]] = bias_ref[...].astype(f32)
    held[5:7, :tokens] = routes_ref[...].astype(f32)
    experts_all = router_ref.shape[1]
    for b in range(router_ref.shape[0] // 16):
        part = router_ref[16 * b : 16 * b + 16, :].astype(f32)
        held[16:32, experts_all * b : experts_all * (b + 1)] = part
    line_ref[tokens:, :] = held[...].astype(jnp.bfloat16)
    for c in copies:
        c.wait()


def start_copies(pairs, sems):
    copies = [pltpu.make_async_copy(s, d, sems.at[i]) for i, (s, d) in enumerate(pairs)]
    for c in copies:
        c.start()
    return copies


def block_copies(shard, core, mats, near, far, outs):
    rows = mats[0].shape[0]
    half = rows // 2
    pairs = []
    for k, (mat, out) in enumerate(zip(mats, outs)):
        begin = pl.multiple_of(shard * rows, rows)
        pairs.append((mat, out.at[pl.ds(begin, rows)]))
        part = pl.ds(k * half, half)
        for r in range(1, 4):
            begin = lax.rem(shard + (4 - r), 4) * rows
            mine = pl.multiple_of(begin + core * half, half)
            other = pl.multiple_of(begin + (1 - core) * half, half)
            pairs.append((near[r - 1].at[part], out.at[pl.ds(mine, half)]))
            pairs.append((far[r - 1].at[part], out.at[pl.ds(other, half)]))
    return pairs


def norm_scale(x):
    return lax.rsqrt(jnp.mean(x * x, axis=1, keepdims=True) + epsilon)


def head_half(block, side):
    lanes = lax.broadcasted_iota(jnp.int32, block.shape, 1)
    keep = (lanes < 64) if side == 0 else (lanes >= 64)
    return jnp.where(keep, block, jnp.zeros_like(block))


def to_column(row):
    n = row.shape[1]
    down = lax.broadcasted_iota(jnp.int32, (n, n), 0)
    across = lax.broadcasted_iota(jnp.int32, (n, n), 1)
    return jnp.sum(jnp.where(down == across, row, jnp.zeros_like(row)), axis=1, keepdims=True)


LAST = (((1,), (1,)), ((), ()))
FIRST = (((0,), (0,)), ((), ()))


def attend_kernel(place_ref, tokens_ref, gain_ref, bias_ref, *refs):
    f32, bf16 = jnp.float32, jnp.bfloat16
    mats, near, far = refs[:3], refs[3:6], refs[6:9]
    weights = refs[10:13]
    hidden_ref, q_ref, k_ref, v_ref, probs_ref, attended_ref, sems = refs[13:20]
    copies = start_copies(
        block_copies(place_ref[0], place_ref[1], mats, near, far, weights), sems
    )
    x = tokens_ref[...].astype(f32)
    hidden = (x * norm_scale(x) * gain_ref[...].astype(f32)).astype(bf16)
    hidden_ref[...] = hidden
    for n, (w, out) in enumerate(zip(weights, (q_ref, k_ref, v_ref))):
        for c in copies[7 * n : 7 * n + 7]:
            c.wait()
        out[...] = jnp.dot(hidden, w[...], preferred_element_type=f32).astype(bf16)
    heads = bias_ref.shape[0]
    for pair in range(heads // 2):
        lanes = slice(pair * 128, pair * 128 + 128)
        q, k, v = q_ref[:, lanes], k_ref[:, lanes], v_ref[:, lanes]
        total = jnp.zeros(q.shape, f32)
        for side in range(2):
            h = 2 * pair + side
            scores = lax.dot_general(q, head_half(k, side), LAST, preferred_element_type=f32)
            scores = scores * 0.125 + bias_ref[h]
            top = jnp.max(scores, axis=1, keepdims=True)
            grown = jnp.exp(scores - top)
            probs = grown / jnp.sum(grown, axis=1, keepdims=True)
            probs_ref[h] = probs
            total = total + jnp.dot(
                probs.astype(bf16), head_half(v, side), preferred_element_type=f32
            )
        attended_ref[:, lanes] = total.astype(bf16)


def middle_kernel(place_ref, tokens_ref, gain_ref, attended_ref, *refs):
    f32 = jnp.float32
    mats, near, far = refs[:1], refs[1:4], refs[4:7]
    weight, middle_ref, moe_ref, sems = refs[8:12]
    copies = start_copies(
        block_copies(place_ref[0], place_ref[1], mats, near, far, [weight]), sems
    )
    for c in copies:
        c.wait()
    middle = tokens_ref[...].astype(f32) + jnp.dot(
        attended_ref[...], weight[...], preferred_element_type=f32
    )
    middle_ref[...] = middle
    moe_ref[...] = (middle * norm_scale(middle) * gain_ref[...].astype(f32)).astype(jnp.bfloat16)


def backward_kernel(
    core_ref,
    tokens_ref,
    cotangent_ref,
    gain_one_ref,
    gain_two_ref,
    ids_ref,
    router_ref,
    middle_ref,
    moe_ref,
    attended_ref,
    hidden_ref,
    q_ref,
    k_ref,
    v_ref,
    probs_ref,
    spots_ref,
    rows_ref,
    *refs,
):
    f32, bf16 = jnp.float32, jnp.bfloat16
    homes, weights = refs[:4], refs[4:8]
    result_ref, tokens_out, kept_ref, given_ref, scores_ref, router_out, gains_out = refs[8:15]
    held, grads_ref, sems = refs[15:18]
    copies = start_copies([(w, held.at[i]) for i, w in enumerate(weights)], sems)
    features = tokens_ref.shape[1]
    core = core_ref[0]

    def leave(mat, left, right):
        grad = lax.dot_general(left, right, FIRST, preferred_element_type=f32).astype(bf16)
        grads_ref[...] = grad
        for x in range(4):
            low = grads_ref[x * 192 : x * 192 + 96, :]
            high = grads_ref[x * 192 + 96 : x * 192 + 192, :]
            at = (mat * 4 + x) * 96
            kept_ref[at : at + 96, :features] = jnp.where(core == 0, low, high)
            given_ref[at : at + 96, :features] = jnp.where(core == 0, high, low)

    home = homes[0][...].astype(f32)
    for piece in homes[1:]:
        home = home + piece[...].astype(f32)
    middle = middle_ref[...]
    result_ref[...] = (middle + home[:, :features]).astype(bf16)
    tail = home[:, features:]
    lane = lax.broadcasted_iota(jnp.int32, tail.shape, 1)
    grad_gates = [
        jnp.sum(jnp.where((lane == k) | (lane == 2 + k), tail, 0.0), axis=1, keepdims=True)
        for k in range(2)
    ]
    moe = moe_ref[...]
    logits = jnp.dot(moe, router_ref[...], preferred_element_type=f32)
    ids = [to_column(ids_ref[k : k + 1, : tail.shape[0]]) for k in range(2)]
    gates = gate_pair(chosen_logit(logits, ids[0]), chosen_logit(logits, ids[1]))
    mix = gates[0] * grad_gates[0] + gates[1] * grad_gates[1]
    spots = lax.broadcasted_iota(jnp.int32, logits.shape, 1)
    grad_logits = jnp.zeros(logits.shape, f32)
    for k in range(2):
        grad_logits = jnp.where(spots == ids[k], gates[k] * (grad_gates[k] - mix), grad_logits)
    grad_logits = grad_logits.astype(bf16)
    slot = lax.broadcasted_iota(jnp.int32, (rows_ref.shape[0], tail.shape[0]), 0)
    pick = ((slot == spots_ref[0:1]) | (slot == spots_ref[1:2])).astype(f32).astype(bf16)
    grad_moe = lax.dot_general(pick, rows_ref[...], FIRST, preferred_element_type=f32)
    grad_moe = grad_moe + lax.dot_general(
        grad_logits, router_ref[...], LAST, preferred_element_type=f32
    )
    router_out[...] = lax.dot_general(moe, grad_logits, FIRST, preferred_element_type=f32)
    scale = norm_scale(middle)
    normed = middle * scale
    gains_out[1:2, :] = jnp.sum(grad_moe * normed, axis=0, keepdims=True)
    inner = grad_moe * gain_two_ref[...].astype(f32)
    grad_middle = cotangent_ref[...].astype(f32) + scale * (
        inner - normed * jnp.mean(inner * normed, axis=1, keepdims=True)
    )
    branch = grad_middle.astype(bf16)
    leave(3, attended_ref[...], branch)
    copies[3].wait()
    grad_attended = lax.dot_general(branch, held[3], LAST, preferred_element_type=f32).astype(bf16)
    grad_q, grad_k, grad_v = [], [], []
    for pair in range(probs_ref.shape[0] // 2):
        lanes = slice(pair * 128, pair * 128 + 128)
        q, k, v = q_ref[:, lanes], k_ref[:, lanes], v_ref[:, lanes]
        grad = grad_attended[:, lanes]
        parts = [jnp.zeros(q.shape, f32) for _ in range(3)]
        for side in range(2):
            h = 2 * pair + side
            probs = probs_ref[h]
            grad_half = head_half(grad, side)
            parts[2] = parts[2] + lax.dot_general(
                probs.astype(bf16), grad_half, FIRST, preferred_element_type=f32
            )
            grad_probs = lax.dot_general(grad_half, v, LAST, preferred_element_type=f32)
            grad_scores = (
                probs * (grad_probs - jnp.sum(probs * grad_probs, axis=1, keepdims=True))
            ).astype(bf16)
            scores_ref[h] = grad_scores
            parts[0] = parts[0] + jnp.dot(
                grad_scores, head_half(k, side), preferred_element_type=f32
            )
            parts[1] = parts[1] + lax.dot_general(
                grad_scores, head_half(q, side), FIRST, preferred_element_type=f32
            )
        grad_q.append((parts[0] * 0.125).astype(bf16))
        grad_k.append((parts[1] * 0.125).astype(bf16))
        grad_v.append(parts[2].astype(bf16))
    hidden = hidden_ref[...]
    grad_hidden = jnp.zeros(hidden.shape, f32)
    for n, parts in enumerate((grad_q, grad_k, grad_v)):
        grad = jnp.concatenate(parts, axis=1)
        leave(n, hidden, grad)
        copies[n].wait()
        grad_hidden = grad_hidden + lax.dot_general(
            grad, held[n], LAST, preferred_element_type=f32
        )
    x = tokens_ref[...].astype(f32)
    scale = norm_scale(x)
    normed = x * scale
    gains_out[0:1, :] = jnp.sum(grad_hidden * normed, axis=0, keepdims=True)
    inner = grad_hidden * gain_one_ref[...].astype(f32)
    tokens_out[...] = grad_middle + scale * (
        inner - normed * jnp.mean(inner * normed, axis=1, keepdims=True)
    )


ANYWHERE = pl.BlockSpec(memory_space=pl.ANY)
SCALARS = pl.BlockSpec(memory_space=pltpu.SMEM)
WHOLE = pl.BlockSpec(memory_space=pltpu.VMEM)
ROOM = pltpu.CompilerParams(vmem_limit_bytes=56 * 1024 * 1024)


def head(core, routes, gain_one, gain_two, bias, router, cotangent, mats):
    bf16 = jnp.bfloat16
    rows, cols = mats[0].shape
    half = rows // 2
    tokens = cotangent.shape[0]
    return pl.pallas_call(
        head_kernel,
        out_shape=[
            jax.ShapeDtypeStruct((tokens + 32, cols), bf16),
            jax.ShapeDtypeStruct((3 * half, cols), bf16),
            jax.ShapeDtypeStruct((half, cols), bf16),
        ],
        in_specs=[SCALARS] + [WHOLE] * 5 + [ANYWHERE] * 5,
        out_specs=[WHOLE] * 3,
        scratch_shapes=[pltpu.VMEM((32, cols), jnp.float32), pltpu.SemaphoreType.DMA((5,))],
        compiler_params=ROOM,
        name="head",
    )(core[None], routes, gain_one, gain_two, bias, router, cotangent, *mats)


def attend(where, tokens, gain, bias, mats, near, far, after):
    rows, cols = mats[0].shape
    full = jax.ShapeDtypeStruct((4 * rows, cols), jnp.bfloat16)
    state = jax.ShapeDtypeStruct(tokens.shape, jnp.bfloat16)
    return pl.pallas_call(
        attend_kernel,
        out_shape=[full] * 3 + [state] * 4 + [jax.ShapeDtypeStruct(bias.shape, jnp.float32), state],
        in_specs=[SCALARS] + [WHOLE] * 3 + [ANYWHERE] * 10,
        out_specs=[WHOLE] * 9,
        scratch_shapes=[pltpu.SemaphoreType.DMA((21,))],
        compiler_params=ROOM,
        name="attend",
    )(where, tokens, gain, bias, *mats, *near, *far, after)


def to_middle(where, tokens, gain, attended, mat, near, far, after):
    rows, cols = mat.shape
    return pl.pallas_call(
        middle_kernel,
        out_shape=[
            jax.ShapeDtypeStruct((4 * rows, cols), jnp.bfloat16),
            jax.ShapeDtypeStruct(tokens.shape, jnp.float32),
            jax.ShapeDtypeStruct(tokens.shape, jnp.bfloat16),
        ],
        in_specs=[SCALARS] + [WHOLE] * 3 + [ANYWHERE] * 8,
        out_specs=[WHOLE] * 3,
        scratch_shapes=[pltpu.SemaphoreType.DMA((7,))],
        compiler_params=ROOM,
        name="middle",
    )(where, tokens, gain, attended, mat, *near, *far, after)


def backward(core, *arrays):
    tokens, router_w, probs = arrays[0], arrays[5], arrays[13]
    count, features = tokens.shape
    bf16, f32 = jnp.bfloat16, jnp.float32
    shape = jax.ShapeDtypeStruct
    return pl.pallas_call(
        backward_kernel,
        out_shape=[
            shape((count, features), bf16),
            shape((count, features), f32),
            shape((2 * features, features), bf16),
            shape((2 * features, features), bf16),
            shape(probs.shape, bf16),
            shape(router_w.shape, f32),
            shape((2, features), f32),
        ],
        in_specs=[SCALARS] + [WHOLE] * 20 + [ANYWHERE] * 4,
        out_specs=[WHOLE] * 7,
        scratch_shapes=[
            pltpu.VMEM((4, features, features), bf16),
            pltpu.VMEM((features, features), bf16),
            pltpu.SemaphoreType.DMA((4,)),
        ],
        compiler_params=ROOM,
        name="backward",
    )(core, *arrays)


def picks_of(places, e, rows):
    row = lax.broadcasted_iota(jnp.int32, (rows, places.shape[1]), 0) + e * rows
    return ((row == places[0:1]) | (row == places[1:2])).astype(jnp.float32).astype(jnp.bfloat16)


def dispatch_grads_kernel(capacity, *refs):
    pieces, (out_ref, places_ref, ids_ref, spots_ref) = refs[:4], refs[4:]
    f32, bf16, i32 = jnp.float32, jnp.bfloat16, jnp.int32
    rows = out_ref.shape[0]
    tokens = spots_ref.shape[1]
    features = pieces[0].shape[1]
    experts_all = 2 * rows // (4 * capacity)
    expert = lax.broadcasted_iota(i32, (experts_all, tokens), 0)
    down = lax.broadcasted_iota(i32, (tokens, tokens), 0)
    across = lax.broadcasted_iota(i32, (tokens, tokens), 1)
    earlier = (down < across).astype(f32).astype(bf16)
    sums = []
    for r in range(4):
        both = pieces[r][tokens : tokens + 16, :tokens].astype(f32)
        ids = [both[5 + k : 6 + k].astype(i32) for k in range(2)]
        match = [expert == i for i in ids]
        named = (match[0] | match[1]).astype(f32).astype(bf16)
        counts = jnp.dot(named, earlier, preferred_element_type=f32)
        here = slice(r * tokens, (r + 1) * tokens)
        for k in range(2):
            slot = jnp.sum(jnp.where(match[k], counts, 0.0), axis=0, keepdims=True).astype(i32)
            owner, local = ids[k] >> 1, ids[k] & 1
            places_ref[k : k + 1, here] = (
                local * rows + owner * (4 * capacity) + r * capacity + slot
            )
            ids_ref[k : k + 1, here] = ids[k]
            if r == 0:
                spots_ref[k : k + 1, :] = owner * 16 + local * capacity + slot
        sums.append(to_column(both[5:6] + both[6:7]))
    sums = jnp.concatenate(sums, axis=0)
    lanes = lax.broadcasted_iota(i32, (4 * tokens, 128), 1)
    line = jnp.concatenate([p[:tokens, :] for p in pieces], axis=0)
    places = places_ref[...]
    extra = jnp.zeros((rows, 128), f32)
    for e in range(2):
        pick = picks_of(places, e, rows)
        out_ref[:, e * features : (e + 1) * features] = jnp.dot(
            pick, line, preferred_element_type=f32
        ).astype(bf16)
        column = jnp.where(lanes == e, sums, 0.0).astype(bf16)
        extra = extra + jnp.dot(pick, column, preferred_element_type=f32)
    out_ref[:, 2 * features :] = extra.astype(bf16)


def dispatch_grads(pieces, rows, capacity, tokens):
    features = pieces[0].shape[1]
    shape = jax.ShapeDtypeStruct
    return pl.pallas_call(
        functools.partial(dispatch_grads_kernel, capacity),
        out_shape=[
            shape((rows, 2 * features + 128), jnp.bfloat16),
            shape((2, 4 * tokens), jnp.int32),
            shape((2, 4 * tokens), jnp.int32),
            shape((2, tokens), jnp.int32),
        ],
        in_specs=[WHOLE] * 4,
        out_specs=[WHOLE] * 4,
        compiler_params=ROOM,
        name="dispatch_grads",
    )(*pieces)


def dispatch_kernel(places_ref, *refs):
    pieces, out_ref = refs[:4], refs[4]
    rows = out_ref.shape[0]
    features = pieces[0].shape[1]
    line = jnp.concatenate([p[...] for p in pieces], axis=0)
    for e in range(2):
        out_ref[:, e * features : (e + 1) * features] = jnp.dot(
            picks_of(places_ref[...], e, rows), line, preferred_element_type=jnp.float32
        ).astype(jnp.bfloat16)


def dispatch(places, pieces, rows):
    return pl.pallas_call(
        dispatch_kernel,
        out_shape=jax.ShapeDtypeStruct((rows, 2 * pieces[0].shape[1]), jnp.bfloat16),
        in_specs=[WHOLE] * 5,
        out_specs=WHOLE,
        compiler_params=ROOM,
        name="dispatch",
    )(places, *pieces)


def chosen_logit(logits, ids):
    lanes = lax.broadcasted_iota(jnp.int32, logits.shape, 1)
    return jnp.sum(jnp.where(lanes == ids, logits, 0.0), axis=1, keepdims=True)


def gate_pair(first, second):
    top = jnp.maximum(first, second)
    one, two = jnp.exp(first - top), jnp.exp(second - top)
    total = one + two
    return one / total, two / total


def expert_kernel(x_ref, in_ref, out_ref, ret_ref, act_ref, rise_ref):
    f32, bf16 = jnp.float32, jnp.bfloat16
    step = 256
    slope = math.sqrt(2.0 / math.pi)

    def chunk(i, carry):
        at = pl.ds(pl.multiple_of(i * step, step), step)
        pre = jnp.dot(x_ref[at, :], in_ref[0], preferred_element_type=f32)
        tanh = jnp.tanh(slope * (pre + 0.044715 * (pre * pre * pre)))
        active = (0.5 * pre * (1.0 + tanh)).astype(bf16)
        act_ref[0, at, :] = active
        ret_ref[at, :] = jnp.dot(active, out_ref[0], preferred_element_type=f32).astype(bf16)
        rise_ref[0, at, :] = 0.5 * (1.0 + tanh) + 0.5 * pre * (1.0 - tanh * tanh) * (
            slope * (1.0 + 3.0 * 0.044715 * (pre * pre))
        )
        return carry

    lax.fori_loop(0, x_ref.shape[0] // step, chunk, 0)


def lanes_of(rows, n):
    return pl.BlockSpec((rows, n), lambda e: (0, e))


def one_of(a, b):
    return pl.BlockSpec((1, a, b), lambda e: (e, 0, 0))


def experts(arrived, w_in, w_out):
    rows = arrived.shape[0]
    features, hidden = w_in.shape[1:]
    return pl.pallas_call(
        expert_kernel,
        grid=(2,),
        out_shape=[
            jax.ShapeDtypeStruct((rows, 2 * features), jnp.bfloat16),
            jax.ShapeDtypeStruct((2, rows, hidden), jnp.bfloat16),
            jax.ShapeDtypeStruct((2, rows, hidden), jnp.float32),
        ],
        in_specs=[lanes_of(rows, features), one_of(features, hidden), one_of(hidden, features)],
        out_specs=[lanes_of(rows, features), one_of(rows, hidden), one_of(rows, hidden)],
        compiler_params=ROOM,
        name="experts",
    )(arrived, w_in, w_out)


def expert_back_kernel(
    capacity, own_ref, x_ref, g_ref, ids_ref, in_ref, out_ref, router_ref, rise_ref, *refs
):
    pre_ref, arr_ref, outs, held = refs[0], refs[1], refs[2:6], refs[6]
    f32, bf16, i32 = jnp.float32, jnp.bfloat16, jnp.int32
    e = pl.program_id(0)
    own = own_ref[0] + e
    rows = x_ref.shape[0]
    step = 256

    def chunk(i, carry):
        at = pl.ds(pl.multiple_of(i * step, step), step)
        ids = ids_ref[at, :].astype(f32)
        lanes = lax.broadcasted_iota(i32, ids.shape, 1)
        other = jnp.sum(jnp.where(lanes == e, ids, 0.0), axis=1, keepdims=True).astype(i32) - own
        logits = jnp.dot(x_ref[at, :], router_ref[...], preferred_element_type=f32)
        gate, _ = gate_pair(chosen_logit(logits, own), chosen_logit(logits, other))
        grown = (gate * g_ref[at, :].astype(f32)).astype(bf16)
        arr_ref[0, at, :] = grown
        back = lax.dot_general(grown, out_ref[0], LAST, preferred_element_type=f32)
        grad = (back * rise_ref[0, at, :]).astype(bf16)
        pre_ref[0, at, :] = grad
        held[at, :] = lax.dot_general(grad, in_ref[0], LAST, preferred_element_type=f32).astype(
            bf16
        )
        return carry

    lax.fori_loop(0, rows // step, chunk, 0)
    part = rows // 4
    here = lax.broadcasted_iota(i32, (part, rows), 0)
    there = lax.broadcasted_iota(i32, (part, rows), 1)
    block = (here * (65536 // capacity + 1)) >> 16
    for r, out in enumerate(outs):
        source = here + block * (3 * capacity) + r * capacity
        pick = (there == source).astype(f32).astype(bf16)
        out[...] = jnp.dot(pick, held[...], preferred_element_type=f32).astype(bf16)


def experts_back(own, arrived, grad_wide, w_in, w_out, router_w, rise, capacity):
    rows = arrived.shape[0]
    features, hidden = w_in.shape[1:]
    bf16 = jnp.bfloat16
    shape = jax.ShapeDtypeStruct
    part = rows // 4
    return pl.pallas_call(
        functools.partial(expert_back_kernel, capacity),
        grid=(2,),
        out_shape=[shape((2, rows, hidden), bf16), shape((2, rows, features), bf16)]
        + [shape((2 * part, features), bf16)] * 4,
        in_specs=[
            SCALARS,
            lanes_of(rows, features),
            lanes_of(rows, features),
            pl.BlockSpec((rows, 128), lambda e: (0, 2 * features // 128)),
            one_of(features, hidden),
            one_of(hidden, features),
            pl.BlockSpec(router_w.shape, lambda e: (0, 0)),
            one_of(rows, hidden),
        ],
        out_specs=[one_of(rows, hidden), one_of(rows, features)]
        + [pl.BlockSpec((part, features), lambda e: (e, 0))] * 4,
        scratch_shapes=[pltpu.VMEM((rows, features), bf16)],
        compiler_params=ROOM,
        name="experts_back",
    )(own[None], arrived, grad_wide, grad_wide, w_in, w_out, router_w, rise)


def weight_grads_kernel(x_ref, pre_ref, act_ref, arr_ref, in_ref, out_ref):
    in_ref[0] = lax.dot_general(x_ref[...], pre_ref[0], FIRST, preferred_element_type=jnp.float32)
    out_ref[0] = lax.dot_general(act_ref[0], arr_ref[0], FIRST, preferred_element_type=jnp.float32)


def weight_grads(arrived, grad_pre, active, grad_arrived):
    rows = arrived.shape[0]
    hidden, features = grad_pre.shape[2], grad_arrived.shape[2]
    step = 256
    cuts = features // step
    whole = lambda n: pl.BlockSpec((1, rows, n), lambda e, j: (e, 0, 0))
    out = lambda n: pl.BlockSpec((1, step, n), lambda e, j: (e, j, 0))
    return pl.pallas_call(
        weight_grads_kernel,
        grid=(2, cuts),
        out_shape=[
            jax.ShapeDtypeStruct((2, features, hidden), jnp.float32),
            jax.ShapeDtypeStruct((2, hidden, features), jnp.float32),
        ],
        in_specs=[
            pl.BlockSpec((rows, step), lambda e, j: (0, e * cuts + j)),
            whole(hidden),
            pl.BlockSpec((1, rows, step), lambda e, j: (e, 0, j)),
            whole(features),
        ],
        out_specs=[out(hidden), out(features)],
        compiler_params=ROOM,
        cost_estimate=pl.CostEstimate(
            flops=8 * rows * features * hidden, bytes_accessed=20_000_000, transcendentals=0
        ),
        name="weight_grads",
    )(arrived, grad_pre, active, grad_arrived)


def sum_rows_kernel(capacity, *refs):
    pieces, out_ref = refs[:4], refs[-1]
    f32, bf16, i32 = jnp.float32, jnp.bfloat16, jnp.int32
    total = pieces[0][...].astype(f32)
    for piece in pieces[1:]:
        total = total + piece[...].astype(f32)
    rows = out_ref.shape[0]
    part = total.shape[0] // 2
    here = lax.broadcasted_iota(i32, (rows, 2 * part), 0)
    there = lax.broadcasted_iota(i32, (rows, 2 * part), 1)
    owner, q = here >> 4, here & 15
    second = q >= capacity
    source = owner * capacity + jnp.where(second, part + q - capacity, q)
    pick = ((there == source) & (q < 2 * capacity)).astype(f32).astype(bf16)
    out_ref[...] = jnp.dot(pick, total.astype(bf16), preferred_element_type=f32).astype(bf16)


def sum_rows(pieces, capacity, after):
    rows, features = pieces[0].shape
    return pl.pallas_call(
        functools.partial(sum_rows_kernel, capacity),
        out_shape=jax.ShapeDtypeStruct((rows // (2 * capacity) * 16, features), jnp.bfloat16),
        in_specs=[WHOLE] * 4 + [ANYWHERE] * len(after),
        out_specs=WHOLE,
        compiler_params=ROOM,
        name="sum_rows",
    )(*pieces, *after)


def combine_kernel(places_ref, ids_ref, router_ref, ret_ref, *refs):
    f32, bf16 = jnp.float32, jnp.bfloat16
    grads, moes, outs = refs[:4], refs[4:8], refs[9:13]
    tokens, features = moes[0].shape
    rows = ret_ref.shape[0]
    row = lax.broadcasted_iota(jnp.int32, (rows, tokens), 0)
    tail_lane = lax.broadcasted_iota(jnp.int32, (tokens, 128), 1)
    for r in range(4):
        here = slice(r * tokens, (r + 1) * tokens)
        logits = jnp.dot(moes[r][...], router_ref[...], preferred_element_type=f32)
        ids = [to_column(ids_ref[k : k + 1, here]) for k in range(2)]
        gates = gate_pair(chosen_logit(logits, ids[0]), chosen_logit(logits, ids[1]))
        total = jnp.zeros((tokens, features), f32)
        tail = jnp.zeros((tokens, 128), f32)
        grad = grads[r][:tokens, :].astype(f32)
        for k in range(2):
            got = jnp.zeros((tokens, features), f32)
            for e in range(2):
                pick = (row + e * rows == places_ref[k : k + 1, here]).astype(f32).astype(bf16)
                got = got + lax.dot_general(
                    pick,
                    ret_ref[:, e * features : (e + 1) * features],
                    FIRST,
                    preferred_element_type=f32,
                )
            total = total + gates[k] * got
            dots = jnp.sum(grad * got, axis=1, keepdims=True)
            high = dots.astype(bf16).astype(f32)
            tail = jnp.where(tail_lane == k, high, tail)
            tail = jnp.where(tail_lane == 2 + k, dots - high, tail)
        outs[r][:, :features] = total.astype(bf16)
        outs[r][:, features:] = tail.astype(bf16)


def combine(places, ids, router_w, returned, grads, moes, after):
    tokens, features = moes[0].shape
    return pl.pallas_call(
        combine_kernel,
        out_shape=[jax.ShapeDtypeStruct((tokens, features + 128), jnp.bfloat16)] * 4,
        in_specs=[WHOLE] * 12 + [ANYWHERE],
        out_specs=[WHOLE] * 4,
        compiler_params=ROOM,
        name="combine",
    )(places, ids, router_w, returned, *grads, *moes, after)


def layer(
    tokens,
    seq_lengths,
    routes,
    gain_attn,
    w_query,
    w_key,
    w_value,
    w_output,
    rel_bias,
    gain_moe,
    w_router,
    w_in,
    w_out,
    cotangent,
):
    row_count, features = tokens.shape
    shard_rows = w_query.shape[0]
    expert_count = w_router.shape[1]
    bucket_count = rel_bias.shape[1]
    head_count = 4 * rel_bias.shape[0]
    capacity = 3 * row_count // expert_count
    bias_size = rel_bias.size
    f32 = jnp.float32
    bf16 = jnp.bfloat16

    shard = lax.axis_index("x").astype(jnp.int32)
    core = lax.axis_index("c").astype(jnp.int32)
    where = jnp.stack([shard, core])
    owners = expert_count // 2
    slot_rows = owners * 4 * capacity

    line, sent_qkv, sent_out = head(
        core,
        routes.T,
        gain_attn[None],
        gain_moe[None],
        rel_bias,
        w_router,
        cotangent,
        (w_query, w_key, w_value, w_output),
    )
    line_grads = along_x(line)
    near_qkv = along_x(sent_qkv)[1:]
    near_out = along_x(sent_out)[1:]
    order = (shard - jnp.arange(4)) % 4
    small = jnp.take(jnp.stack([p[row_count:] for p in line_grads]), order, axis=0)
    gain_one = small[:, 0, :shard_rows].reshape(1, features)
    gain_two = small[:, 1, :shard_rows].reshape(1, features)
    bias_table = small[:, 2:5, :bucket_count].reshape(head_count, bucket_count)
    router_w = (
        small[:, 16:]
        .reshape(4, 16, shard_rows // 16, expert_count)
        .transpose(0, 2, 1, 3)
        .reshape(features, expert_count)
    )

    def to_owners(outgoing):
        return lax.all_to_all(outgoing, ("y", "z", "c"), 0, 0, tiled=True)

    outgoing_grads, places, ids, spots = dispatch_grads(
        line_grads, slot_rows, capacity, row_count
    )
    grad_wide = to_owners(outgoing_grads)
    first_expert = 2 * lax.axis_index(("y", "z", "c")).astype(jnp.int32)

    segments = row_segments(seq_lengths[0], row_count)
    distance, onehot = position_tables(row_count, bucket_count)
    allowed = (segments[:, None] == segments[None, :]) & (distance >= 0)
    position_bias = jnp.einsum("ijb,hb->hij", onehot, bias_table, preferred_element_type=f32)
    masked_bias = jnp.where(allowed[None], position_bias, -1000000000.0)
    far_qkv = [swap_core(part) for part in near_qkv]
    far_out = [swap_core(part) for part in near_out]
    query_w, key_w, value_w, hidden_one, queries, key_rows, value_rows, probs, attended = attend(
        where,
        tokens,
        gain_one,
        masked_bias,
        (w_query, w_key, w_value),
        near_qkv,
        far_qkv,
        outgoing_grads,
    )
    output_w, middle, moe_in = to_middle(
        where, tokens, gain_two, attended, w_output, near_out, far_out, outgoing_grads
    )

    line_moe = along_x(moe_in)
    arrived = to_owners(dispatch(places, line_moe, slot_rows))
    ret, active, rise = experts(arrived, w_in, w_out)
    returned = to_owners(ret)
    grad_pre, grad_arrived, *blocks = experts_back(
        first_expert, arrived, grad_wide, w_in, w_out, router_w, rise, capacity
    )
    summed = [blocks[0]] + [shift_x(blocks[r], -r) for r in range(1, 4)]
    grad_w_in, grad_w_out = weight_grads(arrived, grad_pre, active, grad_arrived)
    rows_home = sum_rows(summed, capacity, (grad_w_in, grad_w_out))
    back_rows = to_owners(rows_home)
    bundle = combine(places, ids, router_w, returned, line_grads, line_moe, rows_home)
    homes = [bundle[0]] + [shift_x(bundle[r], -r) for r in range(1, 4)]
    result, grad_tokens, kept, given, grad_scores, grad_router, grad_gains = backward(
        core[None],
        tokens,
        cotangent,
        gain_one,
        gain_two,
        ids,
        router_w,
        middle,
        moe_in,
        attended,
        hidden_one,
        queries,
        key_rows,
        value_rows,
        probs,
        spots,
        back_rows,
        *homes,
        query_w,
        key_w,
        value_w,
        output_w,
    )
    grad_bias = jnp.einsum("hij,ijb->hb", grad_scores, onehot, preferred_element_type=f32)

    piece = shard_rows // 8
    wide = features + 128
    bias_column = jnp.pad(grad_bias.reshape(4, bias_size), ((0, 0), (0, shard_rows - bias_size)))
    small_grads = jnp.concatenate(
        [grad_router, grad_gains.T, bias_column.reshape(-1, 1)], axis=1
    ).astype(bf16)
    small_grads = jnp.pad(small_grads, ((0, 0), (0, 128 - small_grads.shape[1])))
    small_grads = small_grads.reshape(4, 2, shard_rows // 2, 128)

    def small_half(side):
        part = lax.dynamic_index_in_dim(small_grads, side, 1, keepdims=False).reshape(-1, 128)
        return jnp.pad(part, ((0, kept.shape[0] - part.shape[0]), (0, 0)))

    pairs = ((kept, swap_core(given)), (small_half(core), swap_core(small_half(1 - core))))
    paired = jnp.concatenate(
        [(a.astype(f32) + b.astype(f32)).astype(bf16) for a, b in pairs], axis=1
    )
    spread = lax.all_to_all(paired, ("y", "x", "z"), 0, 0, tiled=True)
    mine = jnp.sum(spread.reshape(64, piece, wide).astype(f32), axis=0).astype(bf16)
    totals = lax.all_to_all(
        jnp.broadcast_to(mine[None], (32, piece, wide)).reshape(32 * piece, wide),
        ("y", "c", "z"),
        0,
        0,
        tiled=True,
    ).reshape(4, shard_rows, wide)
    small_totals = totals[0, :, features:].astype(f32)
    totals = totals[:, :, :features].astype(f32)
    router_total = small_totals[:, :expert_count]
    gain_one_total = small_totals[:, expert_count]
    gain_two_total = small_totals[:, expert_count + 1]
    bias_total = small_totals[:bias_size, expert_count + 2].reshape(rel_bias.shape)
    return (
        result,
        grad_tokens,
        gain_one_total,
        totals[0],
        totals[1],
        totals[2],
        totals[3],
        bias_total,
        gain_two_total,
        router_total,
        grad_w_in,
        grad_w_out,
    )


def solution(mesh):
    cube = Mesh(mesh.devices.reshape(4, 4, 2, 4), ("y", "z", "c", "x"))
    expert = ("y", "z", "c")
    everyone = ("y", "z", "c", "x")
    placed = (
        P(everyone, None),
        P(everyone, None),
        P(everyone, None),
        P("x"),
        P("x", None),
        P("x", None),
        P("x", None),
        P("x", None),
        P("x", None),
        P("x"),
        P("x", None),
        P(expert, None, "x"),
        P(expert, "x", None),
        P(everyone, None),
    )
    return jax.shard_map(
        layer,
        mesh=cube,
        in_specs=placed,
        out_specs=(
            P(everyone, None),
            P(everyone, None),
            P("x"),
            P("x", None),
            P("x", None),
            P("x", None),
            P("x", None),
            P("x", None),
            P("x"),
            P("x", None),
            P(expert, None, "x"),
            P(expert, "x", None),
        ),
        check_vma=False,
    )
```

```python
import functools
import math

import jax
import jax.numpy as jnp
from jax import lax
from jax.experimental import pallas as pl
from jax.experimental.pallas import tpu as pltpu
from jax.sharding import Mesh, PartitionSpec as P

epsilon = 1e-06
bucket_edges = list(range(1, 17)) + [
    int(math.ceil(16.0 * 8.0 ** ((bucket_level - 16) / 16.0))) for bucket_level in range(17, 32)
]


def row_segments(lengths, row_count):
    sequence_ends = jnp.cumsum(lengths)
    positions = jnp.arange(row_count, dtype=jnp.int32)
    return jnp.sum((positions[:, None] >= sequence_ends[None, :]).astype(jnp.int32), axis=1)


def position_tables(row_count, bucket_count):
    positions = jnp.arange(row_count, dtype=jnp.int32)
    distance = positions[:, None] - positions[None, :]
    edge_values = jnp.array(bucket_edges, dtype=jnp.int32)
    bucket = jnp.sum((distance[:, :, None] >= edge_values).astype(jnp.int32), axis=2)
    onehot = (bucket[:, :, None] == jnp.arange(bucket_count, dtype=jnp.int32)).astype(jnp.bfloat16)
    return (distance, onehot)


def shift_x(block, step):
    ranks = lax.axis_size("x")
    return lax.ppermute(block, "x", [(i, (i + step) % ranks) for i in range(ranks)])


def swap_core(block):
    return lax.ppermute(block, "c", [(0, 1), (1, 0)])


def along_x(block):
    return [block, shift_x(block, 1), shift_x(block, 2), shift_x(block, 3)]


def line_kernel(routes_ref, gains_ref, bias_ref, router_ref, cotangent_ref, line_ref, held, sem):
    f32 = jnp.float32
    tokens = cotangent_ref.shape[0]
    copy = pltpu.make_async_copy(cotangent_ref, line_ref.at[pl.ds(0, tokens)], sem)
    copy.start()
    held[...] = jnp.zeros_like(held)
    held[0:2, : gains_ref.shape[1]] = gains_ref[...].astype(f32)
    held[2:5, : bias_ref.shape[1]] = bias_ref[...].astype(f32)
    held[5:7, :tokens] = routes_ref[...].astype(f32)
    width = router_ref.shape[1]
    for b in range(router_ref.shape[0] // 16):
        part = router_ref[16 * b : 16 * b + 16, :].astype(f32)
        held[16:32, width * b : width * (b + 1)] = part
    line_ref[tokens:, :] = held[...].astype(jnp.bfloat16)
    copy.wait()


def pack_kernel(count, core_ref, *refs):
    mats, out_ref, sems = refs[:count], refs[count + 1], refs[count + 2]
    half = mats[0].shape[0] // 2
    start = pl.multiple_of(core_ref[0] * half, half)
    copies = start_copies(
        [
            (m.at[pl.ds(start, half)], out_ref.at[pl.ds(k * half, half)])
            for k, m in enumerate(mats)
        ],
        sems,
    )
    for c in copies:
        c.wait()


def start_copies(pairs, sems):
    copies = [pltpu.make_async_copy(s, d, sems.at[i]) for i, (s, d) in enumerate(pairs)]
    for c in copies:
        c.start()
    return copies


def block_copies(shard, core, mats, near, far, outs):
    rows = mats[0].shape[0]
    half = rows // 2
    pairs = []
    for k, (mat, out) in enumerate(zip(mats, outs)):
        begin = pl.multiple_of(shard * rows, rows)
        pairs.append((mat, out.at[pl.ds(begin, rows)]))
        part = pl.ds(k * half, half)
        for r in range(1, 4):
            begin = lax.rem(shard + (4 - r), 4) * rows
            mine = pl.multiple_of(begin + core * half, half)
            other = pl.multiple_of(begin + (1 - core) * half, half)
            pairs.append((near[r - 1].at[part], out.at[pl.ds(mine, half)]))
            pairs.append((far[r - 1].at[part], out.at[pl.ds(other, half)]))
    return pairs


def norm_scale(x):
    return lax.rsqrt(jnp.mean(x * x, axis=1, keepdims=True) + epsilon)


def head_half(block, side):
    lanes = lax.broadcasted_iota(jnp.int32, block.shape, 1)
    keep = (lanes < 64) if side == 0 else (lanes >= 64)
    return jnp.where(keep, block, jnp.zeros_like(block))


def to_column(row):
    n = row.shape[1]
    down = lax.broadcasted_iota(jnp.int32, (n, n), 0)
    across = lax.broadcasted_iota(jnp.int32, (n, n), 1)
    return jnp.sum(jnp.where(down == across, row, jnp.zeros_like(row)), axis=1, keepdims=True)


def diagonal_sums(scores):
    n = scores.shape[0]
    down = lax.broadcasted_iota(jnp.int32, (n, n), 0)
    step = 1
    while step < n:
        turned = pltpu.roll(scores, n - step, axis=1)
        scores = jnp.where((down & step) != 0, turned, scores)
        step *= 2
    return jnp.sum(scores, axis=0, keepdims=True)


def bucket_marks():
    shape = (128, 128)
    distance = (128 - lax.broadcasted_iota(jnp.int32, shape, 0)) & 127
    bucket = jnp.zeros(shape, jnp.int32)
    for edge in bucket_edges:
        bucket = bucket + (distance >= edge).astype(jnp.int32)
    mark = bucket == lax.broadcasted_iota(jnp.int32, shape, 1)
    return mark.astype(jnp.float32).astype(jnp.bfloat16)


LAST = (((1,), (1,)), ((), ()))
FIRST = (((0,), (0,)), ((), ()))


def attend_kernel(place_ref, tokens_ref, gain_ref, bias_ref, *refs):
    f32, bf16 = jnp.float32, jnp.bfloat16
    mats, near, far = refs[:3], refs[3:6], refs[6:9]
    weights = refs[10:13]
    hidden_ref, q_ref, k_ref, v_ref, probs_ref, attended_ref, sems = refs[13:20]
    copies = start_copies(
        block_copies(place_ref[0], place_ref[1], mats, near, far, weights), sems
    )
    x = tokens_ref[...].astype(f32)
    hidden = (x * norm_scale(x) * gain_ref[...].astype(f32)).astype(bf16)
    hidden_ref[...] = hidden
    for n, (w, out) in enumerate(zip(weights, (q_ref, k_ref, v_ref))):
        for c in copies[7 * n : 7 * n + 7]:
            c.wait()
        out[...] = jnp.dot(hidden, w[...], preferred_element_type=f32).astype(bf16)
    heads = bias_ref.shape[0]
    for pair in range(heads // 2):
        lanes = slice(pair * 128, pair * 128 + 128)
        q, k, v = q_ref[:, lanes], k_ref[:, lanes], v_ref[:, lanes]
        total = jnp.zeros(q.shape, f32)
        for side in range(2):
            h = 2 * pair + side
            scores = lax.dot_general(q, head_half(k, side), LAST, preferred_element_type=f32)
            scores = scores * 0.125 + bias_ref[h]
            top = jnp.max(scores, axis=1, keepdims=True)
            grown = jnp.exp(scores - top)
            probs = grown / jnp.sum(grown, axis=1, keepdims=True)
            probs_ref[h] = probs
            total = total + jnp.dot(
                probs.astype(bf16), head_half(v, side), preferred_element_type=f32
            )
        attended_ref[:, lanes] = total.astype(bf16)


def middle_kernel(place_ref, tokens_ref, gain_ref, attended_ref, *refs):
    f32 = jnp.float32
    mats, near, far = refs[:1], refs[1:4], refs[4:7]
    weight, middle_ref, moe_ref, sems = refs[8:12]
    copies = start_copies(
        block_copies(place_ref[0], place_ref[1], mats, near, far, [weight]), sems
    )
    for c in copies:
        c.wait()
    middle = tokens_ref[...].astype(f32) + jnp.dot(
        attended_ref[...], weight[...], preferred_element_type=f32
    )
    middle_ref[...] = middle
    moe_ref[...] = (middle * norm_scale(middle) * gain_ref[...].astype(f32)).astype(jnp.bfloat16)


def backward_kernel(
    core_ref,
    tokens_ref,
    cotangent_ref,
    gain_one_ref,
    gain_two_ref,
    ids_ref,
    router_ref,
    middle_ref,
    moe_ref,
    attended_ref,
    hidden_ref,
    q_ref,
    k_ref,
    v_ref,
    probs_ref,
    spots_ref,
    rows_ref,
    *refs,
):
    f32, bf16 = jnp.float32, jnp.bfloat16
    homes, weights = refs[:4], refs[4:8]
    result_ref, tokens_out, kept_ref, given_ref = refs[8:12]
    held, grads_ref, small_ref, sems = refs[12:16]
    copies = start_copies([(w, held.at[i]) for i, w in enumerate(weights)], sems)
    features = tokens_ref.shape[1]
    core = core_ref[0]
    small_ref[...] = jnp.zeros_like(small_ref)

    def leave(mat, left, right):
        grad = lax.dot_general(left, right, FIRST, preferred_element_type=f32).astype(bf16)
        grads_ref[...] = grad
        for x in range(4):
            low = grads_ref[x * 192 : x * 192 + 96, :]
            high = grads_ref[x * 192 + 96 : x * 192 + 192, :]
            at = (mat * 4 + x) * 96
            kept_ref[at : at + 96, :features] = jnp.where(core == 0, low, high)
            given_ref[at : at + 96, :features] = jnp.where(core == 0, high, low)

    def leave_gain(row, gain):
        for x in range(4):
            at = (4 + x) * 96 + row
            small_ref[0, at : at + 1, :] = gain[:, x * 192 : x * 192 + 128]
            small_ref[0, at + 1 : at + 2, :64] = gain[:, x * 192 + 128 : x * 192 + 192]

    home = homes[0][...].astype(f32)
    for piece in homes[1:]:
        home = home + piece[...].astype(f32)
    middle = middle_ref[...]
    result_ref[...] = (middle + home[:, :features]).astype(bf16)
    tail = home[:, features:]
    lane = lax.broadcasted_iota(jnp.int32, tail.shape, 1)
    grad_gates = [
        jnp.sum(jnp.where((lane == k) | (lane == 2 + k), tail, 0.0), axis=1, keepdims=True)
        for k in range(2)
    ]
    moe = moe_ref[...]
    logits = lax.dot_general(moe, router_ref[...], LAST, preferred_element_type=f32)
    ids = [to_column(ids_ref[k : k + 1, : tail.shape[0]]) for k in range(2)]
    gates = gate_pair(chosen_logit(logits, ids[0]), chosen_logit(logits, ids[1]))
    mix = gates[0] * grad_gates[0] + gates[1] * grad_gates[1]
    spots = lax.broadcasted_iota(jnp.int32, logits.shape, 1)
    grad_logits = jnp.zeros(logits.shape, f32)
    for k in range(2):
        grad_logits = jnp.where(spots == ids[k], gates[k] * (grad_gates[k] - mix), grad_logits)
    grad_logits = grad_logits.astype(bf16)
    slot = lax.broadcasted_iota(jnp.int32, (rows_ref.shape[0], tail.shape[0]), 0)
    pick = ((slot == spots_ref[0:1]) | (slot == spots_ref[1:2])).astype(f32).astype(bf16)
    grad_moe = lax.dot_general(pick, rows_ref[...], FIRST, preferred_element_type=f32)
    grad_moe = grad_moe + jnp.dot(grad_logits, router_ref[...], preferred_element_type=f32)
    grad_router = lax.dot_general(moe, grad_logits, FIRST, preferred_element_type=f32)
    for x in range(4):
        for side in range(2):
            begin = x * 192 + side * 96
            small_ref[side, x * 96 : x * 96 + 96, : logits.shape[1]] = grad_router[
                begin : begin + 96, :
            ]
    scale = norm_scale(middle)
    normed = middle * scale
    leave_gain(2, jnp.sum(grad_moe * normed, axis=0, keepdims=True))
    inner = grad_moe * gain_two_ref[...].astype(f32)
    grad_middle = cotangent_ref[...].astype(f32) + scale * (
        inner - normed * jnp.mean(inner * normed, axis=1, keepdims=True)
    )
    branch = grad_middle.astype(bf16)
    leave(3, attended_ref[...], branch)
    copies[3].wait()
    grad_attended = lax.dot_general(branch, held[3], LAST, preferred_element_type=f32).astype(bf16)
    grad_q, grad_k, grad_v, diagonals = [], [], [], []
    for pair in range(probs_ref.shape[0] // 2):
        lanes = slice(pair * 128, pair * 128 + 128)
        q, k, v = q_ref[:, lanes], k_ref[:, lanes], v_ref[:, lanes]
        grad = grad_attended[:, lanes]
        parts = [jnp.zeros(q.shape, f32) for _ in range(3)]
        for side in range(2):
            h = 2 * pair + side
            probs = probs_ref[h]
            grad_half = head_half(grad, side)
            parts[2] = parts[2] + lax.dot_general(
                probs.astype(bf16), grad_half, FIRST, preferred_element_type=f32
            )
            grad_probs = lax.dot_general(grad_half, v, LAST, preferred_element_type=f32)
            grad_scores = (
                probs * (grad_probs - jnp.sum(probs * grad_probs, axis=1, keepdims=True))
            ).astype(bf16)
            diagonals.append(diagonal_sums(grad_scores.astype(f32)))
            parts[0] = parts[0] + jnp.dot(
                grad_scores, head_half(k, side), preferred_element_type=f32
            )
            parts[1] = parts[1] + lax.dot_general(
                grad_scores, head_half(q, side), FIRST, preferred_element_type=f32
            )
        grad_q.append((parts[0] * 0.125).astype(bf16))
        grad_k.append((parts[1] * 0.125).astype(bf16))
        grad_v.append(parts[2].astype(bf16))
    left = jnp.concatenate(diagonals, axis=0)
    grad_bias = jnp.zeros((left.shape[0], 128), f32)
    for _ in range(3):
        part = left.astype(bf16)
        left = left - part.astype(f32)
        grad_bias = grad_bias + jnp.dot(part, bucket_marks(), preferred_element_type=f32)
    per = left.shape[0] // 4
    for x in range(4):
        at = (4 + x) * 96 + 4
        small_ref[0, at : at + per, :] = grad_bias[x * per : x * per + per, :]
    hidden = hidden_ref[...]
    grad_hidden = jnp.zeros(hidden.shape, f32)
    for n, parts in enumerate((grad_q, grad_k, grad_v)):
        grad = jnp.concatenate(parts, axis=1)
        leave(n, hidden, grad)
        copies[n].wait()
        grad_hidden = grad_hidden + lax.dot_general(
            grad, held[n], LAST, preferred_element_type=f32
        )
    x = tokens_ref[...].astype(f32)
    scale = norm_scale(x)
    normed = x * scale
    leave_gain(0, jnp.sum(grad_hidden * normed, axis=0, keepdims=True))
    inner = grad_hidden * gain_one_ref[...].astype(f32)
    tokens_out[...] = grad_middle + scale * (
        inner - normed * jnp.mean(inner * normed, axis=1, keepdims=True)
    )
    low, high = small_ref[0], small_ref[1]
    kept_ref[:, features:] = jnp.where(core == 0, low, high).astype(bf16)
    given_ref[:, features:] = jnp.where(core == 0, high, low).astype(bf16)


ANYWHERE = pl.BlockSpec(memory_space=pl.ANY)
SCALARS = pl.BlockSpec(memory_space=pltpu.SMEM)
WHOLE = pl.BlockSpec(memory_space=pltpu.VMEM)
ROOM = pltpu.CompilerParams(vmem_limit_bytes=56 * 1024 * 1024)


def make_line(routes, gains, bias, router, cotangent):
    tokens, cols = cotangent.shape
    return pl.pallas_call(
        line_kernel,
        out_shape=jax.ShapeDtypeStruct((tokens + 32, cols), jnp.bfloat16),
        in_specs=[WHOLE] * 4 + [ANYWHERE],
        out_specs=WHOLE,
        scratch_shapes=[pltpu.VMEM((32, cols), jnp.float32), pltpu.SemaphoreType.DMA],
        compiler_params=ROOM,
        name="line",
    )(routes, gains, bias, router, cotangent)


def pack(core, mats, after):
    rows, cols = mats[0].shape
    count = len(mats)
    return pl.pallas_call(
        functools.partial(pack_kernel, count),
        out_shape=jax.ShapeDtypeStruct((count * rows // 2, cols), jnp.bfloat16),
        in_specs=[SCALARS] + [ANYWHERE] * (count + 1),
        out_specs=WHOLE,
        scratch_shapes=[pltpu.SemaphoreType.DMA((count,))],
        compiler_params=ROOM,
        name="pack",
    )(core[None], *mats, after)


def attend(where, tokens, gain, bias, mats, near, far, after):
    rows, cols = mats[0].shape
    full = jax.ShapeDtypeStruct((4 * rows, cols), jnp.bfloat16)
    state = jax.ShapeDtypeStruct(tokens.shape, jnp.bfloat16)
    return pl.pallas_call(
        attend_kernel,
        out_shape=[full] * 3 + [state] * 4 + [jax.ShapeDtypeStruct(bias.shape, jnp.float32), state],
        in_specs=[SCALARS] + [WHOLE] * 3 + [ANYWHERE] * 10,
        out_specs=[WHOLE] * 9,
        scratch_shapes=[pltpu.SemaphoreType.DMA((21,))],
        compiler_params=ROOM,
        name="attend",
    )(where, tokens, gain, bias, *mats, *near, *far, after)


def to_middle(where, tokens, gain, attended, mat, near, far, after):
    rows, cols = mat.shape
    return pl.pallas_call(
        middle_kernel,
        out_shape=[
            jax.ShapeDtypeStruct((4 * rows, cols), jnp.bfloat16),
            jax.ShapeDtypeStruct(tokens.shape, jnp.float32),
            jax.ShapeDtypeStruct(tokens.shape, jnp.bfloat16),
        ],
        in_specs=[SCALARS] + [WHOLE] * 3 + [ANYWHERE] * 8,
        out_specs=[WHOLE] * 3,
        scratch_shapes=[pltpu.SemaphoreType.DMA((7,))],
        compiler_params=ROOM,
        name="middle",
    )(where, tokens, gain, attended, mat, *near, *far, after)


def backward(core, *arrays):
    tokens = arrays[0]
    count, features = tokens.shape
    bf16, f32 = jnp.bfloat16, jnp.float32
    shape = jax.ShapeDtypeStruct
    return pl.pallas_call(
        backward_kernel,
        out_shape=[
            shape((count, features), bf16),
            shape((count, features), f32),
            shape((2 * features, features + 128), bf16),
            shape((2 * features, features + 128), bf16),
        ],
        in_specs=[SCALARS] + [WHOLE] * 20 + [ANYWHERE] * 4,
        out_specs=[WHOLE] * 4,
        scratch_shapes=[
            pltpu.VMEM((4, features, features), bf16),
            pltpu.VMEM((features, features), bf16),
            pltpu.VMEM((2, 2 * features, 128), f32),
            pltpu.SemaphoreType.DMA((4,)),
        ],
        compiler_params=ROOM,
        name="backward",
    )(core, *arrays)


def finish_kernel(core_ref, own_ref, other_ref, *refs):
    mats, (router_out, gains_out, bias_out) = refs[:4], refs[4:]
    f32 = jnp.float32
    core = core_ref[0]
    half = own_ref.shape[0] // 4
    features = mats[0].shape[1]
    own, other = own_ref[...].astype(f32), other_ref[...].astype(f32)
    low, high = jnp.where(core == 0, own, other), jnp.where(core == 0, other, own)
    for k, out in enumerate(mats):
        here = slice(k * half, (k + 1) * half)
        out[:half, :] = low[here, :features]
        out[half:, :] = high[here, :features]
    wide = router_out.shape[1]
    router_out[:half, :] = low[:half, features : features + wide]
    router_out[half:, :] = high[:half, features : features + wide]
    small = low[half : 2 * half, features:]
    for k in range(2):
        gains_out[k : k + 1, :128] = small[2 * k : 2 * k + 1, :]
        gains_out[k : k + 1, 128:] = small[2 * k + 1 : 2 * k + 2, :64]
    bias_out[...] = small[4 : 4 + bias_out.shape[0], : bias_out.shape[1]]


def finish(core, own, other, shard_rows, experts_all, bias_shape):
    features = own.shape[1] - 128
    shape = lambda *s: jax.ShapeDtypeStruct(s, jnp.float32)
    return pl.pallas_call(
        finish_kernel,
        out_shape=[shape(shard_rows, features)] * 4
        + [shape(shard_rows, experts_all), shape(2, shard_rows), shape(*bias_shape)],
        in_specs=[SCALARS] + [WHOLE] * 2,
        out_specs=[WHOLE] * 7,
        compiler_params=ROOM,
        name="finish",
    )(core, own, other)


def picks_of(places, e, rows):
    row = lax.broadcasted_iota(jnp.int32, (rows, places.shape[1]), 0) + e * rows
    return ((row == places[0:1]) | (row == places[1:2])).astype(jnp.float32).astype(jnp.bfloat16)


def dispatch_grads_kernel(capacity, *refs):
    pieces, (out_ref, places_ref, ids_ref, spots_ref) = refs[:4], refs[4:]
    f32, bf16, i32 = jnp.float32, jnp.bfloat16, jnp.int32
    rows = out_ref.shape[0]
    tokens = spots_ref.shape[1]
    features = pieces[0].shape[1]
    experts_all = 2 * rows // (4 * capacity)
    expert = lax.broadcasted_iota(i32, (experts_all, tokens), 0)
    down = lax.broadcasted_iota(i32, (tokens, tokens), 0)
    across = lax.broadcasted_iota(i32, (tokens, tokens), 1)
    earlier = (down < across).astype(f32).astype(bf16)
    sums = []
    for r in range(4):
        both = pieces[r][tokens : tokens + 16, :tokens].astype(f32)
        ids = [both[5 + k : 6 + k].astype(i32) for k in range(2)]
        match = [expert == i for i in ids]
        named = (match[0] | match[1]).astype(f32).astype(bf16)
        counts = jnp.dot(named, earlier, preferred_element_type=f32)
        here = slice(r * tokens, (r + 1) * tokens)
        for k in range(2):
            slot = jnp.sum(jnp.where(match[k], counts, 0.0), axis=0, keepdims=True).astype(i32)
            owner, local = ids[k] >> 1, ids[k] & 1
            places_ref[k : k + 1, here] = (
                local * rows + owner * (4 * capacity) + r * capacity + slot
            )
            ids_ref[k : k + 1, here] = ids[k]
            if r == 0:
                spots_ref[k : k + 1, :] = owner * 16 + local * capacity + slot
        sums.append(to_column(both[5:6] + both[6:7]))
    sums = jnp.concatenate(sums, axis=0)
    lanes = lax.broadcasted_iota(i32, (4 * tokens, 128), 1)
    line = jnp.concatenate([p[:tokens, :] for p in pieces], axis=0)
    places = places_ref[...]
    extra = jnp.zeros((rows, 128), f32)
    for e in range(2):
        pick = picks_of(places, e, rows)
        out_ref[:, e * features : (e + 1) * features] = jnp.dot(
            pick, line, preferred_element_type=f32
        ).astype(bf16)
        column = jnp.where(lanes == e, sums, 0.0).astype(bf16)
        extra = extra + jnp.dot(pick, column, preferred_element_type=f32)
    out_ref[:, 2 * features :] = extra.astype(bf16)


def dispatch_grads(pieces, rows, capacity, tokens):
    features = pieces[0].shape[1]
    shape = jax.ShapeDtypeStruct
    return pl.pallas_call(
        functools.partial(dispatch_grads_kernel, capacity),
        out_shape=[
            shape((rows, 2 * features + 128), jnp.bfloat16),
            shape((2, 4 * tokens), jnp.int32),
            shape((2, 4 * tokens), jnp.int32),
            shape((2, tokens), jnp.int32),
        ],
        in_specs=[WHOLE] * 4,
        out_specs=[WHOLE] * 4,
        compiler_params=ROOM,
        name="dispatch_grads",
    )(*pieces)


def dispatch_kernel(places_ref, *refs):
    pieces, out_ref = refs[:4], refs[5]
    rows = out_ref.shape[0]
    features = pieces[0].shape[1]
    line = jnp.concatenate([p[...] for p in pieces], axis=0)
    for e in range(2):
        out_ref[:, e * features : (e + 1) * features] = jnp.dot(
            picks_of(places_ref[...], e, rows), line, preferred_element_type=jnp.float32
        ).astype(jnp.bfloat16)


def dispatch(places, pieces, rows, after):
    return pl.pallas_call(
        dispatch_kernel,
        out_shape=jax.ShapeDtypeStruct((rows, 2 * pieces[0].shape[1]), jnp.bfloat16),
        in_specs=[WHOLE] * 5 + [ANYWHERE],
        out_specs=WHOLE,
        compiler_params=ROOM,
        name="dispatch",
    )(places, *pieces, after)


def chosen_logit(logits, ids):
    lanes = lax.broadcasted_iota(jnp.int32, logits.shape, 1)
    return jnp.sum(jnp.where(lanes == ids, logits, 0.0), axis=1, keepdims=True)


def gate_pair(first, second):
    top = jnp.maximum(first, second)
    one, two = jnp.exp(first - top), jnp.exp(second - top)
    total = one + two
    return one / total, two / total


def expert_kernel(x_ref, in_ref, out_ref, ret_ref, act_ref, rise_ref):
    f32, bf16 = jnp.float32, jnp.bfloat16
    step = 256
    slope = math.sqrt(2.0 / math.pi)

    def chunk(i, carry):
        at = pl.ds(pl.multiple_of(i * step, step), step)
        pre = jnp.dot(x_ref[at, :], in_ref[0], preferred_element_type=f32)
        tanh = jnp.tanh(slope * (pre + 0.044715 * (pre * pre * pre)))
        active = (0.5 * pre * (1.0 + tanh)).astype(bf16)
        act_ref[0, at, :] = active
        ret_ref[at, :] = jnp.dot(active, out_ref[0], preferred_element_type=f32).astype(bf16)
        rise_ref[0, at, :] = 0.5 * (1.0 + tanh) + 0.5 * pre * (1.0 - tanh * tanh) * (
            slope * (1.0 + 3.0 * 0.044715 * (pre * pre))
        )
        return carry

    lax.fori_loop(0, x_ref.shape[0] // step, chunk, 0)


def lanes_of(rows, n):
    return pl.BlockSpec((rows, n), lambda e: (0, e))


def one_of(a, b):
    return pl.BlockSpec((1, a, b), lambda e: (e, 0, 0))


def experts(arrived, w_in, w_out):
    rows = arrived.shape[0]
    features, hidden = w_in.shape[1:]
    return pl.pallas_call(
        expert_kernel,
        grid=(2,),
        out_shape=[
            jax.ShapeDtypeStruct((rows, 2 * features), jnp.bfloat16),
            jax.ShapeDtypeStruct((2, rows, hidden), jnp.bfloat16),
            jax.ShapeDtypeStruct((2, rows, hidden), jnp.float32),
        ],
        in_specs=[lanes_of(rows, features), one_of(features, hidden), one_of(hidden, features)],
        out_specs=[lanes_of(rows, features), one_of(rows, hidden), one_of(rows, hidden)],
        compiler_params=ROOM,
        name="experts",
    )(arrived, w_in, w_out)


def expert_back_kernel(
    capacity, own_ref, x_ref, g_ref, ids_ref, in_ref, out_ref, router_ref, rise_ref, *refs
):
    pre_ref, arr_ref, outs, held = refs[0], refs[1], refs[2:6], refs[6]
    f32, bf16, i32 = jnp.float32, jnp.bfloat16, jnp.int32
    e = pl.program_id(0)
    own = own_ref[0] + e
    rows = x_ref.shape[0]
    step = 256

    def chunk(i, carry):
        at = pl.ds(pl.multiple_of(i * step, step), step)
        ids = ids_ref[at, :].astype(f32)
        lanes = lax.broadcasted_iota(i32, ids.shape, 1)
        other = jnp.sum(jnp.where(lanes == e, ids, 0.0), axis=1, keepdims=True).astype(i32) - own
        logits = lax.dot_general(
            x_ref[at, :], router_ref[...], LAST, preferred_element_type=f32
        )
        gate, _ = gate_pair(chosen_logit(logits, own), chosen_logit(logits, other))
        grown = (gate * g_ref[at, :].astype(f32)).astype(bf16)
        arr_ref[0, at, :] = grown
        back = lax.dot_general(grown, out_ref[0], LAST, preferred_element_type=f32)
        grad = (back * rise_ref[0, at, :]).astype(bf16)
        pre_ref[0, at, :] = grad
        held[at, :] = lax.dot_general(grad, in_ref[0], LAST, preferred_element_type=f32).astype(
            bf16
        )
        return carry

    lax.fori_loop(0, rows // step, chunk, 0)
    part = rows // 4
    here = lax.broadcasted_iota(i32, (part, rows), 0)
    there = lax.broadcasted_iota(i32, (part, rows), 1)
    block = (here * (65536 // capacity + 1)) >> 16
    for r, out in enumerate(outs):
        source = here + block * (3 * capacity) + r * capacity
        pick = (there == source).astype(f32).astype(bf16)
        out[...] = jnp.dot(pick, held[...], preferred_element_type=f32).astype(bf16)


def experts_back(own, arrived, grad_wide, w_in, w_out, router_w, rise, capacity):
    rows = arrived.shape[0]
    features, hidden = w_in.shape[1:]
    bf16 = jnp.bfloat16
    shape = jax.ShapeDtypeStruct
    part = rows // 4
    return pl.pallas_call(
        functools.partial(expert_back_kernel, capacity),
        grid=(2,),
        out_shape=[shape((2, rows, hidden), bf16), shape((2, rows, features), bf16)]
        + [shape((2 * part, features), bf16)] * 4,
        in_specs=[
            SCALARS,
            lanes_of(rows, features),
            lanes_of(rows, features),
            pl.BlockSpec((rows, 128), lambda e: (0, 2 * features // 128)),
            one_of(features, hidden),
            one_of(hidden, features),
            pl.BlockSpec(router_w.shape, lambda e: (0, 0)),
            one_of(rows, hidden),
        ],
        out_specs=[one_of(rows, hidden), one_of(rows, features)]
        + [pl.BlockSpec((part, features), lambda e: (e, 0))] * 4,
        scratch_shapes=[pltpu.VMEM((rows, features), bf16)],
        compiler_params=ROOM,
        name="experts_back",
    )(own[None], arrived, grad_wide, grad_wide, w_in, w_out, router_w, rise)


def weight_grads_kernel(x_ref, pre_ref, act_ref, arr_ref, in_ref, out_ref):
    in_ref[0] = lax.dot_general(x_ref[...], pre_ref[0], FIRST, preferred_element_type=jnp.float32)
    out_ref[0] = lax.dot_general(act_ref[0], arr_ref[0], FIRST, preferred_element_type=jnp.float32)


def weight_grads(arrived, grad_pre, active, grad_arrived):
    rows = arrived.shape[0]
    hidden, features = grad_pre.shape[2], grad_arrived.shape[2]
    step = 256
    cuts = features // step
    whole = lambda n: pl.BlockSpec((1, rows, n), lambda e, j: (e, 0, 0))
    out = lambda n: pl.BlockSpec((1, step, n), lambda e, j: (e, j, 0))
    return pl.pallas_call(
        weight_grads_kernel,
        grid=(2, cuts),
        out_shape=[
            jax.ShapeDtypeStruct((2, features, hidden), jnp.float32),
            jax.ShapeDtypeStruct((2, hidden, features), jnp.float32),
        ],
        in_specs=[
            pl.BlockSpec((rows, step), lambda e, j: (0, e * cuts + j)),
            whole(hidden),
            pl.BlockSpec((1, rows, step), lambda e, j: (e, 0, j)),
            whole(features),
        ],
        out_specs=[out(hidden), out(features)],
        compiler_params=ROOM,
        cost_estimate=pl.CostEstimate(
            flops=8 * rows * features * hidden, bytes_accessed=20_000_000, transcendentals=0
        ),
        name="weight_grads",
    )(arrived, grad_pre, active, grad_arrived)


def sum_rows_kernel(capacity, *refs):
    pieces, out_ref = refs[:4], refs[-1]
    f32, bf16, i32 = jnp.float32, jnp.bfloat16, jnp.int32
    total = pieces[0][...].astype(f32)
    for piece in pieces[1:]:
        total = total + piece[...].astype(f32)
    rows = out_ref.shape[0]
    part = total.shape[0] // 2
    here = lax.broadcasted_iota(i32, (rows, 2 * part), 0)
    there = lax.broadcasted_iota(i32, (rows, 2 * part), 1)
    owner, q = here >> 4, here & 15
    second = q >= capacity
    source = owner * capacity + jnp.where(second, part + q - capacity, q)
    pick = ((there == source) & (q < 2 * capacity)).astype(f32).astype(bf16)
    out_ref[...] = jnp.dot(pick, total.astype(bf16), preferred_element_type=f32).astype(bf16)


def sum_rows(pieces, capacity, after):
    rows, features = pieces[0].shape
    return pl.pallas_call(
        functools.partial(sum_rows_kernel, capacity),
        out_shape=jax.ShapeDtypeStruct((rows // (2 * capacity) * 16, features), jnp.bfloat16),
        in_specs=[WHOLE] * 4 + [ANYWHERE] * len(after),
        out_specs=WHOLE,
        compiler_params=ROOM,
        name="sum_rows",
    )(*pieces, *after)


def combine_kernel(places_ref, ids_ref, router_ref, ret_ref, *refs):
    f32, bf16 = jnp.float32, jnp.bfloat16
    grads, moes, outs = refs[:4], refs[4:8], refs[9:13]
    tokens, features = moes[0].shape
    rows = ret_ref.shape[0]
    row = lax.broadcasted_iota(jnp.int32, (rows, tokens), 0)
    tail_lane = lax.broadcasted_iota(jnp.int32, (tokens, 128), 1)
    for r in range(4):
        here = slice(r * tokens, (r + 1) * tokens)
        logits = lax.dot_general(
            moes[r][...], router_ref[...], LAST, preferred_element_type=f32
        )
        ids = [to_column(ids_ref[k : k + 1, here]) for k in range(2)]
        gates = gate_pair(chosen_logit(logits, ids[0]), chosen_logit(logits, ids[1]))
        total = jnp.zeros((tokens, features), f32)
        tail = jnp.zeros((tokens, 128), f32)
        grad = grads[r][:tokens, :].astype(f32)
        for k in range(2):
            got = jnp.zeros((tokens, features), f32)
            for e in range(2):
                pick = (row + e * rows == places_ref[k : k + 1, here]).astype(f32).astype(bf16)
                got = got + lax.dot_general(
                    pick,
                    ret_ref[:, e * features : (e + 1) * features],
                    FIRST,
                    preferred_element_type=f32,
                )
            total = total + gates[k] * got
            dots = jnp.sum(grad * got, axis=1, keepdims=True)
            high = dots.astype(bf16).astype(f32)
            tail = jnp.where(tail_lane == k, high, tail)
            tail = jnp.where(tail_lane == 2 + k, dots - high, tail)
        outs[r][:, :features] = total.astype(bf16)
        outs[r][:, features:] = tail.astype(bf16)


def combine(places, ids, router_w, returned, grads, moes, after):
    tokens, features = moes[0].shape
    return pl.pallas_call(
        combine_kernel,
        out_shape=[jax.ShapeDtypeStruct((tokens, features + 128), jnp.bfloat16)] * 4,
        in_specs=[WHOLE] * 12 + [ANYWHERE],
        out_specs=[WHOLE] * 4,
        compiler_params=ROOM,
        name="combine",
    )(places, ids, router_w, returned, *grads, *moes, after)


def layer(
    tokens,
    seq_lengths,
    routes,
    gain_attn,
    w_query,
    w_key,
    w_value,
    w_output,
    rel_bias,
    gain_moe,
    w_router,
    w_in,
    w_out,
    cotangent,
):
    row_count, features = tokens.shape
    shard_rows = w_query.shape[0]
    expert_count = w_router.shape[1]
    bucket_count = rel_bias.shape[1]
    head_count = 4 * rel_bias.shape[0]
    capacity = 3 * row_count // expert_count
    f32 = jnp.float32
    bf16 = jnp.bfloat16

    shard = lax.axis_index("x").astype(jnp.int32)
    core = lax.axis_index("c").astype(jnp.int32)
    where = jnp.stack([shard, core])
    owners = expert_count // 2
    slot_rows = owners * 4 * capacity

    line = make_line(
        routes.T, jnp.stack([gain_attn, gain_moe]), rel_bias, w_router.T, cotangent
    )
    line_grads = along_x(line)
    near_qkv = along_x(pack(core, (w_query, w_key, w_value), line))[1:]
    order = (shard - jnp.arange(4)) % 4
    small = jnp.take(jnp.stack([p[row_count:] for p in line_grads]), order, axis=0)
    gain_one = small[:, 0, :shard_rows].reshape(1, features)
    gain_two = small[:, 1, :shard_rows].reshape(1, features)
    bias_table = small[:, 2:5, :bucket_count].reshape(head_count, bucket_count)
    router_w = (
        small[:, 16:]
        .reshape(4, 16, expert_count // 16, shard_rows)
        .transpose(2, 1, 0, 3)
        .reshape(expert_count, features)
    )

    def to_owners(outgoing):
        return lax.all_to_all(outgoing, ("y", "z", "c"), 0, 0, tiled=True)

    outgoing_grads, places, ids, spots = dispatch_grads(
        line_grads, slot_rows, capacity, row_count
    )
    grad_wide = to_owners(outgoing_grads)
    near_out = along_x(pack(core, (w_output,), outgoing_grads))[1:]
    first_expert = 2 * lax.axis_index(("y", "z", "c")).astype(jnp.int32)

    segments = row_segments(seq_lengths[0], row_count)
    distance, onehot = position_tables(row_count, bucket_count)
    allowed = (segments[:, None] == segments[None, :]) & (distance >= 0)
    position_bias = jnp.einsum("ijb,hb->hij", onehot, bias_table, preferred_element_type=f32)
    masked_bias = jnp.where(allowed[None], position_bias, -1000000000.0)
    far_qkv = [swap_core(part) for part in near_qkv]
    far_out = [swap_core(part) for part in near_out]
    query_w, key_w, value_w, hidden_one, queries, key_rows, value_rows, probs, attended = attend(
        where,
        tokens,
        gain_one,
        masked_bias,
        (w_query, w_key, w_value),
        near_qkv,
        far_qkv,
        outgoing_grads,
    )
    output_w, middle, moe_in = to_middle(
        where, tokens, gain_two, attended, w_output, near_out, far_out, outgoing_grads
    )

    line_moe = along_x(moe_in)
    arrived = to_owners(dispatch(places, line_moe, slot_rows, grad_wide))
    ret, active, rise = experts(arrived, w_in, w_out)
    returned = to_owners(ret)
    grad_pre, grad_arrived, *blocks = experts_back(
        first_expert, arrived, grad_wide, w_in, w_out, router_w, rise, capacity
    )
    summed = [blocks[0]] + [shift_x(blocks[r], -r) for r in range(1, 4)]
    grad_w_in, grad_w_out = weight_grads(arrived, grad_pre, active, grad_arrived)
    rows_home = sum_rows(summed, capacity, (grad_w_in, grad_w_out))
    back_rows = to_owners(rows_home)
    bundle = combine(places, ids, router_w, returned, line_grads, line_moe, rows_home)
    homes = [bundle[0]] + [shift_x(bundle[r], -r) for r in range(1, 4)]
    result, grad_tokens, kept, given = backward(
        core[None],
        tokens,
        cotangent,
        gain_one,
        gain_two,
        ids,
        router_w,
        middle,
        moe_in,
        attended,
        hidden_one,
        queries,
        key_rows,
        value_rows,
        probs,
        spots,
        back_rows,
        *homes,
        query_w,
        key_w,
        value_w,
        output_w,
    )
    piece = shard_rows // 8
    wide = features + 128
    paired = (kept.astype(f32) + swap_core(given).astype(f32)).astype(bf16)
    spread = lax.all_to_all(paired, ("y", "x", "z"), 0, 0, tiled=True)
    mine = jnp.sum(spread.reshape(64, piece, wide).astype(f32), axis=0).astype(bf16)
    half = lax.all_to_all(
        jnp.broadcast_to(mine[None], (16, piece, wide)).reshape(16 * piece, wide),
        ("y", "z"),
        0,
        0,
        tiled=True,
    )
    *totals, router_total, gain_totals, bias_total = finish(
        core[None], half, swap_core(half), shard_rows, expert_count, rel_bias.shape
    )
    gain_one_total, gain_two_total = gain_totals[0], gain_totals[1]
    return (
        result,
        grad_tokens,
        gain_one_total,
        totals[0],
        totals[1],
        totals[2],
        totals[3],
        bias_total,
        gain_two_total,
        router_total,
        grad_w_in,
        grad_w_out,
    )


def solution(mesh):
    cube = Mesh(mesh.devices.reshape(4, 4, 2, 4), ("y", "z", "c", "x"))
    expert = ("y", "z", "c")
    everyone = ("y", "z", "c", "x")
    placed = (
        P(everyone, None),
        P(everyone, None),
        P(everyone, None),
        P("x"),
        P("x", None),
        P("x", None),
        P("x", None),
        P("x", None),
        P("x", None),
        P("x"),
        P("x", None),
        P(expert, None, "x"),
        P(expert, "x", None),
        P(everyone, None),
    )
    return jax.shard_map(
        layer,
        mesh=cube,
        in_specs=placed,
        out_specs=(
            P(everyone, None),
            P(everyone, None),
            P("x"),
            P("x", None),
            P("x", None),
            P("x", None),
            P("x", None),
            P("x", None),
            P("x"),
            P("x", None),
            P(expert, None, "x"),
            P(expert, "x", None),
        ),
        check_vma=False,
    )
```

```python
import functools
import math

import jax
import jax.numpy as jnp
from jax import lax
from jax.experimental import pallas as pl
from jax.experimental.pallas import tpu as pltpu
from jax.sharding import Mesh, PartitionSpec as P

epsilon = 1e-06
bucket_edges = list(range(1, 17)) + [
    int(math.ceil(16.0 * 8.0 ** ((bucket_level - 16) / 16.0))) for bucket_level in range(17, 32)
]


def row_segments(lengths, row_count):
    sequence_ends = jnp.cumsum(lengths)
    positions = jnp.arange(row_count, dtype=jnp.int32)
    return jnp.sum((positions[:, None] >= sequence_ends[None, :]).astype(jnp.int32), axis=1)


def position_tables(row_count, bucket_count):
    positions = jnp.arange(row_count, dtype=jnp.int32)
    distance = positions[:, None] - positions[None, :]
    edge_values = jnp.array(bucket_edges, dtype=jnp.int32)
    bucket = jnp.sum((distance[:, :, None] >= edge_values).astype(jnp.int32), axis=2)
    onehot = (bucket[:, :, None] == jnp.arange(bucket_count, dtype=jnp.int32)).astype(jnp.bfloat16)
    return (distance, onehot)


def shift(block, axis, step):
    ranks = lax.axis_size(axis)
    return lax.ppermute(block, axis, [(i, (i + step) % ranks) for i in range(ranks)])


def shift_x(block, step):
    return shift(block, "x", step)


def swap_core(block):
    return lax.ppermute(block, "c", [(0, 1), (1, 0)])


def along_x(block):
    return [block, shift_x(block, 1), shift_x(block, 2), shift_x(block, 3)]


def line_kernel(routes_ref, gains_ref, bias_ref, router_ref, cotangent_ref, line_ref, held, sem):
    f32 = jnp.float32
    tokens = cotangent_ref.shape[0]
    copy = pltpu.make_async_copy(cotangent_ref, line_ref.at[pl.ds(0, tokens)], sem)
    copy.start()
    held[...] = jnp.zeros_like(held)
    held[0:2, : gains_ref.shape[1]] = gains_ref[...].astype(f32)
    held[2:5, : bias_ref.shape[1]] = bias_ref[...].astype(f32)
    held[5:7, :tokens] = routes_ref[...].astype(f32)
    width = router_ref.shape[1]
    for b in range(router_ref.shape[0] // 16):
        part = router_ref[16 * b : 16 * b + 16, :].astype(f32)
        held[16:32, width * b : width * (b + 1)] = part
    line_ref[tokens:, :] = held[...].astype(jnp.bfloat16)
    copy.wait()


def pack_kernel(count, core_ref, *refs):
    mats, out_ref, sems = refs[:count], refs[count + 1], refs[count + 2]
    half = mats[0].shape[0] // 2
    start = pl.multiple_of(core_ref[0] * half, half)
    copies = start_copies(
        [
            (m.at[pl.ds(start, half)], out_ref.at[pl.ds(k * half, half)])
            for k, m in enumerate(mats)
        ],
        sems,
    )
    for c in copies:
        c.wait()


def start_copies(pairs, sems):
    copies = [pltpu.make_async_copy(s, d, sems.at[i]) for i, (s, d) in enumerate(pairs)]
    for c in copies:
        c.start()
    return copies


def block_copies(shard, core, mats, near, far, outs):
    rows = mats[0].shape[0]
    half = rows // 2
    pairs = []
    for k, (mat, out) in enumerate(zip(mats, outs)):
        begin = pl.multiple_of(shard * rows, rows)
        pairs.append((mat, out.at[pl.ds(begin, rows)]))
        part = pl.ds(k * half, half)
        for r in range(1, 4):
            begin = lax.rem(shard + (4 - r), 4) * rows
            mine = pl.multiple_of(begin + core * half, half)
            other = pl.multiple_of(begin + (1 - core) * half, half)
            pairs.append((near[r - 1].at[part], out.at[pl.ds(mine, half)]))
            pairs.append((far[r - 1].at[part], out.at[pl.ds(other, half)]))
    return pairs


def norm_scale(x):
    return lax.rsqrt(jnp.mean(x * x, axis=1, keepdims=True) + epsilon)


def head_half(block, side):
    lanes = lax.broadcasted_iota(jnp.int32, block.shape, 1)
    keep = (lanes < 64) if side == 0 else (lanes >= 64)
    return jnp.where(keep, block, jnp.zeros_like(block))


def to_column(row):
    n = row.shape[1]
    down = lax.broadcasted_iota(jnp.int32, (n, n), 0)
    across = lax.broadcasted_iota(jnp.int32, (n, n), 1)
    return jnp.sum(jnp.where(down == across, row, jnp.zeros_like(row)), axis=1, keepdims=True)


def diagonal_sums(scores):
    n = scores.shape[0]
    down = lax.broadcasted_iota(jnp.int32, (n, n), 0)
    step = 1
    while step < n:
        turned = pltpu.roll(scores, n - step, axis=1)
        scores = jnp.where((down & step) != 0, turned, scores)
        step *= 2
    return jnp.sum(scores, axis=0, keepdims=True)


def bucket_marks():
    shape = (128, 128)
    distance = (128 - lax.broadcasted_iota(jnp.int32, shape, 0)) & 127
    bucket = jnp.zeros(shape, jnp.int32)
    for edge in bucket_edges:
        bucket = bucket + (distance >= edge).astype(jnp.int32)
    mark = bucket == lax.broadcasted_iota(jnp.int32, shape, 1)
    return mark.astype(jnp.float32).astype(jnp.bfloat16)


LAST = (((1,), (1,)), ((), ()))
FIRST = (((0,), (0,)), ((), ()))


def attend_kernel(place_ref, tokens_ref, gain_ref, bias_ref, *refs):
    f32, bf16 = jnp.float32, jnp.bfloat16
    mats, near, far = refs[:3], refs[3:6], refs[6:9]
    weights = refs[10:13]
    hidden_ref, q_ref, k_ref, v_ref, probs_ref, attended_ref, sems = refs[13:20]
    copies = start_copies(
        block_copies(place_ref[0], place_ref[1], mats, near, far, weights), sems
    )
    x = tokens_ref[...].astype(f32)
    hidden = (x * norm_scale(x) * gain_ref[...].astype(f32)).astype(bf16)
    hidden_ref[...] = hidden
    for n, (w, out) in enumerate(zip(weights, (q_ref, k_ref, v_ref))):
        for c in copies[7 * n : 7 * n + 7]:
            c.wait()
        out[...] = jnp.dot(hidden, w[...], preferred_element_type=f32).astype(bf16)
    heads = bias_ref.shape[0]
    for pair in range(heads // 2):
        lanes = slice(pair * 128, pair * 128 + 128)
        q, k, v = q_ref[:, lanes], k_ref[:, lanes], v_ref[:, lanes]
        total = jnp.zeros(q.shape, f32)
        for side in range(2):
            h = 2 * pair + side
            scores = lax.dot_general(q, head_half(k, side), LAST, preferred_element_type=f32)
            scores = scores * 0.125 + bias_ref[h]
            top = jnp.max(scores, axis=1, keepdims=True)
            grown = jnp.exp(scores - top)
            probs = grown / jnp.sum(grown, axis=1, keepdims=True)
            probs_ref[h] = probs
            total = total + jnp.dot(
                probs.astype(bf16), head_half(v, side), preferred_element_type=f32
            )
        attended_ref[:, lanes] = total.astype(bf16)


def middle_kernel(place_ref, tokens_ref, gain_ref, attended_ref, *refs):
    f32 = jnp.float32
    mats, near, far = refs[:1], refs[1:4], refs[4:7]
    weight, middle_ref, moe_ref, sems = refs[8:12]
    copies = start_copies(
        block_copies(place_ref[0], place_ref[1], mats, near, far, [weight]), sems
    )
    for c in copies:
        c.wait()
    middle = tokens_ref[...].astype(f32) + jnp.dot(
        attended_ref[...], weight[...], preferred_element_type=f32
    )
    middle_ref[...] = middle
    moe_ref[...] = (middle * norm_scale(middle) * gain_ref[...].astype(f32)).astype(jnp.bfloat16)


def backward_kernel(
    place_ref,
    tokens_ref,
    cotangent_ref,
    gain_one_ref,
    gain_two_ref,
    ids_ref,
    router_ref,
    middle_ref,
    moe_ref,
    attended_ref,
    hidden_ref,
    q_ref,
    k_ref,
    v_ref,
    probs_ref,
    spots_ref,
    rows_ref,
    *refs,
):
    f32, bf16 = jnp.float32, jnp.bfloat16
    homes, weights = refs[:4], refs[4:8]
    result_ref, tokens_out, kept_ref, given_ref = refs[8:12]
    smalls, (held, grads_ref, small_ref, sems) = refs[12:16], refs[16:20]
    copies = start_copies([(w, held.at[i]) for i, w in enumerate(weights)], sems)
    features = tokens_ref.shape[1]
    core = place_ref[1]
    width = features // 4
    small_ref[...] = jnp.zeros_like(small_ref)

    def leave(mat, left, right):
        grad = lax.dot_general(left, right, FIRST, preferred_element_type=f32).astype(bf16)
        grads_ref[...] = grad
        for x in range(4):
            low = grads_ref[x * 192 : x * 192 + 96, :]
            high = grads_ref[x * 192 + 96 : x * 192 + 192, :]
            at = (mat * 4 + x) * 96
            kept_ref[at : at + 96, :] = jnp.where(core == 0, low, high)
            given_ref[at : at + 96, :] = jnp.where(core == 0, high, low)

    def leave_small(row, block):
        for a in range(4):
            small_ref[a, row : row + block.shape[0], :width] = block[:, a * width : (a + 1) * width]

    home = homes[0][...].astype(f32)
    for piece in homes[1:]:
        home = home + piece[...].astype(f32)
    middle = middle_ref[...]
    result_ref[...] = (middle + home[:, :features]).astype(bf16)
    tail = home[:, features:]
    lane = lax.broadcasted_iota(jnp.int32, tail.shape, 1)
    grad_gates = [
        jnp.sum(jnp.where((lane == k) | (lane == 2 + k), tail, 0.0), axis=1, keepdims=True)
        for k in range(2)
    ]
    moe = moe_ref[...]
    logits = lax.dot_general(moe, router_ref[...], LAST, preferred_element_type=f32)
    ids = [to_column(ids_ref[k : k + 1, : tail.shape[0]]) for k in range(2)]
    gates = gate_pair(chosen_logit(logits, ids[0]), chosen_logit(logits, ids[1]))
    mix = gates[0] * grad_gates[0] + gates[1] * grad_gates[1]
    spots = lax.broadcasted_iota(jnp.int32, logits.shape, 1)
    grad_logits = jnp.zeros(logits.shape, f32)
    for k in range(2):
        grad_logits = jnp.where(spots == ids[k], gates[k] * (grad_gates[k] - mix), grad_logits)
    grad_logits = grad_logits.astype(bf16)
    slot = lax.broadcasted_iota(jnp.int32, (rows_ref.shape[0], tail.shape[0]), 0)
    pick = ((slot == spots_ref[0:1]) | (slot == spots_ref[1:2])).astype(f32).astype(bf16)
    grad_moe = lax.dot_general(pick, rows_ref[...], FIRST, preferred_element_type=f32)
    grad_moe = grad_moe + jnp.dot(grad_logits, router_ref[...], preferred_element_type=f32)
    leave_small(0, lax.dot_general(grad_logits, moe, FIRST, preferred_element_type=f32))
    scale = norm_scale(middle)
    normed = middle * scale
    leave_small(65, jnp.sum(grad_moe * normed, axis=0, keepdims=True))
    inner = grad_moe * gain_two_ref[...].astype(f32)
    grad_middle = cotangent_ref[...].astype(f32) + scale * (
        inner - normed * jnp.mean(inner * normed, axis=1, keepdims=True)
    )
    branch = grad_middle.astype(bf16)
    leave(3, attended_ref[...], branch)
    copies[3].wait()
    grad_attended = lax.dot_general(branch, held[3], LAST, preferred_element_type=f32).astype(bf16)
    grad_q, grad_k, grad_v, diagonals = [], [], [], []
    for pair in range(probs_ref.shape[0] // 2):
        lanes = slice(pair * 128, pair * 128 + 128)
        q, k, v = q_ref[:, lanes], k_ref[:, lanes], v_ref[:, lanes]
        grad = grad_attended[:, lanes]
        parts = [jnp.zeros(q.shape, f32) for _ in range(3)]
        for side in range(2):
            h = 2 * pair + side
            probs = probs_ref[h]
            grad_half = head_half(grad, side)
            parts[2] = parts[2] + lax.dot_general(
                probs.astype(bf16), grad_half, FIRST, preferred_element_type=f32
            )
            grad_probs = lax.dot_general(grad_half, v, LAST, preferred_element_type=f32)
            grad_scores = (
                probs * (grad_probs - jnp.sum(probs * grad_probs, axis=1, keepdims=True))
            ).astype(bf16)
            diagonals.append(diagonal_sums(grad_scores.astype(f32)))
            parts[0] = parts[0] + jnp.dot(
                grad_scores, head_half(k, side), preferred_element_type=f32
            )
            parts[1] = parts[1] + lax.dot_general(
                grad_scores, head_half(q, side), FIRST, preferred_element_type=f32
            )
        grad_q.append((parts[0] * 0.125).astype(bf16))
        grad_k.append((parts[1] * 0.125).astype(bf16))
        grad_v.append(parts[2].astype(bf16))
    left = jnp.concatenate(diagonals, axis=0)
    grad_bias = jnp.zeros((left.shape[0], 128), f32)
    for _ in range(3):
        part = left.astype(bf16)
        left = left - part.astype(f32)
        grad_bias = grad_bias + jnp.dot(part, bucket_marks(), preferred_element_type=f32)
    per = left.shape[0] // 4
    for a in range(4):
        small_ref[a, 66 : 66 + per, :128] = grad_bias[a * per : a * per + per, :]
    hidden = hidden_ref[...]
    grad_hidden = jnp.zeros(hidden.shape, f32)
    for n, parts in enumerate((grad_q, grad_k, grad_v)):
        grad = jnp.concatenate(parts, axis=1)
        leave(n, hidden, grad)
        copies[n].wait()
        grad_hidden = grad_hidden + lax.dot_general(
            grad, held[n], LAST, preferred_element_type=f32
        )
    x = tokens_ref[...].astype(f32)
    scale = norm_scale(x)
    normed = x * scale
    leave_small(64, jnp.sum(grad_hidden * normed, axis=0, keepdims=True))
    inner = grad_hidden * gain_one_ref[...].astype(f32)
    tokens_out[...] = grad_middle + scale * (
        inner - normed * jnp.mean(inner * normed, axis=1, keepdims=True)
    )
    for r, out in enumerate(smalls):
        at = (place_ref[0] - r) & 3
        small = small_ref[0]
        for a in range(1, 4):
            small = jnp.where(at == a, small_ref[a], small)
        out[...] = small.astype(bf16)


ANYWHERE = pl.BlockSpec(memory_space=pl.ANY)
SCALARS = pl.BlockSpec(memory_space=pltpu.SMEM)
WHOLE = pl.BlockSpec(memory_space=pltpu.VMEM)
ROOM = pltpu.CompilerParams(vmem_limit_bytes=56 * 1024 * 1024)


def make_line(routes, gains, bias, router, cotangent):
    tokens, cols = cotangent.shape
    return pl.pallas_call(
        line_kernel,
        out_shape=jax.ShapeDtypeStruct((tokens + 32, cols), jnp.bfloat16),
        in_specs=[WHOLE] * 4 + [ANYWHERE],
        out_specs=WHOLE,
        scratch_shapes=[pltpu.VMEM((32, cols), jnp.float32), pltpu.SemaphoreType.DMA],
        compiler_params=ROOM,
        name="line",
    )(routes, gains, bias, router, cotangent)


def pack(core, mats, after):
    rows, cols = mats[0].shape
    count = len(mats)
    return pl.pallas_call(
        functools.partial(pack_kernel, count),
        out_shape=jax.ShapeDtypeStruct((count * rows // 2, cols), jnp.bfloat16),
        in_specs=[SCALARS] + [ANYWHERE] * (count + 1),
        out_specs=WHOLE,
        scratch_shapes=[pltpu.SemaphoreType.DMA((count,))],
        compiler_params=ROOM,
        name="pack",
    )(core[None], *mats, after)


def attend(where, tokens, gain, bias, mats, near, far, after):
    rows, cols = mats[0].shape
    full = jax.ShapeDtypeStruct((4 * rows, cols), jnp.bfloat16)
    state = jax.ShapeDtypeStruct(tokens.shape, jnp.bfloat16)
    return pl.pallas_call(
        attend_kernel,
        out_shape=[full] * 3 + [state] * 4 + [jax.ShapeDtypeStruct(bias.shape, jnp.float32), state],
        in_specs=[SCALARS] + [WHOLE] * 3 + [ANYWHERE] * 10,
        out_specs=[WHOLE] * 9,
        scratch_shapes=[pltpu.SemaphoreType.DMA((21,))],
        compiler_params=ROOM,
        name="attend",
    )(where, tokens, gain, bias, *mats, *near, *far, after)


def to_middle(where, tokens, gain, attended, mat, near, far, after):
    rows, cols = mat.shape
    return pl.pallas_call(
        middle_kernel,
        out_shape=[
            jax.ShapeDtypeStruct((4 * rows, cols), jnp.bfloat16),
            jax.ShapeDtypeStruct(tokens.shape, jnp.float32),
            jax.ShapeDtypeStruct(tokens.shape, jnp.bfloat16),
        ],
        in_specs=[SCALARS] + [WHOLE] * 3 + [ANYWHERE] * 8,
        out_specs=[WHOLE] * 3,
        scratch_shapes=[pltpu.SemaphoreType.DMA((7,))],
        compiler_params=ROOM,
        name="middle",
    )(where, tokens, gain, attended, mat, *near, *far, after)


def backward(where, *arrays):
    tokens = arrays[0]
    count, features = tokens.shape
    bf16, f32 = jnp.bfloat16, jnp.float32
    shape = jax.ShapeDtypeStruct
    return pl.pallas_call(
        backward_kernel,
        out_shape=[
            shape((count, features), bf16),
            shape((count, features), f32),
            shape((2 * features, features), bf16),
            shape((2 * features, features), bf16),
        ]
        + [shape((80, 256), bf16)] * 4,
        in_specs=[SCALARS] + [WHOLE] * 20 + [ANYWHERE] * 4,
        out_specs=[WHOLE] * 8,
        scratch_shapes=[
            pltpu.VMEM((4, features, features), bf16),
            pltpu.VMEM((features, features), bf16),
            pltpu.VMEM((4, 80, 256), f32),
            pltpu.SemaphoreType.DMA((4,)),
        ],
        compiler_params=ROOM,
        name="backward",
    )(where, *arrays)


def pair_kernel(kept_ref, got_ref, *refs):
    f32 = jnp.float32
    smalls, out_ref, passed = refs[:4], refs[4], refs[5:]
    out_ref[...] = (kept_ref[...].astype(f32) + got_ref[...].astype(f32)).astype(jnp.bfloat16)
    for small, out in zip(smalls, passed):
        out[...] = small[...]


def pair(kept, got, smalls):
    rows, features = kept.shape
    block = pl.BlockSpec((rows // 4, features), lambda i: (i, 0))
    small = pl.BlockSpec(smalls[0].shape, lambda i: (0, 0))
    return pl.pallas_call(
        pair_kernel,
        grid=(4,),
        out_shape=[jax.ShapeDtypeStruct(a.shape, a.dtype) for a in (kept, *smalls)],
        in_specs=[block, block] + [small] * 4,
        out_specs=[block] + [small] * 4,
        compiler_params=ROOM,
        name="pair",
    )(kept, got, *smalls)


def finish_kernel(core_ref, own_ref, other_ref, *outs):
    f32 = jnp.float32
    core = core_ref[0]
    half = own_ref.shape[0] // 4
    own, other = own_ref[...].astype(f32), other_ref[...].astype(f32)
    low, high = jnp.where(core == 0, own, other), jnp.where(core == 0, other, own)
    for k, out in enumerate(outs):
        here = slice(k * half, (k + 1) * half)
        out[:half, :] = low[here, :]
        out[half:, :] = high[here, :]


def finish(core, own, other, shard_rows):
    return pl.pallas_call(
        finish_kernel,
        out_shape=[jax.ShapeDtypeStruct((shard_rows, own.shape[1]), jnp.float32)] * 4,
        in_specs=[SCALARS] + [WHOLE] * 2,
        out_specs=[WHOLE] * 4,
        compiler_params=ROOM,
        name="finish",
    )(core, own, other)


def picks_of(places, e, rows):
    row = lax.broadcasted_iota(jnp.int32, (rows, places.shape[1]), 0) + e * rows
    return ((row == places[0:1]) | (row == places[1:2])).astype(jnp.float32).astype(jnp.bfloat16)


def dispatch_grads_kernel(capacity, place_ref, *refs):
    pieces, (out_ref, places_ref, ids_ref, spots_ref) = refs[:4], refs[4:8]
    gains_ref, bias_ref, router_ref = refs[8:]
    f32, bf16, i32 = jnp.float32, jnp.bfloat16, jnp.int32
    rows = out_ref.shape[0]
    tokens = spots_ref.shape[1]
    features = pieces[0].shape[1]
    experts_all = 2 * rows // (4 * capacity)
    expert = lax.broadcasted_iota(i32, (experts_all, tokens), 0)
    down = lax.broadcasted_iota(i32, (tokens, tokens), 0)
    across = lax.broadcasted_iota(i32, (tokens, tokens), 1)
    earlier = (down < across).astype(f32).astype(bf16)
    sums = []
    for r in range(4):
        both = pieces[r][tokens : tokens + 16, :tokens].astype(f32)
        ids = [both[5 + k : 6 + k].astype(i32) for k in range(2)]
        match = [expert == i for i in ids]
        named = (match[0] | match[1]).astype(f32).astype(bf16)
        counts = jnp.dot(named, earlier, preferred_element_type=f32)
        here = slice(r * tokens, (r + 1) * tokens)
        for k in range(2):
            slot = jnp.sum(jnp.where(match[k], counts, 0.0), axis=0, keepdims=True).astype(i32)
            owner, local = ids[k] >> 1, ids[k] & 1
            places_ref[k : k + 1, here] = (
                local * rows + owner * (4 * capacity) + r * capacity + slot
            )
            ids_ref[k : k + 1, here] = ids[k]
            if r == 0:
                spots_ref[k : k + 1, :] = owner * 16 + local * capacity + slot
        sums.append(to_column(both[5:6] + both[6:7]))
    sums = jnp.concatenate(sums, axis=0)
    lanes = lax.broadcasted_iota(i32, (4 * tokens, 128), 1)
    line = jnp.concatenate([p[:tokens, :] for p in pieces], axis=0)
    places = places_ref[...]
    extra = jnp.zeros((rows, 128), f32)
    for e in range(2):
        pick = picks_of(places, e, rows)
        out_ref[:, e * features : (e + 1) * features] = jnp.dot(
            pick, line, preferred_element_type=f32
        ).astype(bf16)
        column = jnp.where(lanes == e, sums, 0.0).astype(bf16)
        extra = extra + jnp.dot(pick, column, preferred_element_type=f32)
    out_ref[:, 2 * features :] = extra.astype(bf16)
    smalls = [p[tokens:, :].astype(f32) for p in pieces]
    width = features // 4
    heads = bias_ref.shape[0] // 4
    for a in range(4):
        at = (place_ref[0] - a) & 3
        small = jnp.zeros_like(smalls[0])
        for k in range(4):
            small = jnp.where(at == k, smalls[k], small)
        here = slice(a * width, (a + 1) * width)
        gains_ref[:, here] = small[0:2, :width]
        bias_ref[a * heads : (a + 1) * heads, :] = small[2 : 2 + heads, : bias_ref.shape[1]]
        for b in range(router_ref.shape[0] // 16):
            router_ref[16 * b : 16 * b + 16, here] = small[16:32, width * b : width * (b + 1)]


def dispatch_grads(where, pieces, rows, capacity, tokens, experts_all, bias_shape):
    features = pieces[0].shape[1]
    shape = jax.ShapeDtypeStruct
    return pl.pallas_call(
        functools.partial(dispatch_grads_kernel, capacity),
        out_shape=[
            shape((rows, 2 * features + 128), jnp.bfloat16),
            shape((2, 4 * tokens), jnp.int32),
            shape((2, 4 * tokens), jnp.int32),
            shape((2, tokens), jnp.int32),
            shape((2, features), jnp.float32),
            shape(bias_shape, jnp.float32),
            shape((experts_all, features), jnp.float32),
        ],
        in_specs=[SCALARS] + [WHOLE] * 4,
        out_specs=[WHOLE] * 7,
        compiler_params=ROOM,
        name="dispatch_grads",
    )(where, *pieces)


def dispatch_kernel(places_ref, *refs):
    pieces, out_ref = refs[:4], refs[5]
    rows = out_ref.shape[0]
    features = pieces[0].shape[1]
    line = jnp.concatenate([p[...] for p in pieces], axis=0)
    for e in range(2):
        out_ref[:, e * features : (e + 1) * features] = jnp.dot(
            picks_of(places_ref[...], e, rows), line, preferred_element_type=jnp.float32
        ).astype(jnp.bfloat16)


def dispatch(places, pieces, rows, after):
    return pl.pallas_call(
        dispatch_kernel,
        out_shape=jax.ShapeDtypeStruct((rows, 2 * pieces[0].shape[1]), jnp.bfloat16),
        in_specs=[WHOLE] * 5 + [ANYWHERE],
        out_specs=WHOLE,
        compiler_params=ROOM,
        name="dispatch",
    )(places, *pieces, after)


def chosen_logit(logits, ids):
    lanes = lax.broadcasted_iota(jnp.int32, logits.shape, 1)
    return jnp.sum(jnp.where(lanes == ids, logits, 0.0), axis=1, keepdims=True)


def gate_pair(first, second):
    top = jnp.maximum(first, second)
    one, two = jnp.exp(first - top), jnp.exp(second - top)
    total = one + two
    return one / total, two / total


def expert_kernel(x_ref, in_ref, out_ref, ret_ref, act_ref, rise_ref):
    f32, bf16 = jnp.float32, jnp.bfloat16
    slope = math.sqrt(2.0 / math.pi)
    pre = jnp.dot(x_ref[...], in_ref[0], preferred_element_type=f32)
    tanh = jnp.tanh(slope * (pre + 0.044715 * (pre * pre * pre)))
    active = (0.5 * pre * (1.0 + tanh)).astype(bf16)
    act_ref[0] = active
    ret_ref[...] = jnp.dot(active, out_ref[0], preferred_element_type=f32).astype(bf16)
    rise_ref[0] = 0.5 * (1.0 + tanh) + 0.5 * pre * (1.0 - tanh * tanh) * (
        slope * (1.0 + 3.0 * 0.044715 * (pre * pre))
    )


STEP = 256


def lanes_of(n):
    return pl.BlockSpec((STEP, n), lambda e, i: (i, e))


def rows_of(n):
    return pl.BlockSpec((1, STEP, n), lambda e, i: (e, i, 0))


def one_of(a, b):
    return pl.BlockSpec((1, a, b), lambda e, i: (e, 0, 0))


def experts(arrived, w_in, w_out):
    rows = arrived.shape[0]
    features, hidden = w_in.shape[1:]
    return pl.pallas_call(
        expert_kernel,
        grid=(2, rows // STEP),
        out_shape=[
            jax.ShapeDtypeStruct((rows, 2 * features), jnp.bfloat16),
            jax.ShapeDtypeStruct((2, rows, hidden), jnp.bfloat16),
            jax.ShapeDtypeStruct((2, rows, hidden), jnp.float32),
        ],
        in_specs=[lanes_of(features), one_of(features, hidden), one_of(hidden, features)],
        out_specs=[lanes_of(features), rows_of(hidden), rows_of(hidden)],
        compiler_params=ROOM,
        name="experts",
    )(arrived, w_in, w_out)


def expert_back_kernel(
    capacity, own_ref, x_ref, g_ref, ids_ref, in_ref, out_ref, router_ref, rise_ref, *refs
):
    pre_ref, arr_ref, outs, held = refs[0], refs[1], refs[2:6], refs[6]
    f32, bf16, i32 = jnp.float32, jnp.bfloat16, jnp.int32
    e, i = pl.program_id(0), pl.program_id(1)
    own = own_ref[0] + e
    rows = held.shape[0]
    ids = ids_ref[...].astype(f32)
    lanes = lax.broadcasted_iota(i32, ids.shape, 1)
    other = jnp.sum(jnp.where(lanes == e, ids, 0.0), axis=1, keepdims=True).astype(i32) - own
    logits = lax.dot_general(x_ref[...], router_ref[...], LAST, preferred_element_type=f32)
    gate, _ = gate_pair(chosen_logit(logits, own), chosen_logit(logits, other))
    grown = (gate * g_ref[...].astype(f32)).astype(bf16)
    arr_ref[0] = grown
    back = lax.dot_general(grown, out_ref[0], LAST, preferred_element_type=f32)
    grad = (back * rise_ref[0]).astype(bf16)
    pre_ref[0] = grad
    at = pl.ds(pl.multiple_of(i * STEP, STEP), STEP)
    held[at, :] = lax.dot_general(grad, in_ref[0], LAST, preferred_element_type=f32).astype(bf16)

    @pl.when(i == rows // STEP - 1)
    def _():
        part = rows // 4
        here = lax.broadcasted_iota(i32, (part, rows), 0)
        there = lax.broadcasted_iota(i32, (part, rows), 1)
        block = (here * (65536 // capacity + 1)) >> 16
        for r, out in enumerate(outs):
            source = here + block * (3 * capacity) + r * capacity
            pick = (there == source).astype(f32).astype(bf16)
            out[...] = jnp.dot(pick, held[...], preferred_element_type=f32).astype(bf16)


def experts_back(own, arrived, grad_wide, w_in, w_out, router_w, rise, capacity):
    rows = arrived.shape[0]
    features, hidden = w_in.shape[1:]
    bf16 = jnp.bfloat16
    shape = jax.ShapeDtypeStruct
    part = rows // 4
    return pl.pallas_call(
        functools.partial(expert_back_kernel, capacity),
        grid=(2, rows // STEP),
        out_shape=[shape((2, rows, hidden), bf16), shape((2, rows, features), bf16)]
        + [shape((2 * part, features), bf16)] * 4,
        in_specs=[
            SCALARS,
            lanes_of(features),
            lanes_of(features),
            pl.BlockSpec((STEP, 128), lambda e, i: (i, 2 * features // 128)),
            one_of(features, hidden),
            one_of(hidden, features),
            pl.BlockSpec(router_w.shape, lambda e, i: (0, 0)),
            rows_of(hidden),
        ],
        out_specs=[rows_of(hidden), rows_of(features)]
        + [pl.BlockSpec((part, features), lambda e, i: (e, 0))] * 4,
        scratch_shapes=[pltpu.VMEM((rows, features), bf16)],
        compiler_params=ROOM,
        name="experts_back",
    )(own[None], arrived, grad_wide, grad_wide, w_in, w_out, router_w, rise)


def weight_grads_kernel(x_ref, pre_ref, act_ref, arr_ref, in_ref, out_ref):
    in_ref[0] = lax.dot_general(x_ref[...], pre_ref[0], FIRST, preferred_element_type=jnp.float32)
    out_ref[0] = lax.dot_general(act_ref[0], arr_ref[0], FIRST, preferred_element_type=jnp.float32)


def weight_grads(arrived, grad_pre, active, grad_arrived):
    rows = arrived.shape[0]
    hidden, features = grad_pre.shape[2], grad_arrived.shape[2]
    step = 256
    cuts = features // step
    whole = lambda n: pl.BlockSpec((1, rows, n), lambda e, j: (e, 0, 0))
    out = lambda n: pl.BlockSpec((1, step, n), lambda e, j: (e, j, 0))
    return pl.pallas_call(
        weight_grads_kernel,
        grid=(2, cuts),
        out_shape=[
            jax.ShapeDtypeStruct((2, features, hidden), jnp.float32),
            jax.ShapeDtypeStruct((2, hidden, features), jnp.float32),
        ],
        in_specs=[
            pl.BlockSpec((rows, step), lambda e, j: (0, e * cuts + j)),
            whole(hidden),
            pl.BlockSpec((1, rows, step), lambda e, j: (e, 0, j)),
            whole(features),
        ],
        out_specs=[out(hidden), out(features)],
        compiler_params=ROOM,
        cost_estimate=pl.CostEstimate(
            flops=8 * rows * features * hidden, bytes_accessed=20_000_000, transcendentals=0
        ),
        name="weight_grads",
    )(arrived, grad_pre, active, grad_arrived)


def sum_rows_kernel(capacity, *refs):
    pieces, out_ref = refs[:4], refs[-1]
    f32, bf16, i32 = jnp.float32, jnp.bfloat16, jnp.int32
    total = pieces[0][...].astype(f32)
    for piece in pieces[1:]:
        total = total + piece[...].astype(f32)
    rows = out_ref.shape[0]
    part = total.shape[0] // 2
    here = lax.broadcasted_iota(i32, (rows, 2 * part), 0)
    there = lax.broadcasted_iota(i32, (rows, 2 * part), 1)
    owner, q = here >> 4, here & 15
    second = q >= capacity
    source = owner * capacity + jnp.where(second, part + q - capacity, q)
    pick = ((there == source) & (q < 2 * capacity)).astype(f32).astype(bf16)
    out_ref[...] = jnp.dot(pick, total.astype(bf16), preferred_element_type=f32).astype(bf16)


def sum_rows(pieces, capacity, after):
    rows, features = pieces[0].shape
    return pl.pallas_call(
        functools.partial(sum_rows_kernel, capacity),
        out_shape=jax.ShapeDtypeStruct((rows // (2 * capacity) * 16, features), jnp.bfloat16),
        in_specs=[WHOLE] * 4 + [ANYWHERE] * len(after),
        out_specs=WHOLE,
        compiler_params=ROOM,
        name="sum_rows",
    )(*pieces, *after)


def combine_kernel(places_ref, ids_ref, router_ref, ret_ref, *refs):
    f32, bf16 = jnp.float32, jnp.bfloat16
    grads, moes, outs = refs[:4], refs[4:8], refs[9:13]
    tokens, features = moes[0].shape
    rows = ret_ref.shape[0]
    row = lax.broadcasted_iota(jnp.int32, (rows, tokens), 0)
    tail_lane = lax.broadcasted_iota(jnp.int32, (tokens, 128), 1)
    for r in range(4):
        here = slice(r * tokens, (r + 1) * tokens)
        logits = lax.dot_general(
            moes[r][...], router_ref[...], LAST, preferred_element_type=f32
        )
        ids = [to_column(ids_ref[k : k + 1, here]) for k in range(2)]
        gates = gate_pair(chosen_logit(logits, ids[0]), chosen_logit(logits, ids[1]))
        total = jnp.zeros((tokens, features), f32)
        tail = jnp.zeros((tokens, 128), f32)
        grad = grads[r][:tokens, :].astype(f32)
        for k in range(2):
            got = jnp.zeros((tokens, features), f32)
            for e in range(2):
                pick = (row + e * rows == places_ref[k : k + 1, here]).astype(f32).astype(bf16)
                got = got + lax.dot_general(
                    pick,
                    ret_ref[:, e * features : (e + 1) * features],
                    FIRST,
                    preferred_element_type=f32,
                )
            total = total + gates[k] * got
            dots = jnp.sum(grad * got, axis=1, keepdims=True)
            high = dots.astype(bf16).astype(f32)
            tail = jnp.where(tail_lane == k, high, tail)
            tail = jnp.where(tail_lane == 2 + k, dots - high, tail)
        outs[r][:, :features] = total.astype(bf16)
        outs[r][:, features:] = tail.astype(bf16)


def combine(places, ids, router_w, returned, grads, moes, after):
    tokens, features = moes[0].shape
    return pl.pallas_call(
        combine_kernel,
        out_shape=[jax.ShapeDtypeStruct((tokens, features + 128), jnp.bfloat16)] * 4,
        in_specs=[WHOLE] * 12 + [ANYWHERE],
        out_specs=[WHOLE] * 4,
        compiler_params=ROOM,
        name="combine",
    )(places, ids, router_w, returned, *grads, *moes, after)


def layer(
    tokens,
    seq_lengths,
    routes,
    gain_attn,
    w_query,
    w_key,
    w_value,
    w_output,
    rel_bias,
    gain_moe,
    w_router,
    w_in,
    w_out,
    cotangent,
):
    row_count, features = tokens.shape
    shard_rows = w_query.shape[0]
    expert_count = w_router.shape[1]
    bucket_count = rel_bias.shape[1]
    head_count = 4 * rel_bias.shape[0]
    capacity = 3 * row_count // expert_count
    f32 = jnp.float32
    bf16 = jnp.bfloat16

    shard = lax.axis_index("x").astype(jnp.int32)
    core = lax.axis_index("c").astype(jnp.int32)
    where = jnp.stack([shard, core])
    owners = expert_count // 2
    slot_rows = owners * 4 * capacity

    line = make_line(
        routes.T, jnp.stack([gain_attn, gain_moe]), rel_bias, w_router.T, cotangent
    )
    line_grads = along_x(line)
    sent_qkv = pack(core, (w_query, w_key, w_value), line)
    near_qkv = along_x(sent_qkv)[1:]
    near_out = along_x(pack(core, (w_output,), sent_qkv))[1:]
    def to_owners(outgoing):
        return lax.all_to_all(outgoing, ("y", "z", "c"), 0, 0, tiled=True)

    outgoing_grads, places, ids, spots, gains, bias_table, router_f = dispatch_grads(
        where,
        line_grads,
        slot_rows,
        capacity,
        row_count,
        expert_count,
        (head_count, bucket_count),
    )
    gain_one, gain_two = gains[0:1], gains[1:2]
    bias_table, router_w = bias_table.astype(bf16), router_f.astype(bf16)
    grad_wide = to_owners(outgoing_grads)
    first_expert = 2 * lax.axis_index(("y", "z", "c")).astype(jnp.int32)

    segments = row_segments(seq_lengths[0], row_count)
    distance, onehot = position_tables(row_count, bucket_count)
    allowed = (segments[:, None] == segments[None, :]) & (distance >= 0)
    position_bias = jnp.einsum("ijb,hb->hij", onehot, bias_table, preferred_element_type=f32)
    masked_bias = jnp.where(allowed[None], position_bias, -1000000000.0)
    far_qkv = [swap_core(part) for part in near_qkv]
    far_out = [swap_core(part) for part in near_out]
    query_w, key_w, value_w, hidden_one, queries, key_rows, value_rows, probs, attended = attend(
        where,
        tokens,
        gain_one,
        masked_bias,
        (w_query, w_key, w_value),
        near_qkv,
        far_qkv,
        outgoing_grads,
    )
    output_w, middle, moe_in = to_middle(
        where, tokens, gain_two, attended, w_output, near_out, far_out, outgoing_grads
    )

    line_moe = along_x(moe_in)
    arrived = to_owners(dispatch(places, line_moe, slot_rows, grad_wide))
    ret, active, rise = experts(arrived, w_in, w_out)
    returned = to_owners(ret)
    grad_pre, grad_arrived, *blocks = experts_back(
        first_expert, arrived, grad_wide, w_in, w_out, router_w, rise, capacity
    )
    summed = [blocks[0]] + [shift_x(blocks[r], -r) for r in range(1, 4)]
    grad_w_in, grad_w_out = weight_grads(arrived, grad_pre, active, grad_arrived)
    bundle = combine(places, ids, router_w, returned, line_grads, line_moe, grad_w_in)
    back_rows = to_owners(sum_rows(summed, capacity, (grad_w_out, bundle[0])))
    homes = [bundle[0]] + [shift_x(bundle[r], -r) for r in range(1, 4)]
    result, grad_tokens, kept, given, *smalls = backward(
        where,
        tokens,
        cotangent,
        gain_one,
        gain_two,
        ids,
        router_w,
        middle,
        moe_in,
        attended,
        hidden_one,
        queries,
        key_rows,
        value_rows,
        probs,
        spots,
        back_rows,
        *homes,
        query_w,
        key_w,
        value_w,
        output_w,
    )
    piece = shard_rows // 8
    paired, *smalls = pair(kept, swap_core(given), smalls)
    spread = lax.all_to_all(paired, ("y", "x", "z"), 0, 0, tiled=True)
    mine = jnp.sum(spread.reshape(64, piece, features).astype(f32), axis=0).astype(bf16)
    half = lax.all_to_all(
        jnp.broadcast_to(mine[None], (16, piece, features)).reshape(16 * piece, features),
        ("y", "z"),
        0,
        0,
        tiled=True,
    )
    totals = finish(core[None], half, swap_core(half), shard_rows)

    def total_of(parts):
        whole = parts[0].astype(f32)
        for part in parts[1:]:
            whole = whole + part.astype(f32)
        return whole

    small = total_of([smalls[0]] + [shift(smalls[r], "x", -r) for r in range(1, 4)]).astype(bf16)
    small = total_of([small, swap_core(small)]).astype(bf16)
    for axis in ("y", "z"):
        small = total_of([small] + [shift(small, axis, r) for r in range(1, 4)])
        if axis == "y":
            small = small.astype(bf16)
    router_total = small[:expert_count, :shard_rows].T
    gain_one_total = small[expert_count, :shard_rows]
    gain_two_total = small[expert_count + 1, :shard_rows]
    bias_total = small[66 : 66 + rel_bias.shape[0], :bucket_count]
    return (
        result,
        grad_tokens,
        gain_one_total,
        totals[0],
        totals[1],
        totals[2],
        totals[3],
        bias_total,
        gain_two_total,
        router_total,
        grad_w_in,
        grad_w_out,
    )


def solution(mesh):
    cube = Mesh(mesh.devices.reshape(4, 4, 2, 4), ("y", "z", "c", "x"))
    expert = ("y", "z", "c")
    everyone = ("y", "z", "c", "x")
    placed = (
        P(everyone, None),
        P(everyone, None),
        P(everyone, None),
        P("x"),
        P("x", None),
        P("x", None),
        P("x", None),
        P("x", None),
        P("x", None),
        P("x"),
        P("x", None),
        P(expert, None, "x"),
        P(expert, "x", None),
        P(everyone, None),
    )
    return jax.shard_map(
        layer,
        mesh=cube,
        in_specs=placed,
        out_specs=(
            P(everyone, None),
            P(everyone, None),
            P("x"),
            P("x", None),
            P("x", None),
            P("x", None),
            P("x", None),
            P("x", None),
            P("x"),
            P("x", None),
            P(expert, None, "x"),
            P(expert, "x", None),
        ),
        check_vma=False,
    )
```

```python
import functools
import math

import jax
import jax.numpy as jnp
from jax import lax
from jax.experimental import pallas as pl
from jax.experimental.pallas import tpu as pltpu
from jax.sharding import Mesh, PartitionSpec as P

epsilon = 1e-06
bucket_edges = list(range(1, 17)) + [
    int(math.ceil(16.0 * 8.0 ** ((bucket_level - 16) / 16.0))) for bucket_level in range(17, 32)
]


def row_segments(lengths, row_count):
    sequence_ends = jnp.cumsum(lengths)
    positions = jnp.arange(row_count, dtype=jnp.int32)
    return jnp.sum((positions[:, None] >= sequence_ends[None, :]).astype(jnp.int32), axis=1)


def position_tables(row_count, bucket_count):
    positions = jnp.arange(row_count, dtype=jnp.int32)
    distance = positions[:, None] - positions[None, :]
    edge_values = jnp.array(bucket_edges, dtype=jnp.int32)
    bucket = jnp.sum((distance[:, :, None] >= edge_values).astype(jnp.int32), axis=2)
    onehot = (bucket[:, :, None] == jnp.arange(bucket_count, dtype=jnp.int32)).astype(jnp.bfloat16)
    return (distance, onehot)


def shift(block, axis, step):
    ranks = lax.axis_size(axis)
    return lax.ppermute(block, axis, [(i, (i + step) % ranks) for i in range(ranks)])


def shift_x(block, step):
    return shift(block, "x", step)


def swap_core(block):
    return lax.ppermute(block, "c", [(0, 1), (1, 0)])


def along_x(block):
    return [block, shift_x(block, 1), shift_x(block, 2), shift_x(block, 3)]


def line_kernel(routes_ref, gains_ref, bias_ref, router_ref, cotangent_ref, line_ref, held, sem):
    f32 = jnp.float32
    tokens = cotangent_ref.shape[0]
    copy = pltpu.make_async_copy(cotangent_ref, line_ref.at[pl.ds(0, tokens)], sem)
    copy.start()
    held[...] = jnp.zeros_like(held)
    held[0:2, : gains_ref.shape[1]] = gains_ref[...].astype(f32)
    held[2:5, : bias_ref.shape[1]] = bias_ref[...].astype(f32)
    held[5:7, :tokens] = routes_ref[...].astype(f32)
    width = router_ref.shape[1]
    for b in range(router_ref.shape[0] // 16):
        part = router_ref[16 * b : 16 * b + 16, :].astype(f32)
        held[16:32, width * b : width * (b + 1)] = part
    line_ref[tokens:, :] = held[...].astype(jnp.bfloat16)
    copy.wait()


def pack_kernel(count, core_ref, *refs):
    mats, out_ref, sems = refs[:count], refs[count + 1], refs[count + 2]
    half = mats[0].shape[0] // 2
    start = pl.multiple_of(core_ref[0] * half, half)
    copies = start_copies(
        [
            (m.at[pl.ds(start, half)], out_ref.at[pl.ds(k * half, half)])
            for k, m in enumerate(mats)
        ],
        sems,
    )
    for c in copies:
        c.wait()


def start_copies(pairs, sems):
    copies = [pltpu.make_async_copy(s, d, sems.at[i]) for i, (s, d) in enumerate(pairs)]
    for c in copies:
        c.start()
    return copies


def block_copies(shard, core, mats, near, far, outs):
    rows = mats[0].shape[0]
    half = rows // 2
    pairs = []
    for k, (mat, out) in enumerate(zip(mats, outs)):
        begin = pl.multiple_of(shard * rows, rows)
        pairs.append((mat, out.at[pl.ds(begin, rows)]))
        part = pl.ds(k * half, half)
        for r in range(1, 4):
            begin = lax.rem(shard + (4 - r), 4) * rows
            mine = pl.multiple_of(begin + core * half, half)
            other = pl.multiple_of(begin + (1 - core) * half, half)
            pairs.append((near[r - 1].at[part], out.at[pl.ds(mine, half)]))
            pairs.append((far[r - 1].at[part], out.at[pl.ds(other, half)]))
    return pairs


def norm_scale(x):
    return lax.rsqrt(jnp.mean(x * x, axis=1, keepdims=True) + epsilon)


def head_half(block, side):
    lanes = lax.broadcasted_iota(jnp.int32, block.shape, 1)
    keep = (lanes < 64) if side == 0 else (lanes >= 64)
    return jnp.where(keep, block, jnp.zeros_like(block))


def to_column(row):
    n = row.shape[1]
    down = lax.broadcasted_iota(jnp.int32, (n, n), 0)
    across = lax.broadcasted_iota(jnp.int32, (n, n), 1)
    return jnp.sum(jnp.where(down == across, row, jnp.zeros_like(row)), axis=1, keepdims=True)


def diagonal_sums(scores):
    n = scores.shape[0]
    down = lax.broadcasted_iota(jnp.int32, (n, n), 0)
    step = 1
    while step < n:
        turned = pltpu.roll(scores, n - step, axis=1)
        scores = jnp.where((down & step) != 0, turned, scores)
        step *= 2
    return jnp.sum(scores, axis=0, keepdims=True)


def bucket_marks():
    shape = (128, 128)
    distance = (128 - lax.broadcasted_iota(jnp.int32, shape, 0)) & 127
    bucket = jnp.zeros(shape, jnp.int32)
    for edge in bucket_edges:
        bucket = bucket + (distance >= edge).astype(jnp.int32)
    mark = bucket == lax.broadcasted_iota(jnp.int32, shape, 1)
    return mark.astype(jnp.float32).astype(jnp.bfloat16)


LAST = (((1,), (1,)), ((), ()))
FIRST = (((0,), (0,)), ((), ()))


def attend_kernel(place_ref, tokens_ref, gain_ref, bias_ref, *refs):
    f32, bf16 = jnp.float32, jnp.bfloat16
    mats, near, far = refs[:3], refs[3:6], refs[6:9]
    hidden_ref, q_ref, k_ref, v_ref, probs_ref, attended_ref = refs[9:15]
    held, sems = refs[15:]
    weights = [held.at[n] for n in range(3)]
    copies = start_copies(
        block_copies(place_ref[0], place_ref[1], mats, near, far, weights), sems
    )
    x = tokens_ref[...].astype(f32)
    hidden = (x * norm_scale(x) * gain_ref[...].astype(f32)).astype(bf16)
    hidden_ref[...] = hidden
    for n, (w, out) in enumerate(zip(weights, (q_ref, k_ref, v_ref))):
        for c in copies[7 * n : 7 * n + 7]:
            c.wait()
        out[...] = jnp.dot(hidden, w[...], preferred_element_type=f32).astype(bf16)
    heads = bias_ref.shape[0]
    for pair in range(heads // 2):
        lanes = slice(pair * 128, pair * 128 + 128)
        q, k, v = q_ref[:, lanes], k_ref[:, lanes], v_ref[:, lanes]
        total = jnp.zeros(q.shape, f32)
        for side in range(2):
            h = 2 * pair + side
            scores = lax.dot_general(q, head_half(k, side), LAST, preferred_element_type=f32)
            scores = scores * 0.125 + bias_ref[h]
            top = jnp.max(scores, axis=1, keepdims=True)
            grown = jnp.exp(scores - top)
            probs = grown / jnp.sum(grown, axis=1, keepdims=True)
            probs_ref[h] = probs
            total = total + jnp.dot(
                probs.astype(bf16), head_half(v, side), preferred_element_type=f32
            )
        attended_ref[:, lanes] = total.astype(bf16)


def middle_kernel(place_ref, tokens_ref, gain_ref, attended_ref, *refs):
    f32 = jnp.float32
    mats, near, far = refs[:1], refs[1:4], refs[4:7]
    middle_ref, moe_ref, weight, sems = refs[7:11]
    copies = start_copies(
        block_copies(place_ref[0], place_ref[1], mats, near, far, [weight]), sems
    )
    for c in copies:
        c.wait()
    middle = tokens_ref[...].astype(f32) + jnp.dot(
        attended_ref[...], weight[...], preferred_element_type=f32
    )
    middle_ref[...] = middle
    moe_ref[...] = (middle * norm_scale(middle) * gain_ref[...].astype(f32)).astype(jnp.bfloat16)


def backward_kernel(
    place_ref,
    tokens_ref,
    cotangent_ref,
    gain_one_ref,
    gain_two_ref,
    ids_ref,
    router_ref,
    middle_ref,
    moe_ref,
    attended_ref,
    hidden_ref,
    q_ref,
    k_ref,
    v_ref,
    probs_ref,
    spots_ref,
    rows_ref,
    *refs,
):
    f32, bf16 = jnp.float32, jnp.bfloat16
    homes, mats, near_far = refs[:4], refs[4:8], refs[8:20]
    result_ref, tokens_out, kept_ref, given_ref = refs[20:24]
    held, grads_ref, small_ref, sides_ref, sems, out_sems = refs[24:30]
    weights = [held.at[n] for n in range(4)]
    qkv = block_copies(
        place_ref[0], place_ref[1], mats[:3], near_far[0:3], near_far[3:6], weights[:3]
    )
    out = block_copies(
        place_ref[0], place_ref[1], mats[3:], near_far[6:9], near_far[9:12], weights[3:]
    )
    copies = start_copies(qkv + out, sems)
    leaving = []
    features = tokens_ref.shape[1]
    core = place_ref[1]
    width = features // 4
    small_ref[...] = jnp.zeros_like(small_ref)

    def leave(mat, left, right):
        grad = lax.dot_general(left, right, FIRST, preferred_element_type=f32).astype(bf16)
        grads_ref[mat] = grad
        half = 96
        pairs = []
        for x in range(4):
            into = pl.ds((mat * 4 + x) * half, half)
            for target, side in ((kept_ref, core), (given_ref, 1 - core)):
                begin = pl.multiple_of(x * 2 * half + side * half, half)
                source = grads_ref.at[mat, pl.ds(begin, half)]
                pairs.append((source, target.at[into, pl.ds(0, features)]))
        leaving.extend(start_copies(pairs, out_sems.at[mat]))

    def leave_wide(mats_rows, block):
        for x in range(4):
            for (mat, row), begin, size in zip(mats_rows, (0, 128), (128, 64)):
                at = (mat * 4 + x) * 96 + row
                small_ref[at : at + block.shape[0], :size] = block[
                    :, x * width + begin : x * width + begin + size
                ]

    home = homes[0][...].astype(f32)
    for piece in homes[1:]:
        home = home + piece[...].astype(f32)
    middle = middle_ref[...]
    result_ref[...] = (middle + home[:, :features]).astype(bf16)
    tail = home[:, features:]
    lane = lax.broadcasted_iota(jnp.int32, tail.shape, 1)
    grad_gates = [
        jnp.sum(jnp.where((lane == k) | (lane == 2 + k), tail, 0.0), axis=1, keepdims=True)
        for k in range(2)
    ]
    moe = moe_ref[...]
    logits = lax.dot_general(moe, router_ref[...], LAST, preferred_element_type=f32)
    ids = [to_column(ids_ref[k : k + 1, : tail.shape[0]]) for k in range(2)]
    gates = gate_pair(chosen_logit(logits, ids[0]), chosen_logit(logits, ids[1]))
    mix = gates[0] * grad_gates[0] + gates[1] * grad_gates[1]
    spots = lax.broadcasted_iota(jnp.int32, logits.shape, 1)
    grad_logits = jnp.zeros(logits.shape, f32)
    for k in range(2):
        grad_logits = jnp.where(spots == ids[k], gates[k] * (grad_gates[k] - mix), grad_logits)
    grad_logits = grad_logits.astype(bf16)
    slot = lax.broadcasted_iota(jnp.int32, (rows_ref.shape[0], tail.shape[0]), 0)
    pick = ((slot == spots_ref[0:1]) | (slot == spots_ref[1:2])).astype(f32).astype(bf16)
    grad_moe = lax.dot_general(pick, rows_ref[...], FIRST, preferred_element_type=f32)
    grad_moe = grad_moe + jnp.dot(grad_logits, router_ref[...], preferred_element_type=f32)
    leave_wide(
        ((0, 0), (1, 0)),
        lax.dot_general(grad_logits, moe, FIRST, preferred_element_type=f32),
    )
    scale = norm_scale(middle)
    normed = middle * scale
    leave_wide(((2, 2), (2, 3)), jnp.sum(grad_moe * normed, axis=0, keepdims=True))
    inner = grad_moe * gain_two_ref[...].astype(f32)
    grad_middle = cotangent_ref[...].astype(f32) + scale * (
        inner - normed * jnp.mean(inner * normed, axis=1, keepdims=True)
    )
    branch = grad_middle.astype(bf16)
    leave(3, attended_ref[...], branch)
    for c in copies[21:]:
        c.wait()
    grad_attended = lax.dot_general(branch, held[3], LAST, preferred_element_type=f32).astype(bf16)
    grad_q, grad_k, grad_v, diagonals = [], [], [], []
    for pair in range(probs_ref.shape[0] // 2):
        lanes = slice(pair * 128, pair * 128 + 128)
        q, k, v = q_ref[:, lanes], k_ref[:, lanes], v_ref[:, lanes]
        grad = grad_attended[:, lanes]
        parts = [jnp.zeros(q.shape, f32) for _ in range(3)]
        for side in range(2):
            h = 2 * pair + side
            probs = probs_ref[h]
            grad_half = head_half(grad, side)
            parts[2] = parts[2] + lax.dot_general(
                probs.astype(bf16), grad_half, FIRST, preferred_element_type=f32
            )
            grad_probs = lax.dot_general(grad_half, v, LAST, preferred_element_type=f32)
            grad_scores = (
                probs * (grad_probs - jnp.sum(probs * grad_probs, axis=1, keepdims=True))
            ).astype(bf16)
            diagonals.append(diagonal_sums(grad_scores.astype(f32)))
            parts[0] = parts[0] + jnp.dot(
                grad_scores, head_half(k, side), preferred_element_type=f32
            )
            parts[1] = parts[1] + lax.dot_general(
                grad_scores, head_half(q, side), FIRST, preferred_element_type=f32
            )
        grad_q.append((parts[0] * 0.125).astype(bf16))
        grad_k.append((parts[1] * 0.125).astype(bf16))
        grad_v.append(parts[2].astype(bf16))
    left = jnp.concatenate(diagonals, axis=0)
    grad_bias = jnp.zeros((left.shape[0], 128), f32)
    for _ in range(3):
        part = left.astype(bf16)
        left = left - part.astype(f32)
        grad_bias = grad_bias + jnp.dot(part, bucket_marks(), preferred_element_type=f32)
    per = left.shape[0] // 4
    for a in range(4):
        at = (8 + a) * 96 + 4
        small_ref[at : at + per, :] = grad_bias[a * per : a * per + per, :]
    hidden = hidden_ref[...]
    grad_hidden = jnp.zeros(hidden.shape, f32)
    for n, parts in enumerate((grad_q, grad_k, grad_v)):
        grad = jnp.concatenate(parts, axis=1)
        leave(n, hidden, grad)
        for c in copies[7 * n : 7 * n + 7]:
            c.wait()
        grad_hidden = grad_hidden + lax.dot_general(
            grad, held[n], LAST, preferred_element_type=f32
        )
    x = tokens_ref[...].astype(f32)
    scale = norm_scale(x)
    normed = x * scale
    leave_wide(((2, 0), (2, 1)), jnp.sum(grad_hidden * normed, axis=0, keepdims=True))
    inner = grad_hidden * gain_one_ref[...].astype(f32)
    tokens_out[...] = grad_middle + scale * (
        inner - normed * jnp.mean(inner * normed, axis=1, keepdims=True)
    )
    small = small_ref[...].astype(bf16)
    none = jnp.zeros_like(small)
    sides_ref[0] = jnp.where(core == 0, small, none)
    sides_ref[1] = jnp.where(core == 0, none, small)
    lanes = pl.ds(features, 128)
    pairs = [
        (sides_ref.at[0], kept_ref.at[:, lanes]),
        (sides_ref.at[1], given_ref.at[:, lanes]),
    ]
    leaving.extend(start_copies(pairs, out_sems.at[4]))
    for c in leaving:
        c.wait()


ANYWHERE = pl.BlockSpec(memory_space=pl.ANY)
SCALARS = pl.BlockSpec(memory_space=pltpu.SMEM)
WHOLE = pl.BlockSpec(memory_space=pltpu.VMEM)
ROOM = pltpu.CompilerParams(vmem_limit_bytes=56 * 1024 * 1024)


def make_line(routes, gains, bias, router, cotangent):
    tokens, cols = cotangent.shape
    return pl.pallas_call(
        line_kernel,
        out_shape=jax.ShapeDtypeStruct((tokens + 32, cols), jnp.bfloat16),
        in_specs=[WHOLE] * 4 + [ANYWHERE],
        out_specs=WHOLE,
        scratch_shapes=[pltpu.VMEM((32, cols), jnp.float32), pltpu.SemaphoreType.DMA],
        compiler_params=ROOM,
        name="line",
    )(routes, gains, bias, router, cotangent)


def pack(core, mats, after):
    rows, cols = mats[0].shape
    count = len(mats)
    return pl.pallas_call(
        functools.partial(pack_kernel, count),
        out_shape=jax.ShapeDtypeStruct((count * rows // 2, cols), jnp.bfloat16),
        in_specs=[SCALARS] + [ANYWHERE] * (count + 1),
        out_specs=WHOLE,
        scratch_shapes=[pltpu.SemaphoreType.DMA((count,))],
        compiler_params=ROOM,
        name="pack",
    )(core[None], *mats, after)


def attend(where, tokens, gain, bias, mats, near, far):
    rows, cols = mats[0].shape
    state = jax.ShapeDtypeStruct(tokens.shape, jnp.bfloat16)
    return pl.pallas_call(
        attend_kernel,
        out_shape=[state] * 4 + [jax.ShapeDtypeStruct(bias.shape, jnp.float32), state],
        in_specs=[SCALARS] + [WHOLE] * 3 + [ANYWHERE] * 9,
        out_specs=[WHOLE] * 6,
        scratch_shapes=[
            pltpu.VMEM((3, 4 * rows, cols), jnp.bfloat16),
            pltpu.SemaphoreType.DMA((21,)),
        ],
        compiler_params=ROOM,
        name="attend",
    )(where, tokens, gain, bias, *mats, *near, *far)


def to_middle(where, tokens, gain, attended, mat, near, far):
    rows, cols = mat.shape
    return pl.pallas_call(
        middle_kernel,
        out_shape=[
            jax.ShapeDtypeStruct(tokens.shape, jnp.float32),
            jax.ShapeDtypeStruct(tokens.shape, jnp.bfloat16),
        ],
        in_specs=[SCALARS] + [WHOLE] * 3 + [ANYWHERE] * 7,
        out_specs=[WHOLE] * 2,
        scratch_shapes=[
            pltpu.VMEM((4 * rows, cols), jnp.bfloat16),
            pltpu.SemaphoreType.DMA((7,)),
        ],
        compiler_params=ROOM,
        name="middle",
    )(where, tokens, gain, attended, mat, *near, *far)


def backward(where, *arrays):
    tokens = arrays[0]
    count, features = tokens.shape
    bf16, f32 = jnp.bfloat16, jnp.float32
    shape = jax.ShapeDtypeStruct
    return pl.pallas_call(
        backward_kernel,
        out_shape=[
            shape((count, features), bf16),
            shape((count, features), f32),
            shape((2 * features, features + 128), bf16),
            shape((2 * features, features + 128), bf16),
        ],
        in_specs=[SCALARS] + [WHOLE] * 20 + [ANYWHERE] * 16,
        out_specs=[WHOLE] * 2 + [ANYWHERE] * 2,
        scratch_shapes=[
            pltpu.VMEM((4, features, features), bf16),
            pltpu.VMEM((4, features, features), bf16),
            pltpu.VMEM((2 * features, 128), f32),
            pltpu.VMEM((2, 2 * features, 128), bf16),
            pltpu.SemaphoreType.DMA((28,)),
            pltpu.SemaphoreType.DMA((5, 8)),
        ],
        compiler_params=ROOM,
        name="backward",
    )(where, *arrays)


def finish_kernel(core_ref, own_ref, other_ref, *refs):
    mats, (router_out, gains_out, bias_out) = refs[:4], refs[4:]
    f32 = jnp.float32
    core = core_ref[0]
    half = own_ref.shape[0] // 4
    features = mats[0].shape[1]
    own, other = own_ref[...].astype(f32), other_ref[...].astype(f32)
    low, high = jnp.where(core == 0, own, other), jnp.where(core == 0, other, own)
    for k, out in enumerate(mats):
        here = slice(k * half, (k + 1) * half)
        out[:half, :] = low[here, :features]
        out[half:, :] = high[here, :features]
    small = low[:, features:]
    tall = router_out.shape[0]
    router_out[:, :128] = small[:tall, :]
    router_out[:, 128:] = small[half : half + tall, :64]
    for k in range(2):
        at = 2 * half + 2 * k
        gains_out[k : k + 1, :128] = small[at : at + 1, :]
        gains_out[k : k + 1, 128:] = small[at + 1 : at + 2, :64]
    at = 2 * half + 4
    bias_out[...] = small[at : at + bias_out.shape[0], : bias_out.shape[1]]


def finish(core, own, other, shard_rows, experts_all, bias_shape):
    features = own.shape[1] - 128
    shape = lambda *s: jax.ShapeDtypeStruct(s, jnp.float32)
    return pl.pallas_call(
        finish_kernel,
        out_shape=[shape(shard_rows, features)] * 4
        + [shape(experts_all, shard_rows), shape(2, shard_rows), shape(*bias_shape)],
        in_specs=[SCALARS] + [WHOLE] * 2,
        out_specs=[WHOLE] * 7,
        compiler_params=ROOM,
        name="finish",
    )(core, own, other)


def picks_of(places, e, rows):
    row = lax.broadcasted_iota(jnp.int32, (rows, places.shape[1]), 0) + e * rows
    return ((row == places[0:1]) | (row == places[1:2])).astype(jnp.float32).astype(jnp.bfloat16)


def dispatch_grads_kernel(capacity, place_ref, *refs):
    pieces, (out_ref, places_ref, ids_ref, spots_ref) = refs[:4], refs[6:10]
    gains_ref, bias_ref, router_ref, picks_ref = refs[10:]
    f32, bf16, i32 = jnp.float32, jnp.bfloat16, jnp.int32
    rows = out_ref.shape[0]
    tokens = spots_ref.shape[1]
    features = pieces[0].shape[1]
    experts_all = 2 * rows // (4 * capacity)
    expert = lax.broadcasted_iota(i32, (experts_all, tokens), 0)
    down = lax.broadcasted_iota(i32, (tokens, tokens), 0)
    across = lax.broadcasted_iota(i32, (tokens, tokens), 1)
    earlier = (down < across).astype(f32).astype(bf16)
    sums = []
    for r in range(4):
        both = pieces[r][tokens : tokens + 16, :tokens].astype(f32)
        ids = [both[5 + k : 6 + k].astype(i32) for k in range(2)]
        match = [expert == i for i in ids]
        named = (match[0] | match[1]).astype(f32).astype(bf16)
        counts = jnp.dot(named, earlier, preferred_element_type=f32)
        here = slice(r * tokens, (r + 1) * tokens)
        for k in range(2):
            slot = jnp.sum(jnp.where(match[k], counts, 0.0), axis=0, keepdims=True).astype(i32)
            owner, local = ids[k] >> 1, ids[k] & 1
            places_ref[k : k + 1, here] = (
                local * rows + owner * (4 * capacity) + r * capacity + slot
            )
            ids_ref[k : k + 1, here] = ids[k]
            if r == 0:
                spots_ref[k : k + 1, :] = owner * 16 + local * capacity + slot
        sums.append(to_column(both[5:6] + both[6:7]))
    sums = jnp.concatenate(sums, axis=0)
    lanes = lax.broadcasted_iota(i32, (4 * tokens, 128), 1)
    line = jnp.concatenate([p[:tokens, :] for p in pieces], axis=0)
    places = places_ref[...]
    extra = jnp.zeros((rows, 128), f32)
    for e in range(2):
        pick = picks_of(places, e, rows)
        picks_ref[e] = pick
        out_ref[:, e * features : (e + 1) * features] = jnp.dot(
            pick, line, preferred_element_type=f32
        ).astype(bf16)
        column = jnp.where(lanes == e, sums, 0.0).astype(bf16)
        extra = extra + jnp.dot(pick, column, preferred_element_type=f32)
    out_ref[:, 2 * features :] = extra.astype(bf16)
    smalls = [p[tokens:, :].astype(f32) for p in pieces]
    width = features // 4
    heads = bias_ref.shape[0] // 4
    for a in range(4):
        at = (place_ref[0] - a) & 3
        small = jnp.zeros_like(smalls[0])
        for k in range(4):
            small = jnp.where(at == k, smalls[k], small)
        here = slice(a * width, (a + 1) * width)
        gains_ref[:, here] = small[0:2, :width]
        bias_ref[a * heads : (a + 1) * heads, :] = small[2 : 2 + heads, : bias_ref.shape[1]]
        for b in range(router_ref.shape[0] // 16):
            router_ref[16 * b : 16 * b + 16, here] = small[16:32, width * b : width * (b + 1)]


def dispatch_grads(where, pieces, rows, capacity, tokens, experts_all, bias_shape, after):
    features = pieces[0].shape[1]
    shape = jax.ShapeDtypeStruct
    return pl.pallas_call(
        functools.partial(dispatch_grads_kernel, capacity),
        out_shape=[
            shape((rows, 2 * features + 128), jnp.bfloat16),
            shape((2, 4 * tokens), jnp.int32),
            shape((2, 4 * tokens), jnp.int32),
            shape((2, tokens), jnp.int32),
            shape((2, features), jnp.float32),
            shape(bias_shape, jnp.float32),
            shape((experts_all, features), jnp.float32),
            shape((2, rows, 4 * tokens), jnp.bfloat16),
        ],
        in_specs=[SCALARS] + [WHOLE] * 4 + [ANYWHERE] * 2,
        out_specs=[WHOLE] * 8,
        compiler_params=ROOM,
        name="dispatch_grads",
    )(where, *pieces, *after)


def dispatch_kernel(picks_ref, *refs):
    pieces, out_ref = refs[:4], refs[5]
    features = pieces[0].shape[1]
    line = jnp.concatenate([p[...] for p in pieces], axis=0)
    for e in range(2):
        out_ref[:, e * features : (e + 1) * features] = jnp.dot(
            picks_ref[e], line, preferred_element_type=jnp.float32
        ).astype(jnp.bfloat16)


def dispatch(picks, pieces, after):
    return pl.pallas_call(
        dispatch_kernel,
        out_shape=jax.ShapeDtypeStruct((picks.shape[1], 2 * pieces[0].shape[1]), jnp.bfloat16),
        in_specs=[WHOLE] * 5 + [ANYWHERE],
        out_specs=WHOLE,
        compiler_params=ROOM,
        name="dispatch",
    )(picks, *pieces, after)


def chosen_logit(logits, ids):
    lanes = lax.broadcasted_iota(jnp.int32, logits.shape, 1)
    return jnp.sum(jnp.where(lanes == ids, logits, 0.0), axis=1, keepdims=True)


def gate_pair(first, second):
    top = jnp.maximum(first, second)
    one, two = jnp.exp(first - top), jnp.exp(second - top)
    total = one + two
    return one / total, two / total


def expert_kernel(x_ref, in_ref, out_ref, ret_ref, act_ref, rise_ref):
    f32, bf16 = jnp.float32, jnp.bfloat16
    slope = math.sqrt(2.0 / math.pi)
    pre = jnp.dot(x_ref[...], in_ref[0], preferred_element_type=f32)
    tanh = jnp.tanh(slope * (pre + 0.044715 * (pre * pre * pre)))
    active = (0.5 * pre * (1.0 + tanh)).astype(bf16)
    act_ref[0] = active
    ret_ref[...] = jnp.dot(active, out_ref[0], preferred_element_type=f32).astype(bf16)
    rise_ref[0] = 0.5 * (1.0 + tanh) + 0.5 * pre * (1.0 - tanh * tanh) * (
        slope * (1.0 + 3.0 * 0.044715 * (pre * pre))
    )


STEP = 256


def lanes_of(n):
    return pl.BlockSpec((STEP, n), lambda e, i: (i, e))


def rows_of(n):
    return pl.BlockSpec((1, STEP, n), lambda e, i: (e, i, 0))


def one_of(a, b):
    return pl.BlockSpec((1, a, b), lambda e, i: (e, 0, 0))


def experts(arrived, w_in, w_out):
    rows = arrived.shape[0]
    features, hidden = w_in.shape[1:]
    return pl.pallas_call(
        expert_kernel,
        grid=(2, rows // STEP),
        out_shape=[
            jax.ShapeDtypeStruct((rows, 2 * features), jnp.bfloat16),
            jax.ShapeDtypeStruct((2, rows, hidden), jnp.bfloat16),
            jax.ShapeDtypeStruct((2, rows, hidden), jnp.float32),
        ],
        in_specs=[lanes_of(features), one_of(features, hidden), one_of(hidden, features)],
        out_specs=[lanes_of(features), rows_of(hidden), rows_of(hidden)],
        compiler_params=ROOM,
        name="experts",
    )(arrived, w_in, w_out)


def early_kernel(g_ref, out_ref, back_ref):
    back_ref[0] = lax.dot_general(
        g_ref[...], out_ref[0], LAST, preferred_element_type=jnp.float32
    )


def early_product(grad_wide, w_out, after):
    rows = grad_wide.shape[0]
    hidden, features = w_out.shape[1:]
    return pl.pallas_call(
        lambda g, w, _, out: early_kernel(g, w, out),
        grid=(2, rows // STEP),
        out_shape=jax.ShapeDtypeStruct((2, rows, hidden), jnp.float32),
        in_specs=[lanes_of(features), one_of(hidden, features), ANYWHERE],
        out_specs=rows_of(hidden),
        compiler_params=ROOM,
        name="early_product",
    )(grad_wide, w_out, after)


def expert_back_kernel(
    capacity, own_ref, x_ref, g_ref, ids_ref, in_ref, router_ref, rise_ref, back_ref, *refs
):
    pre_ref, arr_ref, outs, held = refs[0], refs[1], refs[2:6], refs[6]
    f32, bf16, i32 = jnp.float32, jnp.bfloat16, jnp.int32
    e = pl.program_id(0)
    own = own_ref[0] + e
    rows = x_ref.shape[0]

    def chunk(i, carry):
        at = pl.ds(pl.multiple_of(i * STEP, STEP), STEP)
        ids = ids_ref[at, :].astype(f32)
        lanes = lax.broadcasted_iota(i32, ids.shape, 1)
        other = jnp.sum(jnp.where(lanes == e, ids, 0.0), axis=1, keepdims=True).astype(i32) - own
        logits = lax.dot_general(x_ref[at, :], router_ref[...], LAST, preferred_element_type=f32)
        gate, _ = gate_pair(chosen_logit(logits, own), chosen_logit(logits, other))
        arr_ref[0, at, :] = (gate * g_ref[at, :].astype(f32)).astype(bf16)
        grad = (gate * back_ref[0, at, :] * rise_ref[0, at, :]).astype(bf16)
        pre_ref[0, at, :] = grad
        held[at, :] = lax.dot_general(grad, in_ref[0], LAST, preferred_element_type=f32).astype(
            bf16
        )
        return carry

    lax.fori_loop(0, rows // STEP, chunk, 0)
    part = rows // 4
    here = lax.broadcasted_iota(i32, (part, rows), 0)
    there = lax.broadcasted_iota(i32, (part, rows), 1)
    block = (here * (65536 // capacity + 1)) >> 16
    for r, out in enumerate(outs):
        source = here + block * (3 * capacity) + r * capacity
        pick = (there == source).astype(f32).astype(bf16)
        out[...] = jnp.dot(pick, held[...], preferred_element_type=f32).astype(bf16)


def experts_back(own, arrived, grad_wide, w_in, router_w, rise, back, capacity):
    rows = arrived.shape[0]
    features, hidden = w_in.shape[1:]
    bf16 = jnp.bfloat16
    shape = jax.ShapeDtypeStruct
    part = rows // 4
    lanes = lambda n: pl.BlockSpec((rows, n), lambda e: (0, e))
    one = lambda a, b: pl.BlockSpec((1, a, b), lambda e: (e, 0, 0))
    return pl.pallas_call(
        functools.partial(expert_back_kernel, capacity),
        grid=(2,),
        out_shape=[shape((2, rows, hidden), bf16), shape((2, rows, features), bf16)]
        + [shape((2 * part, features), bf16)] * 4,
        in_specs=[
            SCALARS,
            lanes(features),
            lanes(features),
            pl.BlockSpec((rows, 128), lambda e: (0, 2 * features // 128)),
            one(features, hidden),
            pl.BlockSpec(router_w.shape, lambda e: (0, 0)),
            one(rows, hidden),
            one(rows, hidden),
        ],
        out_specs=[one(rows, hidden), one(rows, features)]
        + [pl.BlockSpec((part, features), lambda e: (e, 0))] * 4,
        scratch_shapes=[pltpu.VMEM((rows, features), bf16)],
        compiler_params=ROOM,
        name="experts_back",
    )(own[None], arrived, grad_wide, grad_wide, w_in, router_w, rise, back)


def weight_grads_kernel(x_ref, pre_ref, act_ref, arr_ref, in_ref, out_ref):
    in_ref[0] = lax.dot_general(x_ref[...], pre_ref[0], FIRST, preferred_element_type=jnp.float32)
    out_ref[0] = lax.dot_general(act_ref[0], arr_ref[0], FIRST, preferred_element_type=jnp.float32)


def weight_grads(arrived, grad_pre, active, grad_arrived):
    rows = arrived.shape[0]
    hidden, features = grad_pre.shape[2], grad_arrived.shape[2]
    step = 256
    cuts = features // step
    whole = lambda n: pl.BlockSpec((1, rows, n), lambda e, j: (e, 0, 0))
    out = lambda n: pl.BlockSpec((1, step, n), lambda e, j: (e, j, 0))
    return pl.pallas_call(
        weight_grads_kernel,
        grid=(2, cuts),
        out_shape=[
            jax.ShapeDtypeStruct((2, features, hidden), jnp.float32),
            jax.ShapeDtypeStruct((2, hidden, features), jnp.float32),
        ],
        in_specs=[
            pl.BlockSpec((rows, step), lambda e, j: (0, e * cuts + j)),
            whole(hidden),
            pl.BlockSpec((1, rows, step), lambda e, j: (e, 0, j)),
            whole(features),
        ],
        out_specs=[out(hidden), out(features)],
        compiler_params=ROOM,
        cost_estimate=pl.CostEstimate(
            flops=8 * rows * features * hidden, bytes_accessed=20_000_000, transcendentals=0
        ),
        name="weight_grads",
    )(arrived, grad_pre, active, grad_arrived)


def sum_rows_kernel(capacity, *refs):
    pieces, out_ref = refs[:4], refs[-1]
    f32, bf16, i32 = jnp.float32, jnp.bfloat16, jnp.int32
    total = pieces[0][...].astype(f32)
    for piece in pieces[1:]:
        total = total + piece[...].astype(f32)
    rows = out_ref.shape[0]
    part = total.shape[0] // 2
    here = lax.broadcasted_iota(i32, (rows, 2 * part), 0)
    there = lax.broadcasted_iota(i32, (rows, 2 * part), 1)
    owner, q = here >> 4, here & 15
    second = q >= capacity
    source = owner * capacity + jnp.where(second, part + q - capacity, q)
    pick = ((there == source) & (q < 2 * capacity)).astype(f32).astype(bf16)
    out_ref[...] = jnp.dot(pick, total.astype(bf16), preferred_element_type=f32).astype(bf16)


def sum_rows(pieces, capacity, after):
    rows, features = pieces[0].shape
    return pl.pallas_call(
        functools.partial(sum_rows_kernel, capacity),
        out_shape=jax.ShapeDtypeStruct((rows // (2 * capacity) * 16, features), jnp.bfloat16),
        in_specs=[WHOLE] * 4 + [ANYWHERE] * len(after),
        out_specs=WHOLE,
        compiler_params=ROOM,
        name="sum_rows",
    )(*pieces, *after)


def combine_kernel(places_ref, ids_ref, router_ref, ret_ref, *refs):
    f32, bf16 = jnp.float32, jnp.bfloat16
    grads, moes, outs = refs[:4], refs[4:8], refs[9:13]
    tokens, features = moes[0].shape
    rows = ret_ref.shape[0]
    row = lax.broadcasted_iota(jnp.int32, (rows, tokens), 0)
    tail_lane = lax.broadcasted_iota(jnp.int32, (tokens, 128), 1)
    for r in range(4):
        here = slice(r * tokens, (r + 1) * tokens)
        logits = lax.dot_general(
            moes[r][...], router_ref[...], LAST, preferred_element_type=f32
        )
        ids = [to_column(ids_ref[k : k + 1, here]) for k in range(2)]
        gates = gate_pair(chosen_logit(logits, ids[0]), chosen_logit(logits, ids[1]))
        total = jnp.zeros((tokens, features), f32)
        tail = jnp.zeros((tokens, 128), f32)
        grad = grads[r][:tokens, :].astype(f32)
        for k in range(2):
            got = jnp.zeros((tokens, features), f32)
            for e in range(2):
                pick = (row + e * rows == places_ref[k : k + 1, here]).astype(f32).astype(bf16)
                got = got + lax.dot_general(
                    pick,
                    ret_ref[:, e * features : (e + 1) * features],
                    FIRST,
                    preferred_element_type=f32,
                )
            total = total + gates[k] * got
            dots = jnp.sum(grad * got, axis=1, keepdims=True)
            high = dots.astype(bf16).astype(f32)
            tail = jnp.where(tail_lane == k, high, tail)
            tail = jnp.where(tail_lane == 2 + k, dots - high, tail)
        outs[r][:, :features] = total.astype(bf16)
        outs[r][:, features:] = tail.astype(bf16)


def combine(places, ids, router_w, returned, grads, moes, after):
    tokens, features = moes[0].shape
    return pl.pallas_call(
        combine_kernel,
        out_shape=[jax.ShapeDtypeStruct((tokens, features + 128), jnp.bfloat16)] * 4,
        in_specs=[WHOLE] * 12 + [ANYWHERE],
        out_specs=[WHOLE] * 4,
        compiler_params=ROOM,
        name="combine",
    )(places, ids, router_w, returned, *grads, *moes, after)


def layer(
    tokens,
    seq_lengths,
    routes,
    gain_attn,
    w_query,
    w_key,
    w_value,
    w_output,
    rel_bias,
    gain_moe,
    w_router,
    w_in,
    w_out,
    cotangent,
):
    row_count, features = tokens.shape
    shard_rows = w_query.shape[0]
    expert_count = w_router.shape[1]
    bucket_count = rel_bias.shape[1]
    head_count = 4 * rel_bias.shape[0]
    capacity = 3 * row_count // expert_count
    f32 = jnp.float32
    bf16 = jnp.bfloat16

    shard = lax.axis_index("x").astype(jnp.int32)
    core = lax.axis_index("c").astype(jnp.int32)
    where = jnp.stack([shard, core])
    owners = expert_count // 2
    slot_rows = owners * 4 * capacity

    line = make_line(
        routes.T, jnp.stack([gain_attn, gain_moe]), rel_bias, w_router.T, cotangent
    )
    line_grads = along_x(line)
    sent_qkv = pack(core, (w_query, w_key, w_value), line)
    near_qkv = along_x(sent_qkv)[1:]
    sent_out = pack(core, (w_output,), sent_qkv)
    near_out = along_x(sent_out)[1:]
    def to_owners(outgoing):
        return lax.all_to_all(outgoing, ("y", "z", "c"), 0, 0, tiled=True)

    outgoing_grads, places, ids, spots, gains, bias_table, router_f, picks = dispatch_grads(
        where,
        line_grads,
        slot_rows,
        capacity,
        row_count,
        expert_count,
        (head_count, bucket_count),
        (sent_qkv, sent_out),
    )
    gain_one, gain_two = gains[0:1], gains[1:2]
    bias_table, router_w = bias_table.astype(bf16), router_f.astype(bf16)
    grad_wide = to_owners(outgoing_grads)
    first_expert = 2 * lax.axis_index(("y", "z", "c")).astype(jnp.int32)

    segments = row_segments(seq_lengths[0], row_count)
    distance, onehot = position_tables(row_count, bucket_count)
    allowed = (segments[:, None] == segments[None, :]) & (distance >= 0)
    position_bias = jnp.einsum("ijb,hb->hij", onehot, bias_table, preferred_element_type=f32)
    masked_bias = jnp.where(allowed[None], position_bias, -1000000000.0)
    far_qkv = [swap_core(part) for part in near_qkv]
    far_out = [swap_core(part) for part in near_out]
    hidden_one, queries, key_rows, value_rows, probs, attended = attend(
        where,
        tokens,
        gain_one,
        masked_bias,
        (w_query, w_key, w_value),
        near_qkv,
        far_qkv,
    )
    middle, moe_in = to_middle(
        where, tokens, gain_two, attended, w_output, near_out, far_out
    )

    line_moe = along_x(moe_in)
    outgoing = dispatch(picks, line_moe, grad_wide)
    arrived = to_owners(outgoing)
    early = early_product(grad_wide, w_out, outgoing)
    ret, active, rise = experts(arrived, w_in, w_out)
    returned = to_owners(ret)
    grad_pre, grad_arrived, *blocks = experts_back(
        first_expert, arrived, grad_wide, w_in, router_w, rise, early, capacity
    )
    summed = [blocks[0]] + [shift_x(blocks[r], -r) for r in range(1, 4)]
    grad_w_in, grad_w_out = weight_grads(arrived, grad_pre, active, grad_arrived)
    bundle = combine(places, ids, router_w, returned, line_grads, line_moe, grad_w_in)
    back_rows = to_owners(sum_rows(summed, capacity, (grad_w_out, bundle[0])))
    homes = [bundle[0]] + [shift_x(bundle[r], -r) for r in range(1, 4)]
    result, grad_tokens, kept, given = backward(
        where,
        tokens,
        cotangent,
        gain_one,
        gain_two,
        ids,
        router_w,
        middle,
        moe_in,
        attended,
        hidden_one,
        queries,
        key_rows,
        value_rows,
        probs,
        spots,
        back_rows,
        *homes,
        w_query,
        w_key,
        w_value,
        w_output,
        *near_qkv,
        *far_qkv,
        *near_out,
        *far_out,
    )
    piece = shard_rows // 8
    wide = features + 128
    paired = (kept.astype(f32) + swap_core(given).astype(f32)).astype(bf16)
    spread = lax.all_to_all(paired, ("y", "x", "z"), 0, 0, tiled=True)
    mine = jnp.sum(spread.reshape(64, piece, wide).astype(f32), axis=0).astype(bf16)
    half = lax.all_to_all(
        jnp.broadcast_to(mine[None], (16, piece, wide)).reshape(16 * piece, wide),
        ("y", "z"),
        0,
        0,
        tiled=True,
    )
    *totals, router_total, gain_totals, bias_total = finish(
        core[None], half, swap_core(half), shard_rows, expert_count, rel_bias.shape
    )
    router_total = router_total.T
    gain_one_total, gain_two_total = gain_totals[0], gain_totals[1]
    return (
        result,
        grad_tokens,
        gain_one_total,
        totals[0],
        totals[1],
        totals[2],
        totals[3],
        bias_total,
        gain_two_total,
        router_total,
        grad_w_in,
        grad_w_out,
    )


def solution(mesh):
    cube = Mesh(mesh.devices.reshape(4, 4, 2, 4), ("y", "z", "c", "x"))
    expert = ("y", "z", "c")
    everyone = ("y", "z", "c", "x")
    placed = (
        P(everyone, None),
        P(everyone, None),
        P(everyone, None),
        P("x"),
        P("x", None),
        P("x", None),
        P("x", None),
        P("x", None),
        P("x", None),
        P("x"),
        P("x", None),
        P(expert, None, "x"),
        P(expert, "x", None),
        P(everyone, None),
    )
    return jax.shard_map(
        layer,
        mesh=cube,
        in_specs=placed,
        out_specs=(
            P(everyone, None),
            P(everyone, None),
            P("x"),
            P("x", None),
            P("x", None),
            P("x", None),
            P("x", None),
            P("x", None),
            P("x"),
            P("x", None),
            P(expert, None, "x"),
            P(expert, "x", None),
        ),
        check_vma=False,
    )
```

```python
import functools
import math

import jax
import jax.numpy as jnp
from jax import lax
from jax.experimental import pallas as pl
from jax.experimental.pallas import tpu as pltpu
from jax.sharding import Mesh, PartitionSpec as P

epsilon = 1e-06
bucket_edges = list(range(1, 17)) + [
    int(math.ceil(16.0 * 8.0 ** ((bucket_level - 16) / 16.0))) for bucket_level in range(17, 32)
]


def row_segments(lengths, row_count):
    sequence_ends = jnp.cumsum(lengths)
    positions = jnp.arange(row_count, dtype=jnp.int32)
    return jnp.sum((positions[:, None] >= sequence_ends[None, :]).astype(jnp.int32), axis=1)


def position_tables(row_count, bucket_count):
    positions = jnp.arange(row_count, dtype=jnp.int32)
    distance = positions[:, None] - positions[None, :]
    edge_values = jnp.array(bucket_edges, dtype=jnp.int32)
    bucket = jnp.sum((distance[:, :, None] >= edge_values).astype(jnp.int32), axis=2)
    onehot = (bucket[:, :, None] == jnp.arange(bucket_count, dtype=jnp.int32)).astype(jnp.bfloat16)
    return (distance, onehot)


def shift(block, axis, step):
    ranks = lax.axis_size(axis)
    return lax.ppermute(block, axis, [(i, (i + step) % ranks) for i in range(ranks)])


def shift_x(block, step):
    return shift(block, "x", step)


def swap_core(block):
    return lax.ppermute(block, "c", [(0, 1), (1, 0)])


def along_x(block):
    return [block, shift_x(block, 1), shift_x(block, 2), shift_x(block, 3)]


def line_kernel(routes_ref, gains_ref, bias_ref, router_ref, cotangent_ref, line_ref, held, sem):
    f32 = jnp.float32
    tokens = cotangent_ref.shape[0]
    copy = pltpu.make_async_copy(cotangent_ref, line_ref.at[pl.ds(0, tokens)], sem)
    copy.start()
    held[...] = jnp.zeros_like(held)
    held[0:2, : gains_ref.shape[1]] = gains_ref[...].astype(f32)
    held[2:5, : bias_ref.shape[1]] = bias_ref[...].astype(f32)
    held[5:7, :tokens] = routes_ref[...].astype(f32)
    width = router_ref.shape[1]
    for b in range(router_ref.shape[0] // 16):
        part = router_ref[16 * b : 16 * b + 16, :].astype(f32)
        held[16:32, width * b : width * (b + 1)] = part
    line_ref[tokens:, :] = held[...].astype(jnp.bfloat16)
    copy.wait()


def pack_kernel(count, core_ref, *refs):
    mats, out_ref, sems = refs[:count], refs[count + 1], refs[count + 2]
    half = mats[0].shape[0] // 2
    start = pl.multiple_of(core_ref[0] * half, half)
    copies = start_copies(
        [
            (m.at[pl.ds(start, half)], out_ref.at[pl.ds(k * half, half)])
            for k, m in enumerate(mats)
        ],
        sems,
    )
    for c in copies:
        c.wait()


def start_copies(pairs, sems):
    copies = [pltpu.make_async_copy(s, d, sems.at[i]) for i, (s, d) in enumerate(pairs)]
    for c in copies:
        c.start()
    return copies


def block_copies(shard, core, mats, near, far, outs):
    rows = mats[0].shape[0]
    half = rows // 2
    pairs = []
    for k, (mat, out) in enumerate(zip(mats, outs)):
        begin = pl.multiple_of(shard * rows, rows)
        pairs.append((mat, out.at[pl.ds(begin, rows)]))
        part = pl.ds(k * half, half)
        for r in range(1, 4):
            begin = lax.rem(shard + (4 - r), 4) * rows
            mine = pl.multiple_of(begin + core * half, half)
            other = pl.multiple_of(begin + (1 - core) * half, half)
            pairs.append((near[r - 1].at[part], out.at[pl.ds(mine, half)]))
            pairs.append((far[r - 1].at[part], out.at[pl.ds(other, half)]))
    return pairs


def whole_copies(shard, mat, near, out):
    rows = mat.shape[0]
    pairs = []
    for r, piece in enumerate([mat, *near]):
        begin = pl.multiple_of(lax.rem(shard + (4 - r), 4) * rows, rows)
        pairs.append((piece, out.at[pl.ds(begin, rows)]))
    return pairs


def norm_scale(x):
    return lax.rsqrt(jnp.mean(x * x, axis=1, keepdims=True) + epsilon)


def head_half(block, side):
    lanes = lax.broadcasted_iota(jnp.int32, block.shape, 1)
    keep = (lanes < 64) if side == 0 else (lanes >= 64)
    return jnp.where(keep, block, jnp.zeros_like(block))


def to_column(row):
    n = row.shape[1]
    down = lax.broadcasted_iota(jnp.int32, (n, n), 0)
    across = lax.broadcasted_iota(jnp.int32, (n, n), 1)
    return jnp.sum(jnp.where(down == across, row, jnp.zeros_like(row)), axis=1, keepdims=True)


def diagonal_sums(scores):
    n = scores.shape[0]
    down = lax.broadcasted_iota(jnp.int32, (n, n), 0)
    step = 1
    while step < n:
        turned = pltpu.roll(scores, n - step, axis=1)
        scores = jnp.where((down & step) != 0, turned, scores)
        step *= 2
    return jnp.sum(scores, axis=0, keepdims=True)


def bucket_marks():
    shape = (128, 128)
    distance = (128 - lax.broadcasted_iota(jnp.int32, shape, 0)) & 127
    bucket = jnp.zeros(shape, jnp.int32)
    for edge in bucket_edges:
        bucket = bucket + (distance >= edge).astype(jnp.int32)
    mark = bucket == lax.broadcasted_iota(jnp.int32, shape, 1)
    return mark.astype(jnp.float32).astype(jnp.bfloat16)


LAST = (((1,), (1,)), ((), ()))
FIRST = (((0,), (0,)), ((), ()))


def attend_kernel(place_ref, tokens_ref, gain_ref, bias_ref, *refs):
    f32, bf16 = jnp.float32, jnp.bfloat16
    mats, near, far = refs[:3], refs[3:6], refs[6:9]
    hidden_ref, q_ref, k_ref, v_ref, probs_ref, attended_ref = refs[9:15]
    held, sems = refs[15:]
    weights = [held.at[n] for n in range(3)]
    copies = start_copies(
        block_copies(place_ref[0], place_ref[1], mats, near, far, weights), sems
    )
    x = tokens_ref[...].astype(f32)
    hidden = (x * norm_scale(x) * gain_ref[...].astype(f32)).astype(bf16)
    hidden_ref[...] = hidden
    for n, (w, out) in enumerate(zip(weights, (q_ref, k_ref, v_ref))):
        for c in copies[7 * n : 7 * n + 7]:
            c.wait()
        out[...] = jnp.dot(hidden, w[...], preferred_element_type=f32).astype(bf16)
    heads = bias_ref.shape[0]
    for pair in range(heads // 2):
        lanes = slice(pair * 128, pair * 128 + 128)
        q, k, v = q_ref[:, lanes], k_ref[:, lanes], v_ref[:, lanes]
        total = jnp.zeros(q.shape, f32)
        for side in range(2):
            h = 2 * pair + side
            scores = lax.dot_general(q, head_half(k, side), LAST, preferred_element_type=f32)
            scores = scores * 0.125 + bias_ref[h]
            top = jnp.max(scores, axis=1, keepdims=True)
            grown = jnp.exp(scores - top)
            probs = grown / jnp.sum(grown, axis=1, keepdims=True)
            probs_ref[h] = probs
            total = total + jnp.dot(
                probs.astype(bf16), head_half(v, side), preferred_element_type=f32
            )
        attended_ref[:, lanes] = total.astype(bf16)


def middle_kernel(place_ref, tokens_ref, gain_ref, attended_ref, *refs):
    f32 = jnp.float32
    mat, near = refs[0], refs[1:4]
    middle_ref, moe_ref, weight, sems = refs[4:8]
    copies = start_copies(whole_copies(place_ref[0], mat, near, weight), sems)
    for c in copies:
        c.wait()
    middle = tokens_ref[...].astype(f32) + jnp.dot(
        attended_ref[...], weight[...], preferred_element_type=f32
    )
    middle_ref[...] = middle
    moe_ref[...] = (middle * norm_scale(middle) * gain_ref[...].astype(f32)).astype(jnp.bfloat16)


def backward_kernel(
    place_ref,
    tokens_ref,
    cotangent_ref,
    gain_one_ref,
    gain_two_ref,
    ids_ref,
    router_ref,
    middle_ref,
    moe_ref,
    attended_ref,
    hidden_ref,
    q_ref,
    k_ref,
    v_ref,
    probs_ref,
    spots_ref,
    rows_ref,
    *refs,
):
    f32, bf16 = jnp.float32, jnp.bfloat16
    homes, mats, near, far, near_out = refs[:4], refs[4:8], refs[8:11], refs[11:14], refs[14:17]
    result_ref, tokens_out, kept_ref, given_ref = refs[17:21]
    held, grads_ref, small_ref, sems = refs[21:]
    weights = [held.at[n] for n in range(4)]
    copies = start_copies(
        block_copies(place_ref[0], place_ref[1], mats[:3], near, far, weights[:3])
        + whole_copies(place_ref[0], mats[3], near_out, weights[3]),
        sems,
    )
    features = tokens_ref.shape[1]
    core = place_ref[1]
    width = features // 4
    small_ref[...] = jnp.zeros_like(small_ref)

    def leave(mat, left, right):
        grad = lax.dot_general(left, right, FIRST, preferred_element_type=f32).astype(bf16)
        grads_ref[...] = grad
        for x in range(4):
            low = grads_ref[x * 192 : x * 192 + 96, :]
            high = grads_ref[x * 192 + 96 : x * 192 + 192, :]
            at = (mat * 4 + x) * 96
            kept_ref[at : at + 96, :features] = jnp.where(core == 0, low, high)
            given_ref[at : at + 96, :features] = jnp.where(core == 0, high, low)

    def leave_wide(mats_rows, block):
        for x in range(4):
            for (mat, row), begin, size in zip(mats_rows, (0, 128), (128, 64)):
                at = (mat * 4 + x) * 96 + row
                small_ref[at : at + block.shape[0], :size] = block[
                    :, x * width + begin : x * width + begin + size
                ]

    home = homes[0][...].astype(f32)
    for piece in homes[1:]:
        home = home + piece[...].astype(f32)
    middle = middle_ref[...]
    result_ref[...] = (middle + home[:, :features]).astype(bf16)
    tail = home[:, features:]
    lane = lax.broadcasted_iota(jnp.int32, tail.shape, 1)
    grad_gates = [
        jnp.sum(jnp.where((lane == k) | (lane == 2 + k), tail, 0.0), axis=1, keepdims=True)
        for k in range(2)
    ]
    moe = moe_ref[...]
    logits = lax.dot_general(moe, router_ref[...], LAST, preferred_element_type=f32)
    ids = [to_column(ids_ref[k : k + 1, : tail.shape[0]]) for k in range(2)]
    gates = gate_pair(chosen_logit(logits, ids[0]), chosen_logit(logits, ids[1]))
    mix = gates[0] * grad_gates[0] + gates[1] * grad_gates[1]
    spots = lax.broadcasted_iota(jnp.int32, logits.shape, 1)
    grad_logits = jnp.zeros(logits.shape, f32)
    for k in range(2):
        grad_logits = jnp.where(spots == ids[k], gates[k] * (grad_gates[k] - mix), grad_logits)
    grad_logits = grad_logits.astype(bf16)
    slot = lax.broadcasted_iota(jnp.int32, (rows_ref.shape[0], tail.shape[0]), 0)
    pick = ((slot == spots_ref[0:1]) | (slot == spots_ref[1:2])).astype(f32).astype(bf16)
    grad_moe = lax.dot_general(pick, rows_ref[...], FIRST, preferred_element_type=f32)
    grad_moe = grad_moe + jnp.dot(grad_logits, router_ref[...], preferred_element_type=f32)
    leave_wide(
        ((0, 0), (1, 0)),
        lax.dot_general(grad_logits, moe, FIRST, preferred_element_type=f32),
    )
    scale = norm_scale(middle)
    normed = middle * scale
    leave_wide(((2, 2), (2, 3)), jnp.sum(grad_moe * normed, axis=0, keepdims=True))
    inner = grad_moe * gain_two_ref[...].astype(f32)
    grad_middle = cotangent_ref[...].astype(f32) + scale * (
        inner - normed * jnp.mean(inner * normed, axis=1, keepdims=True)
    )
    branch = grad_middle.astype(bf16)
    leave(3, attended_ref[...], branch)
    for c in copies[21:]:
        c.wait()
    grad_attended = lax.dot_general(branch, held[3], LAST, preferred_element_type=f32).astype(bf16)
    grad_q, grad_k, grad_v, diagonals = [], [], [], []
    for pair in range(probs_ref.shape[0] // 2):
        lanes = slice(pair * 128, pair * 128 + 128)
        q, k, v = q_ref[:, lanes], k_ref[:, lanes], v_ref[:, lanes]
        grad = grad_attended[:, lanes]
        parts = [jnp.zeros(q.shape, f32) for _ in range(3)]
        for side in range(2):
            h = 2 * pair + side
            probs = probs_ref[h]
            grad_half = head_half(grad, side)
            parts[2] = parts[2] + lax.dot_general(
                probs.astype(bf16), grad_half, FIRST, preferred_element_type=f32
            )
            grad_probs = lax.dot_general(grad_half, v, LAST, preferred_element_type=f32)
            grad_scores = (
                probs * (grad_probs - jnp.sum(probs * grad_probs, axis=1, keepdims=True))
            ).astype(bf16)
            diagonals.append(diagonal_sums(grad_scores.astype(f32)))
            parts[0] = parts[0] + jnp.dot(
                grad_scores, head_half(k, side), preferred_element_type=f32
            )
            parts[1] = parts[1] + lax.dot_general(
                grad_scores, head_half(q, side), FIRST, preferred_element_type=f32
            )
        grad_q.append((parts[0] * 0.125).astype(bf16))
        grad_k.append((parts[1] * 0.125).astype(bf16))
        grad_v.append(parts[2].astype(bf16))
    left = jnp.concatenate(diagonals, axis=0)
    grad_bias = jnp.zeros((left.shape[0], 128), f32)
    for _ in range(3):
        part = left.astype(bf16)
        left = left - part.astype(f32)
        grad_bias = grad_bias + jnp.dot(part, bucket_marks(), preferred_element_type=f32)
    per = left.shape[0] // 4
    for a in range(4):
        at = (8 + a) * 96 + 4
        small_ref[at : at + per, :] = grad_bias[a * per : a * per + per, :]
    hidden = hidden_ref[...]
    grad_hidden = jnp.zeros(hidden.shape, f32)
    for n, parts in enumerate((grad_q, grad_k, grad_v)):
        grad = jnp.concatenate(parts, axis=1)
        leave(n, hidden, grad)
        for c in copies[7 * n : 7 * n + 7]:
            c.wait()
        grad_hidden = grad_hidden + lax.dot_general(
            grad, held[n], LAST, preferred_element_type=f32
        )
    x = tokens_ref[...].astype(f32)
    scale = norm_scale(x)
    normed = x * scale
    leave_wide(((2, 0), (2, 1)), jnp.sum(grad_hidden * normed, axis=0, keepdims=True))
    inner = grad_hidden * gain_one_ref[...].astype(f32)
    tokens_out[...] = grad_middle + scale * (
        inner - normed * jnp.mean(inner * normed, axis=1, keepdims=True)
    )
    small = small_ref[...].astype(bf16)
    none = jnp.zeros_like(small)
    kept_ref[:, features:] = jnp.where(core == 0, small, none)
    given_ref[:, features:] = jnp.where(core == 0, none, small)


ANYWHERE = pl.BlockSpec(memory_space=pl.ANY)
SCALARS = pl.BlockSpec(memory_space=pltpu.SMEM)
WHOLE = pl.BlockSpec(memory_space=pltpu.VMEM)
ROOM = pltpu.CompilerParams(vmem_limit_bytes=56 * 1024 * 1024)


def make_line(routes, gains, bias, router, cotangent):
    tokens, cols = cotangent.shape
    return pl.pallas_call(
        line_kernel,
        out_shape=jax.ShapeDtypeStruct((tokens + 32, cols), jnp.bfloat16),
        in_specs=[WHOLE] * 4 + [ANYWHERE],
        out_specs=WHOLE,
        scratch_shapes=[pltpu.VMEM((32, cols), jnp.float32), pltpu.SemaphoreType.DMA],
        compiler_params=ROOM,
        name="line",
    )(routes, gains, bias, router, cotangent)


def pack(core, mats, after):
    rows, cols = mats[0].shape
    count = len(mats)
    return pl.pallas_call(
        functools.partial(pack_kernel, count),
        out_shape=jax.ShapeDtypeStruct((count * rows // 2, cols), jnp.bfloat16),
        in_specs=[SCALARS] + [ANYWHERE] * (count + 1),
        out_specs=WHOLE,
        scratch_shapes=[pltpu.SemaphoreType.DMA((count,))],
        compiler_params=ROOM,
        name="pack",
    )(core[None], *mats, after)


def hold_back_kernel(mat_ref, _, out_ref):
    out_ref[...] = mat_ref[...]


def hold_back(mat, after):
    return pl.pallas_call(
        hold_back_kernel,
        out_shape=jax.ShapeDtypeStruct(mat.shape, mat.dtype),
        in_specs=[WHOLE, ANYWHERE],
        out_specs=WHOLE,
        name="hold_back",
    )(mat, after)


def attend(where, tokens, gain, bias, mats, near, far):
    rows, cols = mats[0].shape
    state = jax.ShapeDtypeStruct(tokens.shape, jnp.bfloat16)
    return pl.pallas_call(
        attend_kernel,
        out_shape=[state] * 4 + [jax.ShapeDtypeStruct(bias.shape, jnp.float32), state],
        in_specs=[SCALARS] + [WHOLE] * 3 + [ANYWHERE] * 9,
        out_specs=[WHOLE] * 6,
        scratch_shapes=[
            pltpu.VMEM((3, 4 * rows, cols), jnp.bfloat16),
            pltpu.SemaphoreType.DMA((21,)),
        ],
        compiler_params=ROOM,
        cost_estimate=pl.CostEstimate(
            flops=80000000000, bytes_accessed=300000000, transcendentals=0
        ),
        name="attend",
    )(where, tokens, gain, bias, *mats, *near, *far)


def to_middle(where, tokens, gain, attended, mat, near):
    rows, cols = mat.shape
    return pl.pallas_call(
        middle_kernel,
        out_shape=[
            jax.ShapeDtypeStruct(tokens.shape, jnp.float32),
            jax.ShapeDtypeStruct(tokens.shape, jnp.bfloat16),
        ],
        in_specs=[SCALARS] + [WHOLE] * 3 + [ANYWHERE] * 4,
        out_specs=[WHOLE] * 2,
        scratch_shapes=[
            pltpu.VMEM((4 * rows, cols), jnp.bfloat16),
            pltpu.SemaphoreType.DMA((4,)),
        ],
        compiler_params=ROOM,
        name="middle",
    )(where, tokens, gain, attended, mat, *near)


def backward(where, *arrays):
    tokens = arrays[0]
    count, features = tokens.shape
    bf16, f32 = jnp.bfloat16, jnp.float32
    shape = jax.ShapeDtypeStruct
    return pl.pallas_call(
        backward_kernel,
        out_shape=[
            shape((count, features), bf16),
            shape((count, features), f32),
            shape((2 * features, features + 128), bf16),
            shape((2 * features, features + 128), bf16),
        ],
        in_specs=[SCALARS] + [WHOLE] * 20 + [ANYWHERE] * 13,
        out_specs=[WHOLE] * 4,
        scratch_shapes=[
            pltpu.VMEM((4, features, features), bf16),
            pltpu.VMEM((features, features), bf16),
            pltpu.VMEM((2 * features, 128), f32),
            pltpu.SemaphoreType.DMA((25,)),
        ],
        compiler_params=ROOM,
        name="backward",
    )(where, *arrays)


def finish_kernel(core_ref, own_ref, other_ref, *refs):
    mats, (router_out, gains_out, bias_out) = refs[:4], refs[4:]
    f32 = jnp.float32
    core = core_ref[0]
    half = own_ref.shape[0] // 4
    features = mats[0].shape[1]
    own, other = own_ref[...].astype(f32), other_ref[...].astype(f32)
    low, high = jnp.where(core == 0, own, other), jnp.where(core == 0, other, own)
    for k, out in enumerate(mats):
        here = slice(k * half, (k + 1) * half)
        out[:half, :] = low[here, :features]
        out[half:, :] = high[here, :features]
    small = low[:, features:]
    tall = router_out.shape[0]
    router_out[:, :128] = small[:tall, :]
    router_out[:, 128:] = small[half : half + tall, :64]
    for k in range(2):
        at = 2 * half + 2 * k
        gains_out[k : k + 1, :128] = small[at : at + 1, :]
        gains_out[k : k + 1, 128:] = small[at + 1 : at + 2, :64]
    at = 2 * half + 4
    bias_out[...] = small[at : at + bias_out.shape[0], : bias_out.shape[1]]


def finish(core, own, other, shard_rows, experts_all, bias_shape):
    features = own.shape[1] - 128
    shape = lambda *s: jax.ShapeDtypeStruct(s, jnp.float32)
    return pl.pallas_call(
        finish_kernel,
        out_shape=[shape(shard_rows, features)] * 4
        + [shape(experts_all, shard_rows), shape(2, shard_rows), shape(*bias_shape)],
        in_specs=[SCALARS] + [WHOLE] * 2,
        out_specs=[WHOLE] * 7,
        compiler_params=ROOM,
        name="finish",
    )(core, own, other)


def picks_of(places, e, rows):
    row = lax.broadcasted_iota(jnp.int32, (rows, places.shape[1]), 0) + e * rows
    return ((row == places[0:1]) | (row == places[1:2])).astype(jnp.float32).astype(jnp.bfloat16)


def dispatch_grads_kernel(capacity, place_ref, *refs):
    pieces, (out_ref, places_ref, ids_ref, spots_ref) = refs[:4], refs[5:9]
    gains_ref, bias_ref, router_ref = refs[9:]
    f32, bf16, i32 = jnp.float32, jnp.bfloat16, jnp.int32
    rows = out_ref.shape[0]
    tokens = spots_ref.shape[1]
    features = pieces[0].shape[1]
    experts_all = 2 * rows // (4 * capacity)
    expert = lax.broadcasted_iota(i32, (experts_all, tokens), 0)
    down = lax.broadcasted_iota(i32, (tokens, tokens), 0)
    across = lax.broadcasted_iota(i32, (tokens, tokens), 1)
    earlier = (down < across).astype(f32).astype(bf16)
    sums = []
    for r in range(4):
        both = pieces[r][tokens : tokens + 16, :tokens].astype(f32)
        ids = [both[5 + k : 6 + k].astype(i32) for k in range(2)]
        match = [expert == i for i in ids]
        named = (match[0] | match[1]).astype(f32).astype(bf16)
        counts = jnp.dot(named, earlier, preferred_element_type=f32)
        here = slice(r * tokens, (r + 1) * tokens)
        for k in range(2):
            slot = jnp.sum(jnp.where(match[k], counts, 0.0), axis=0, keepdims=True).astype(i32)
            owner, local = ids[k] >> 1, ids[k] & 1
            places_ref[k : k + 1, here] = (
                local * rows + owner * (4 * capacity) + r * capacity + slot
            )
            ids_ref[k : k + 1, here] = ids[k]
            if r == 0:
                spots_ref[k : k + 1, :] = owner * 16 + local * capacity + slot
        sums.append(to_column(both[5:6] + both[6:7]))
    sums = jnp.concatenate(sums, axis=0)
    lanes = lax.broadcasted_iota(i32, (4 * tokens, 128), 1)
    line = jnp.concatenate([p[:tokens, :] for p in pieces], axis=0)
    places = places_ref[...]
    extra = jnp.zeros((rows, 128), f32)
    for e in range(2):
        pick = picks_of(places, e, rows)
        out_ref[:, e * features : (e + 1) * features] = jnp.dot(
            pick, line, preferred_element_type=f32
        ).astype(bf16)
        column = jnp.where(lanes == e, sums, 0.0).astype(bf16)
        extra = extra + jnp.dot(pick, column, preferred_element_type=f32)
    out_ref[:, 2 * features :] = extra.astype(bf16)
    smalls = [p[tokens:, :].astype(f32) for p in pieces]
    width = features // 4
    heads = bias_ref.shape[0] // 4
    for a in range(4):
        at = (place_ref[0] - a) & 3
        small = jnp.zeros_like(smalls[0])
        for k in range(4):
            small = jnp.where(at == k, smalls[k], small)
        here = slice(a * width, (a + 1) * width)
        gains_ref[:, here] = small[0:2, :width]
        bias_ref[a * heads : (a + 1) * heads, :] = small[2 : 2 + heads, : bias_ref.shape[1]]
        for b in range(router_ref.shape[0] // 16):
            router_ref[16 * b : 16 * b + 16, here] = small[16:32, width * b : width * (b + 1)]


def dispatch_grads(where, pieces, rows, capacity, tokens, experts_all, bias_shape, after):
    features = pieces[0].shape[1]
    shape = jax.ShapeDtypeStruct
    return pl.pallas_call(
        functools.partial(dispatch_grads_kernel, capacity),
        out_shape=[
            shape((rows, 2 * features + 128), jnp.bfloat16),
            shape((2, 4 * tokens), jnp.int32),
            shape((2, 4 * tokens), jnp.int32),
            shape((2, tokens), jnp.int32),
            shape((2, features), jnp.float32),
            shape(bias_shape, jnp.float32),
            shape((experts_all, features), jnp.float32),
        ],
        in_specs=[SCALARS] + [WHOLE] * 4 + [ANYWHERE],
        out_specs=[WHOLE] * 7,
        compiler_params=ROOM,
        cost_estimate=pl.CostEstimate(
            flops=30000000000, bytes_accessed=100000000, transcendentals=0
        ),
        name="dispatch_grads",
    )(where, *pieces, after)


def dispatch_kernel(places_ref, *refs):
    pieces, out_ref = refs[:4], refs[5]
    rows = out_ref.shape[0]
    features = pieces[0].shape[1]
    line = jnp.concatenate([p[...] for p in pieces], axis=0)
    for e in range(2):
        out_ref[:, e * features : (e + 1) * features] = jnp.dot(
            picks_of(places_ref[...], e, rows), line, preferred_element_type=jnp.float32
        ).astype(jnp.bfloat16)


def dispatch(places, pieces, rows, after):
    return pl.pallas_call(
        dispatch_kernel,
        out_shape=jax.ShapeDtypeStruct((rows, 2 * pieces[0].shape[1]), jnp.bfloat16),
        in_specs=[WHOLE] * 5 + [ANYWHERE],
        out_specs=WHOLE,
        compiler_params=ROOM,
        name="dispatch",
    )(places, *pieces, after)


def chosen_logit(logits, ids):
    lanes = lax.broadcasted_iota(jnp.int32, logits.shape, 1)
    return jnp.sum(jnp.where(lanes == ids, logits, 0.0), axis=1, keepdims=True)


def gate_pair(first, second):
    top = jnp.maximum(first, second)
    one, two = jnp.exp(first - top), jnp.exp(second - top)
    total = one + two
    return one / total, two / total


def expert_kernel(x_ref, in_ref, out_ref, ret_ref, act_ref, rise_ref):
    f32, bf16 = jnp.float32, jnp.bfloat16
    slope = math.sqrt(2.0 / math.pi)
    pre = jnp.dot(x_ref[...], in_ref[0], preferred_element_type=f32)
    tanh = jnp.tanh(slope * (pre + 0.044715 * (pre * pre * pre)))
    active = (0.5 * pre * (1.0 + tanh)).astype(bf16)
    act_ref[0] = active
    ret_ref[...] = jnp.dot(active, out_ref[0], preferred_element_type=f32).astype(bf16)
    rise_ref[0] = 0.5 * (1.0 + tanh) + 0.5 * pre * (1.0 - tanh * tanh) * (
        slope * (1.0 + 3.0 * 0.044715 * (pre * pre))
    )


STEP = 256


def lanes_of(n):
    return pl.BlockSpec((STEP, n), lambda e, i: (i, e))


def rows_of(n):
    return pl.BlockSpec((1, STEP, n), lambda e, i: (e, i, 0))


def one_of(a, b):
    return pl.BlockSpec((1, a, b), lambda e, i: (e, 0, 0))


def experts(arrived, w_in, w_out):
    rows = arrived.shape[0]
    features, hidden = w_in.shape[1:]
    return pl.pallas_call(
        expert_kernel,
        grid=(2, rows // STEP),
        out_shape=[
            jax.ShapeDtypeStruct((rows, 2 * features), jnp.bfloat16),
            jax.ShapeDtypeStruct((2, rows, hidden), jnp.bfloat16),
            jax.ShapeDtypeStruct((2, rows, hidden), jnp.float32),
        ],
        in_specs=[lanes_of(features), one_of(features, hidden), one_of(hidden, features)],
        out_specs=[lanes_of(features), rows_of(hidden), rows_of(hidden)],
        compiler_params=ROOM,
        name="experts",
    )(arrived, w_in, w_out)


def expert_back_kernel(
    capacity, own_ref, x_ref, g_ref, ids_ref, in_ref, out_ref, router_ref, rise_ref, *refs
):
    pre_ref, arr_ref, outs, held = refs[0], refs[1], refs[2:6], refs[6]
    f32, bf16, i32 = jnp.float32, jnp.bfloat16, jnp.int32
    e = pl.program_id(0)
    own = own_ref[0] + e
    rows = x_ref.shape[0]
    step = 256

    def chunk(i, carry):
        at = pl.ds(pl.multiple_of(i * step, step), step)
        ids = ids_ref[at, :].astype(f32)
        lanes = lax.broadcasted_iota(i32, ids.shape, 1)
        other = jnp.sum(jnp.where(lanes == e, ids, 0.0), axis=1, keepdims=True).astype(i32) - own
        logits = lax.dot_general(
            x_ref[at, :], router_ref[...], LAST, preferred_element_type=f32
        )
        gate, _ = gate_pair(chosen_logit(logits, own), chosen_logit(logits, other))
        grown = (gate * g_ref[at, :].astype(f32)).astype(bf16)
        arr_ref[0, at, :] = grown
        back = lax.dot_general(grown, out_ref[0], LAST, preferred_element_type=f32)
        grad = (back * rise_ref[0, at, :]).astype(bf16)
        pre_ref[0, at, :] = grad
        held[at, :] = lax.dot_general(grad, in_ref[0], LAST, preferred_element_type=f32).astype(
            bf16
        )
        return carry

    lax.fori_loop(0, rows // step, chunk, 0)
    part = rows // 4
    here = lax.broadcasted_iota(i32, (part, rows), 0)
    there = lax.broadcasted_iota(i32, (part, rows), 1)
    block = (here * (65536 // capacity + 1)) >> 16
    for r, out in enumerate(outs):
        source = here + block * (3 * capacity) + r * capacity
        pick = (there == source).astype(f32).astype(bf16)
        out[...] = jnp.dot(pick, held[...], preferred_element_type=f32).astype(bf16)


def experts_back(own, arrived, grad_wide, w_in, w_out, router_w, rise, capacity):
    rows = arrived.shape[0]
    features, hidden = w_in.shape[1:]
    bf16 = jnp.bfloat16
    shape = jax.ShapeDtypeStruct
    part = rows // 4
    lanes = lambda n: pl.BlockSpec((rows, n), lambda e: (0, e))
    one = lambda a, b: pl.BlockSpec((1, a, b), lambda e: (e, 0, 0))
    return pl.pallas_call(
        functools.partial(expert_back_kernel, capacity),
        grid=(2,),
        out_shape=[shape((2, rows, hidden), bf16), shape((2, rows, features), bf16)]
        + [shape((2 * part, features), bf16)] * 4,
        in_specs=[
            SCALARS,
            lanes(features),
            lanes(features),
            pl.BlockSpec((rows, 128), lambda e: (0, 2 * features // 128)),
            one(features, hidden),
            one(hidden, features),
            pl.BlockSpec(router_w.shape, lambda e: (0, 0)),
            one(rows, hidden),
        ],
        out_specs=[one(rows, hidden), one(rows, features)]
        + [pl.BlockSpec((part, features), lambda e: (e, 0))] * 4,
        scratch_shapes=[pltpu.VMEM((rows, features), bf16)],
        compiler_params=ROOM,
        name="experts_back",
    )(own[None], arrived, grad_wide, grad_wide, w_in, w_out, router_w, rise)


def weight_grads_kernel(x_ref, pre_ref, act_ref, arr_ref, in_ref, out_ref):
    in_ref[0] = lax.dot_general(x_ref[...], pre_ref[0], FIRST, preferred_element_type=jnp.float32)
    out_ref[0] = lax.dot_general(act_ref[0], arr_ref[0], FIRST, preferred_element_type=jnp.float32)


def weight_grads(arrived, grad_pre, active, grad_arrived):
    rows = arrived.shape[0]
    hidden, features = grad_pre.shape[2], grad_arrived.shape[2]
    step = 256
    cuts = features // step
    whole = lambda n: pl.BlockSpec((1, rows, n), lambda e, j: (e, 0, 0))
    out = lambda n: pl.BlockSpec((1, step, n), lambda e, j: (e, j, 0))
    return pl.pallas_call(
        weight_grads_kernel,
        grid=(2, cuts),
        out_shape=[
            jax.ShapeDtypeStruct((2, features, hidden), jnp.float32),
            jax.ShapeDtypeStruct((2, hidden, features), jnp.float32),
        ],
        in_specs=[
            pl.BlockSpec((rows, step), lambda e, j: (0, e * cuts + j)),
            whole(hidden),
            pl.BlockSpec((1, rows, step), lambda e, j: (e, 0, j)),
            whole(features),
        ],
        out_specs=[out(hidden), out(features)],
        compiler_params=ROOM,
        cost_estimate=pl.CostEstimate(
            flops=8 * rows * features * hidden, bytes_accessed=20_000_000, transcendentals=0
        ),
        name="weight_grads",
    )(arrived, grad_pre, active, grad_arrived)


def sum_rows_kernel(capacity, *refs):
    pieces, out_ref = refs[:4], refs[-1]
    f32, bf16, i32 = jnp.float32, jnp.bfloat16, jnp.int32
    total = pieces[0][...].astype(f32)
    for piece in pieces[1:]:
        total = total + piece[...].astype(f32)
    rows = out_ref.shape[0]
    part = total.shape[0] // 2
    here = lax.broadcasted_iota(i32, (rows, 2 * part), 0)
    there = lax.broadcasted_iota(i32, (rows, 2 * part), 1)
    owner, q = here >> 4, here & 15
    second = q >= capacity
    source = owner * capacity + jnp.where(second, part + q - capacity, q)
    pick = ((there == source) & (q < 2 * capacity)).astype(f32).astype(bf16)
    out_ref[...] = jnp.dot(pick, total.astype(bf16), preferred_element_type=f32).astype(bf16)


def sum_rows(pieces, capacity, after):
    rows, features = pieces[0].shape
    return pl.pallas_call(
        functools.partial(sum_rows_kernel, capacity),
        out_shape=jax.ShapeDtypeStruct((rows // (2 * capacity) * 16, features), jnp.bfloat16),
        in_specs=[WHOLE] * 4 + [ANYWHERE] * len(after),
        out_specs=WHOLE,
        compiler_params=ROOM,
        cost_estimate=pl.CostEstimate(
            flops=20000000000, bytes_accessed=60000000, transcendentals=0
        ),
        name="sum_rows",
    )(*pieces, *after)


def combine_kernel(places_ref, ids_ref, router_ref, ret_ref, *refs):
    f32, bf16 = jnp.float32, jnp.bfloat16
    grads, moes, outs = refs[:4], refs[4:8], refs[9:13]
    tokens, features = moes[0].shape
    rows = ret_ref.shape[0]
    row = lax.broadcasted_iota(jnp.int32, (rows, tokens), 0)
    tail_lane = lax.broadcasted_iota(jnp.int32, (tokens, 128), 1)
    for r in range(4):
        here = slice(r * tokens, (r + 1) * tokens)
        logits = lax.dot_general(
            moes[r][...], router_ref[...], LAST, preferred_element_type=f32
        )
        ids = [to_column(ids_ref[k : k + 1, here]) for k in range(2)]
        gates = gate_pair(chosen_logit(logits, ids[0]), chosen_logit(logits, ids[1]))
        total = jnp.zeros((tokens, features), f32)
        tail = jnp.zeros((tokens, 128), f32)
        grad = grads[r][:tokens, :].astype(f32)
        for k in range(2):
            got = jnp.zeros((tokens, features), f32)
            for e in range(2):
                pick = (row + e * rows == places_ref[k : k + 1, here]).astype(f32).astype(bf16)
                got = got + lax.dot_general(
                    pick,
                    ret_ref[:, e * features : (e + 1) * features],
                    FIRST,
                    preferred_element_type=f32,
                )
            total = total + gates[k] * got
            dots = jnp.sum(grad * got, axis=1, keepdims=True)
            high = dots.astype(bf16).astype(f32)
            tail = jnp.where(tail_lane == k, high, tail)
            tail = jnp.where(tail_lane == 2 + k, dots - high, tail)
        outs[r][:, :features] = total.astype(bf16)
        outs[r][:, features:] = tail.astype(bf16)


def combine(places, ids, router_w, returned, grads, moes, after):
    tokens, features = moes[0].shape
    return pl.pallas_call(
        combine_kernel,
        out_shape=[jax.ShapeDtypeStruct((tokens, features + 128), jnp.bfloat16)] * 4,
        in_specs=[WHOLE] * 12 + [ANYWHERE],
        out_specs=[WHOLE] * 4,
        compiler_params=ROOM,
        name="combine",
    )(places, ids, router_w, returned, *grads, *moes, after)


def layer(
    tokens,
    seq_lengths,
    routes,
    gain_attn,
    w_query,
    w_key,
    w_value,
    w_output,
    rel_bias,
    gain_moe,
    w_router,
    w_in,
    w_out,
    cotangent,
):
    row_count, features = tokens.shape
    shard_rows = w_query.shape[0]
    expert_count = w_router.shape[1]
    bucket_count = rel_bias.shape[1]
    head_count = 4 * rel_bias.shape[0]
    capacity = 3 * row_count // expert_count
    f32 = jnp.float32
    bf16 = jnp.bfloat16

    shard = lax.axis_index("x").astype(jnp.int32)
    core = lax.axis_index("c").astype(jnp.int32)
    where = jnp.stack([shard, core])
    owners = expert_count // 2
    slot_rows = owners * 4 * capacity

    line = make_line(
        routes.T, jnp.stack([gain_attn, gain_moe]), rel_bias, w_router.T, cotangent
    )
    line_grads = along_x(line)
    sent = pack(core, (w_query, w_key, w_value), line)
    near = along_x(sent)[1:]
    def to_owners(outgoing):
        return lax.all_to_all(outgoing, ("y", "z", "c"), 0, 0, tiled=True)

    outgoing_grads, places, ids, spots, gains, bias_table, router_f = dispatch_grads(
        where,
        line_grads,
        slot_rows,
        capacity,
        row_count,
        expert_count,
        (head_count, bucket_count),
        line,
    )
    gain_one, gain_two = gains[0:1], gains[1:2]
    bias_table, router_w = bias_table.astype(bf16), router_f.astype(bf16)
    grad_wide = to_owners(outgoing_grads)
    near_out = along_x(hold_back(w_output, outgoing_grads))[1:]
    first_expert = 2 * lax.axis_index(("y", "z", "c")).astype(jnp.int32)

    segments = row_segments(seq_lengths[0], row_count)
    distance, onehot = position_tables(row_count, bucket_count)
    allowed = (segments[:, None] == segments[None, :]) & (distance >= 0)
    position_bias = jnp.einsum("ijb,hb->hij", onehot, bias_table, preferred_element_type=f32)
    masked_bias = jnp.where(allowed[None], position_bias, -1000000000.0)
    far = [swap_core(piece) for piece in near]
    hidden_one, queries, key_rows, value_rows, probs, attended = attend(
        where,
        tokens,
        gain_one,
        masked_bias,
        (w_query, w_key, w_value),
        near,
        far,
    )
    middle, moe_in = to_middle(
        where, tokens, gain_two, attended, w_output, near_out
    )

    line_moe = along_x(moe_in)
    arrived = to_owners(dispatch(places, line_moe, slot_rows, grad_wide))
    ret, active, rise = experts(arrived, w_in, w_out)
    returned = to_owners(ret)
    grad_pre, grad_arrived, *blocks = experts_back(
        first_expert, arrived, grad_wide, w_in, w_out, router_w, rise, capacity
    )
    summed = [blocks[0]] + [shift_x(blocks[r], -r) for r in range(1, 4)]
    grad_w_in, grad_w_out = weight_grads(arrived, grad_pre, active, grad_arrived)
    bundle = combine(places, ids, router_w, returned, line_grads, line_moe, grad_w_in)
    back_rows = to_owners(sum_rows(summed, capacity, (grad_w_out, bundle[0])))
    homes = [bundle[0]] + [shift_x(bundle[r], -r) for r in range(1, 4)]
    result, grad_tokens, kept, given = backward(
        where,
        tokens,
        cotangent,
        gain_one,
        gain_two,
        ids,
        router_w,
        middle,
        moe_in,
        attended,
        hidden_one,
        queries,
        key_rows,
        value_rows,
        probs,
        spots,
        back_rows,
        *homes,
        w_query,
        w_key,
        w_value,
        w_output,
        *near,
        *far,
        *near_out,
    )
    piece = shard_rows // 8
    wide = features + 128
    paired = (kept.astype(f32) + swap_core(given).astype(f32)).astype(bf16)
    spread = lax.all_to_all(paired, ("y", "x", "z"), 0, 0, tiled=True)
    mine = jnp.sum(spread.reshape(64, piece, wide).astype(f32), axis=0).astype(bf16)
    half = lax.all_to_all(
        jnp.broadcast_to(mine[None], (16, piece, wide)).reshape(16 * piece, wide),
        ("y", "z"),
        0,
        0,
        tiled=True,
    )
    *totals, router_total, gain_totals, bias_total = finish(
        core[None], half, swap_core(half), shard_rows, expert_count, rel_bias.shape
    )
    router_total = router_total.T
    gain_one_total, gain_two_total = gain_totals[0], gain_totals[1]
    return (
        result,
        grad_tokens,
        gain_one_total,
        totals[0],
        totals[1],
        totals[2],
        totals[3],
        bias_total,
        gain_two_total,
        router_total,
        grad_w_in,
        grad_w_out,
    )


def solution(mesh):
    cube = Mesh(mesh.devices.reshape(4, 4, 2, 4), ("y", "z", "c", "x"))
    expert = ("y", "z", "c")
    everyone = ("y", "z", "c", "x")
    placed = (
        P(everyone, None),
        P(everyone, None),
        P(everyone, None),
        P("x"),
        P("x", None),
        P("x", None),
        P("x", None),
        P("x", None),
        P("x", None),
        P("x"),
        P("x", None),
        P(expert, None, "x"),
        P(expert, "x", None),
        P(everyone, None),
    )
    return jax.shard_map(
        layer,
        mesh=cube,
        in_specs=placed,
        out_specs=(
            P(everyone, None),
            P(everyone, None),
            P("x"),
            P("x", None),
            P("x", None),
            P("x", None),
            P("x", None),
            P("x", None),
            P("x"),
            P("x", None),
            P(expert, None, "x"),
            P(expert, "x", None),
        ),
        check_vma=False,
    )
```

```python
import functools
import math

import jax
import jax.numpy as jnp
from jax import lax
from jax.experimental import pallas as pl
from jax.experimental.pallas import tpu as pltpu
from jax.sharding import Mesh, PartitionSpec as P

epsilon = 1e-06
bucket_edges = list(range(1, 17)) + [
    int(math.ceil(16.0 * 8.0 ** ((bucket_level - 16) / 16.0))) for bucket_level in range(17, 32)
]


def row_segments(lengths, row_count):
    sequence_ends = jnp.cumsum(lengths)
    positions = jnp.arange(row_count, dtype=jnp.int32)
    return jnp.sum((positions[:, None] >= sequence_ends[None, :]).astype(jnp.int32), axis=1)


def position_tables(row_count, bucket_count):
    positions = jnp.arange(row_count, dtype=jnp.int32)
    distance = positions[:, None] - positions[None, :]
    edge_values = jnp.array(bucket_edges, dtype=jnp.int32)
    bucket = jnp.sum((distance[:, :, None] >= edge_values).astype(jnp.int32), axis=2)
    onehot = (bucket[:, :, None] == jnp.arange(bucket_count, dtype=jnp.int32)).astype(jnp.bfloat16)
    return (distance, onehot)


def shift(block, axis, step):
    ranks = lax.axis_size(axis)
    return lax.ppermute(block, axis, [(i, (i + step) % ranks) for i in range(ranks)])


def shift_x(block, step):
    return shift(block, "x", step)


def swap_core(block):
    return lax.ppermute(block, "c", [(0, 1), (1, 0)])


def along_x(block):
    return [block, shift_x(block, 1), shift_x(block, 2), shift_x(block, 3)]


def line_kernel(routes_ref, gains_ref, bias_ref, router_ref, cotangent_ref, line_ref, held, sem):
    f32 = jnp.float32
    tokens = cotangent_ref.shape[0]
    copy = pltpu.make_async_copy(cotangent_ref, line_ref.at[pl.ds(0, tokens)], sem)
    copy.start()
    held[...] = jnp.zeros_like(held)
    held[0:2, : gains_ref.shape[1]] = gains_ref[...].astype(f32)
    held[2:5, : bias_ref.shape[1]] = bias_ref[...].astype(f32)
    held[5:7, :tokens] = routes_ref[...].astype(f32)
    width = router_ref.shape[1]
    for b in range(router_ref.shape[0] // 16):
        part = router_ref[16 * b : 16 * b + 16, :].astype(f32)
        held[16:32, width * b : width * (b + 1)] = part
    line_ref[tokens:, :] = held[...].astype(jnp.bfloat16)
    copy.wait()


def pack_kernel(count, core_ref, *refs):
    mats, out_ref, sems = refs[:count], refs[count + 1], refs[count + 2]
    half = mats[0].shape[0] // 2
    start = pl.multiple_of(core_ref[0] * half, half)
    copies = start_copies(
        [
            (m.at[pl.ds(start, half)], out_ref.at[pl.ds(k * half, half)])
            for k, m in enumerate(mats)
        ],
        sems,
    )
    for c in copies:
        c.wait()


def start_copies(pairs, sems):
    copies = [pltpu.make_async_copy(s, d, sems.at[i]) for i, (s, d) in enumerate(pairs)]
    for c in copies:
        c.start()
    return copies


def block_copies(shard, core, mats, near, far, outs):
    rows = mats[0].shape[0]
    half = rows // 2
    pairs = []
    for k, (mat, out) in enumerate(zip(mats, outs)):
        begin = pl.multiple_of(shard * rows, rows)
        pairs.append((mat, out.at[pl.ds(begin, rows)]))
        part = pl.ds(k * half, half)
        for r in range(1, 4):
            begin = lax.rem(shard + (4 - r), 4) * rows
            mine = pl.multiple_of(begin + core * half, half)
            other = pl.multiple_of(begin + (1 - core) * half, half)
            pairs.append((near[r - 1].at[part], out.at[pl.ds(mine, half)]))
            pairs.append((far[r - 1].at[part], out.at[pl.ds(other, half)]))
    return pairs


def whole_copies(shard, mat, near, out):
    rows = mat.shape[0]
    pairs = []
    for r, piece in enumerate([mat, *near]):
        begin = pl.multiple_of(lax.rem(shard + (4 - r), 4) * rows, rows)
        pairs.append((piece, out.at[pl.ds(begin, rows)]))
    return pairs


def norm_scale(x):
    return lax.rsqrt(jnp.mean(x * x, axis=1, keepdims=True) + epsilon)


def head_half(block, side):
    lanes = lax.broadcasted_iota(jnp.int32, block.shape, 1)
    keep = (lanes < 64) if side == 0 else (lanes >= 64)
    return jnp.where(keep, block, jnp.zeros_like(block))


def to_column(row):
    n = row.shape[1]
    down = lax.broadcasted_iota(jnp.int32, (n, n), 0)
    across = lax.broadcasted_iota(jnp.int32, (n, n), 1)
    return jnp.sum(jnp.where(down == across, row, jnp.zeros_like(row)), axis=1, keepdims=True)


def diagonal_sums(scores):
    n = scores.shape[0]
    down = lax.broadcasted_iota(jnp.int32, (n, n), 0)
    step = 1
    while step < n:
        turned = pltpu.roll(scores, n - step, axis=1)
        scores = jnp.where((down & step) != 0, turned, scores)
        step *= 2
    return jnp.sum(scores, axis=0, keepdims=True)


def bucket_marks():
    shape = (128, 128)
    distance = (128 - lax.broadcasted_iota(jnp.int32, shape, 0)) & 127
    bucket = jnp.zeros(shape, jnp.int32)
    for edge in bucket_edges:
        bucket = bucket + (distance >= edge).astype(jnp.int32)
    mark = bucket == lax.broadcasted_iota(jnp.int32, shape, 1)
    return mark.astype(jnp.float32).astype(jnp.bfloat16)


LAST = (((1,), (1,)), ((), ()))
FIRST = (((0,), (0,)), ((), ()))


def attend_kernel(place_ref, tokens_ref, gain_ref, bias_ref, *refs):
    f32, bf16 = jnp.float32, jnp.bfloat16
    mats, near, far = refs[:3], refs[3:6], refs[6:9]
    hidden_ref, q_ref, k_ref, v_ref, probs_ref, attended_ref = refs[9:15]
    held, sems = refs[15:]
    weights = [held.at[n] for n in range(3)]
    copies = start_copies(
        block_copies(place_ref[0], place_ref[1], mats, near, far, weights), sems
    )
    x = tokens_ref[...].astype(f32)
    hidden = (x * norm_scale(x) * gain_ref[...].astype(f32)).astype(bf16)
    hidden_ref[...] = hidden
    for n, (w, out) in enumerate(zip(weights, (q_ref, k_ref, v_ref))):
        for c in copies[7 * n : 7 * n + 7]:
            c.wait()
        out[...] = jnp.dot(hidden, w[...], preferred_element_type=f32).astype(bf16)
    heads = bias_ref.shape[0]
    for pair in range(heads // 2):
        lanes = slice(pair * 128, pair * 128 + 128)
        q, k, v = q_ref[:, lanes], k_ref[:, lanes], v_ref[:, lanes]
        total = jnp.zeros(q.shape, f32)
        for side in range(2):
            h = 2 * pair + side
            scores = lax.dot_general(q, head_half(k, side), LAST, preferred_element_type=f32)
            scores = scores * 0.125 + bias_ref[h]
            top = jnp.max(scores, axis=1, keepdims=True)
            grown = jnp.exp(scores - top)
            probs = grown / jnp.sum(grown, axis=1, keepdims=True)
            probs_ref[h] = probs
            total = total + jnp.dot(
                probs.astype(bf16), head_half(v, side), preferred_element_type=f32
            )
        attended_ref[:, lanes] = total.astype(bf16)


def middle_kernel(place_ref, tokens_ref, gain_ref, attended_ref, *refs):
    f32 = jnp.float32
    mat, near = refs[0], refs[1:4]
    middle_ref, moe_ref, weight, sems = refs[4:8]
    copies = start_copies(whole_copies(place_ref[0], mat, near, weight), sems)
    for c in copies:
        c.wait()
    middle = tokens_ref[...].astype(f32) + jnp.dot(
        attended_ref[...], weight[...], preferred_element_type=f32
    )
    middle_ref[...] = middle
    moe_ref[...] = (middle * norm_scale(middle) * gain_ref[...].astype(f32)).astype(jnp.bfloat16)


def backward_kernel(
    place_ref,
    tokens_ref,
    cotangent_ref,
    gain_one_ref,
    gain_two_ref,
    ids_ref,
    router_ref,
    middle_ref,
    moe_ref,
    attended_ref,
    hidden_ref,
    q_ref,
    k_ref,
    v_ref,
    probs_ref,
    spots_ref,
    rows_ref,
    *refs,
):
    f32, bf16 = jnp.float32, jnp.bfloat16
    homes, mats, near, far, near_out = refs[:4], refs[4:8], refs[8:11], refs[11:14], refs[14:17]
    result_ref, tokens_out, kept_ref, given_ref = refs[17:21]
    held, grads_ref, small_ref, sems = refs[21:]
    weights = [held.at[n] for n in range(4)]
    copies = start_copies(
        block_copies(place_ref[0], place_ref[1], mats[:3], near, far, weights[:3])
        + whole_copies(place_ref[0], mats[3], near_out, weights[3]),
        sems,
    )
    features = tokens_ref.shape[1]
    core = place_ref[1]
    width = features // 4
    small_ref[...] = jnp.zeros_like(small_ref)

    def leave(mat, left, right):
        grad = lax.dot_general(left, right, FIRST, preferred_element_type=f32).astype(bf16)
        grads_ref[...] = grad
        for x in range(4):
            low = grads_ref[x * 192 : x * 192 + 96, :]
            high = grads_ref[x * 192 + 96 : x * 192 + 192, :]
            at = (mat * 4 + x) * 96
            kept_ref[at : at + 96, :features] = jnp.where(core == 0, low, high)
            given_ref[at : at + 96, :features] = jnp.where(core == 0, high, low)

    def leave_wide(mats_rows, block):
        for x in range(4):
            for (mat, row), begin, size in zip(mats_rows, (0, 128), (128, 64)):
                at = (mat * 4 + x) * 96 + row
                small_ref[at : at + block.shape[0], :size] = block[
                    :, x * width + begin : x * width + begin + size
                ]

    home = homes[0][...].astype(f32)
    for piece in homes[1:]:
        home = home + piece[...].astype(f32)
    middle = middle_ref[...]
    result_ref[...] = (middle + home[:, :features]).astype(bf16)
    tail = home[:, features:]
    lane = lax.broadcasted_iota(jnp.int32, tail.shape, 1)
    grad_gates = [
        jnp.sum(jnp.where((lane == k) | (lane == 2 + k), tail, 0.0), axis=1, keepdims=True)
        for k in range(2)
    ]
    moe = moe_ref[...]
    logits = lax.dot_general(moe, router_ref[...], LAST, preferred_element_type=f32)
    ids = [to_column(ids_ref[k : k + 1, : tail.shape[0]]) for k in range(2)]
    gates = gate_pair(chosen_logit(logits, ids[0]), chosen_logit(logits, ids[1]))
    mix = gates[0] * grad_gates[0] + gates[1] * grad_gates[1]
    spots = lax.broadcasted_iota(jnp.int32, logits.shape, 1)
    grad_logits = jnp.zeros(logits.shape, f32)
    for k in range(2):
        grad_logits = jnp.where(spots == ids[k], gates[k] * (grad_gates[k] - mix), grad_logits)
    grad_logits = grad_logits.astype(bf16)
    slot = lax.broadcasted_iota(jnp.int32, (rows_ref.shape[0], tail.shape[0]), 0)
    pick = ((slot == spots_ref[0:1]) | (slot == spots_ref[1:2])).astype(f32).astype(bf16)
    grad_moe = lax.dot_general(pick, rows_ref[...], FIRST, preferred_element_type=f32)
    grad_moe = grad_moe + jnp.dot(grad_logits, router_ref[...], preferred_element_type=f32)
    leave_wide(
        ((0, 0), (1, 0)),
        lax.dot_general(grad_logits, moe, FIRST, preferred_element_type=f32),
    )
    scale = norm_scale(middle)
    normed = middle * scale
    leave_wide(((2, 2), (2, 3)), jnp.sum(grad_moe * normed, axis=0, keepdims=True))
    inner = grad_moe * gain_two_ref[...].astype(f32)
    grad_middle = cotangent_ref[...].astype(f32) + scale * (
        inner - normed * jnp.mean(inner * normed, axis=1, keepdims=True)
    )
    branch = grad_middle.astype(bf16)
    leave(3, attended_ref[...], branch)
    for c in copies[21:]:
        c.wait()
    grad_attended = lax.dot_general(branch, held[3], LAST, preferred_element_type=f32).astype(bf16)
    grad_q, grad_k, grad_v, diagonals = [], [], [], []
    for pair in range(probs_ref.shape[0] // 2):
        lanes = slice(pair * 128, pair * 128 + 128)
        q, k, v = q_ref[:, lanes], k_ref[:, lanes], v_ref[:, lanes]
        grad = grad_attended[:, lanes]
        parts = [jnp.zeros(q.shape, f32) for _ in range(3)]
        for side in range(2):
            h = 2 * pair + side
            probs = probs_ref[h]
            grad_half = head_half(grad, side)
            parts[2] = parts[2] + lax.dot_general(
                probs.astype(bf16), grad_half, FIRST, preferred_element_type=f32
            )
            grad_probs = lax.dot_general(grad_half, v, LAST, preferred_element_type=f32)
            grad_scores = (
                probs * (grad_probs - jnp.sum(probs * grad_probs, axis=1, keepdims=True))
            ).astype(bf16)
            diagonals.append(diagonal_sums(grad_scores.astype(f32)))
            parts[0] = parts[0] + jnp.dot(
                grad_scores, head_half(k, side), preferred_element_type=f32
            )
            parts[1] = parts[1] + lax.dot_general(
                grad_scores, head_half(q, side), FIRST, preferred_element_type=f32
            )
        grad_q.append((parts[0] * 0.125).astype(bf16))
        grad_k.append((parts[1] * 0.125).astype(bf16))
        grad_v.append(parts[2].astype(bf16))
    left = jnp.concatenate(diagonals, axis=0)
    grad_bias = jnp.zeros((left.shape[0], 128), f32)
    for _ in range(3):
        part = left.astype(bf16)
        left = left - part.astype(f32)
        grad_bias = grad_bias + jnp.dot(part, bucket_marks(), preferred_element_type=f32)
    per = left.shape[0] // 4
    for a in range(4):
        at = (8 + a) * 96 + 4
        small_ref[at : at + per, :] = grad_bias[a * per : a * per + per, :]
    hidden = hidden_ref[...]
    grad_hidden = jnp.zeros(hidden.shape, f32)
    for n, parts in enumerate((grad_q, grad_k, grad_v)):
        grad = jnp.concatenate(parts, axis=1)
        leave(n, hidden, grad)
        for c in copies[7 * n : 7 * n + 7]:
            c.wait()
        grad_hidden = grad_hidden + lax.dot_general(
            grad, held[n], LAST, preferred_element_type=f32
        )
    x = tokens_ref[...].astype(f32)
    scale = norm_scale(x)
    normed = x * scale
    leave_wide(((2, 0), (2, 1)), jnp.sum(grad_hidden * normed, axis=0, keepdims=True))
    inner = grad_hidden * gain_one_ref[...].astype(f32)
    tokens_out[...] = grad_middle + scale * (
        inner - normed * jnp.mean(inner * normed, axis=1, keepdims=True)
    )
    small = small_ref[...].astype(bf16)
    none = jnp.zeros_like(small)
    kept_ref[:, features:] = jnp.where(core == 0, small, none)
    given_ref[:, features:] = jnp.where(core == 0, none, small)


ANYWHERE = pl.BlockSpec(memory_space=pl.ANY)
SCALARS = pl.BlockSpec(memory_space=pltpu.SMEM)
WHOLE = pl.BlockSpec(memory_space=pltpu.VMEM)
ROOM = pltpu.CompilerParams(vmem_limit_bytes=56 * 1024 * 1024)


def make_line(routes, gains, bias, router, cotangent):
    tokens, cols = cotangent.shape
    return pl.pallas_call(
        line_kernel,
        out_shape=jax.ShapeDtypeStruct((tokens + 32, cols), jnp.bfloat16),
        in_specs=[WHOLE] * 4 + [ANYWHERE],
        out_specs=WHOLE,
        scratch_shapes=[pltpu.VMEM((32, cols), jnp.float32), pltpu.SemaphoreType.DMA],
        compiler_params=ROOM,
        name="line",
    )(routes, gains, bias, router, cotangent)


def pack(core, mats, after):
    rows, cols = mats[0].shape
    count = len(mats)
    return pl.pallas_call(
        functools.partial(pack_kernel, count),
        out_shape=jax.ShapeDtypeStruct((count * rows // 2, cols), jnp.bfloat16),
        in_specs=[SCALARS] + [ANYWHERE] * (count + 1),
        out_specs=WHOLE,
        scratch_shapes=[pltpu.SemaphoreType.DMA((count,))],
        compiler_params=ROOM,
        name="pack",
    )(core[None], *mats, after)


def hold_back_kernel(mat_ref, _, out_ref):
    out_ref[...] = mat_ref[...]


def hold_back(mat, after):
    return pl.pallas_call(
        hold_back_kernel,
        out_shape=jax.ShapeDtypeStruct(mat.shape, mat.dtype),
        in_specs=[WHOLE, ANYWHERE],
        out_specs=WHOLE,
        name="hold_back",
    )(mat, after)


def attend(where, tokens, gain, bias, mats, near, far):
    rows, cols = mats[0].shape
    state = jax.ShapeDtypeStruct(tokens.shape, jnp.bfloat16)
    return pl.pallas_call(
        attend_kernel,
        out_shape=[state] * 4 + [jax.ShapeDtypeStruct(bias.shape, jnp.float32), state],
        in_specs=[SCALARS] + [WHOLE] * 3 + [ANYWHERE] * 9,
        out_specs=[WHOLE] * 6,
        scratch_shapes=[
            pltpu.VMEM((3, 4 * rows, cols), jnp.bfloat16),
            pltpu.SemaphoreType.DMA((21,)),
        ],
        compiler_params=ROOM,
        cost_estimate=pl.CostEstimate(
            flops=80000000000, bytes_accessed=300000000, transcendentals=0
        ),
        name="attend",
    )(where, tokens, gain, bias, *mats, *near, *far)


def to_middle(where, tokens, gain, attended, mat, near):
    rows, cols = mat.shape
    return pl.pallas_call(
        middle_kernel,
        out_shape=[
            jax.ShapeDtypeStruct(tokens.shape, jnp.float32),
            jax.ShapeDtypeStruct(tokens.shape, jnp.bfloat16),
        ],
        in_specs=[SCALARS] + [WHOLE] * 3 + [ANYWHERE] * 4,
        out_specs=[WHOLE] * 2,
        scratch_shapes=[
            pltpu.VMEM((4 * rows, cols), jnp.bfloat16),
            pltpu.SemaphoreType.DMA((4,)),
        ],
        compiler_params=ROOM,
        name="middle",
    )(where, tokens, gain, attended, mat, *near)


def backward(where, *arrays):
    tokens = arrays[0]
    count, features = tokens.shape
    bf16, f32 = jnp.bfloat16, jnp.float32
    shape = jax.ShapeDtypeStruct
    return pl.pallas_call(
        backward_kernel,
        out_shape=[
            shape((count, features), bf16),
            shape((count, features), f32),
            shape((2 * features, features + 128), bf16),
            shape((2 * features, features + 128), bf16),
        ],
        in_specs=[SCALARS] + [WHOLE] * 20 + [ANYWHERE] * 13,
        out_specs=[WHOLE] * 4,
        scratch_shapes=[
            pltpu.VMEM((4, features, features), bf16),
            pltpu.VMEM((features, features), bf16),
            pltpu.VMEM((2 * features, 128), f32),
            pltpu.SemaphoreType.DMA((25,)),
        ],
        compiler_params=ROOM,
        name="backward",
    )(where, *arrays)


def finish_kernel(core_ref, own_ref, other_ref, *refs):
    mats, (router_out, gains_out, bias_out) = refs[:4], refs[4:]
    f32 = jnp.float32
    core = core_ref[0]
    half = own_ref.shape[0] // 4
    features = mats[0].shape[1]
    own, other = own_ref[...].astype(f32), other_ref[...].astype(f32)
    low, high = jnp.where(core == 0, own, other), jnp.where(core == 0, other, own)
    for k, out in enumerate(mats):
        here = slice(k * half, (k + 1) * half)
        out[:half, :] = low[here, :features]
        out[half:, :] = high[here, :features]
    small = low[:, features:]
    tall = router_out.shape[0]
    router_out[:, :128] = small[:tall, :]
    router_out[:, 128:] = small[half : half + tall, :64]
    for k in range(2):
        at = 2 * half + 2 * k
        gains_out[k : k + 1, :128] = small[at : at + 1, :]
        gains_out[k : k + 1, 128:] = small[at + 1 : at + 2, :64]
    at = 2 * half + 4
    bias_out[...] = small[at : at + bias_out.shape[0], : bias_out.shape[1]]


def finish(core, own, other, shard_rows, experts_all, bias_shape):
    features = own.shape[1] - 128
    shape = lambda *s: jax.ShapeDtypeStruct(s, jnp.float32)
    return pl.pallas_call(
        finish_kernel,
        out_shape=[shape(shard_rows, features)] * 4
        + [shape(experts_all, shard_rows), shape(2, shard_rows), shape(*bias_shape)],
        in_specs=[SCALARS] + [WHOLE] * 2,
        out_specs=[WHOLE] * 7,
        compiler_params=ROOM,
        name="finish",
    )(core, own, other)


def picks_of(places, e, rows):
    row = lax.broadcasted_iota(jnp.int32, (rows, places.shape[1]), 0) + e * rows
    return ((row == places[0:1]) | (row == places[1:2])).astype(jnp.float32).astype(jnp.bfloat16)


def dispatch_grads_kernel(capacity, place_ref, *refs):
    pieces, (out_ref, places_ref, ids_ref, spots_ref) = refs[:4], refs[5:9]
    gains_ref, bias_ref, router_ref = refs[9:]
    f32, bf16, i32 = jnp.float32, jnp.bfloat16, jnp.int32
    rows = out_ref.shape[0]
    tokens = spots_ref.shape[1]
    features = pieces[0].shape[1]
    experts_all = 2 * rows // (4 * capacity)
    expert = lax.broadcasted_iota(i32, (experts_all, tokens), 0)
    down = lax.broadcasted_iota(i32, (tokens, tokens), 0)
    across = lax.broadcasted_iota(i32, (tokens, tokens), 1)
    earlier = (down < across).astype(f32).astype(bf16)
    sums = []
    for r in range(4):
        both = pieces[r][tokens : tokens + 16, :tokens].astype(f32)
        ids = [both[5 + k : 6 + k].astype(i32) for k in range(2)]
        match = [expert == i for i in ids]
        named = (match[0] | match[1]).astype(f32).astype(bf16)
        counts = jnp.dot(named, earlier, preferred_element_type=f32)
        here = slice(r * tokens, (r + 1) * tokens)
        for k in range(2):
            slot = jnp.sum(jnp.where(match[k], counts, 0.0), axis=0, keepdims=True).astype(i32)
            owner, local = ids[k] >> 1, ids[k] & 1
            places_ref[k : k + 1, here] = (
                local * rows + owner * (4 * capacity) + r * capacity + slot
            )
            ids_ref[k : k + 1, here] = ids[k]
            if r == 0:
                spots_ref[k : k + 1, :] = owner * 16 + local * capacity + slot
        sums.append(to_column(both[5:6] + both[6:7]))
    sums = jnp.concatenate(sums, axis=0)
    lanes = lax.broadcasted_iota(i32, (4 * tokens, 128), 1)
    line = jnp.concatenate([p[:tokens, :] for p in pieces], axis=0)
    places = places_ref[...]
    extra = jnp.zeros((rows, 128), f32)
    for e in range(2):
        pick = picks_of(places, e, rows)
        out_ref[:, e * features : (e + 1) * features] = jnp.dot(
            pick, line, preferred_element_type=f32
        ).astype(bf16)
        column = jnp.where(lanes == e, sums, 0.0).astype(bf16)
        extra = extra + jnp.dot(pick, column, preferred_element_type=f32)
    out_ref[:, 2 * features :] = extra.astype(bf16)
    smalls = [p[tokens:, :].astype(f32) for p in pieces]
    width = features // 4
    heads = bias_ref.shape[0] // 4
    for a in range(4):
        at = (place_ref[0] - a) & 3
        small = jnp.zeros_like(smalls[0])
        for k in range(4):
            small = jnp.where(at == k, smalls[k], small)
        here = slice(a * width, (a + 1) * width)
        gains_ref[:, here] = small[0:2, :width]
        bias_ref[a * heads : (a + 1) * heads, :] = small[2 : 2 + heads, : bias_ref.shape[1]]
        for b in range(router_ref.shape[0] // 16):
            router_ref[16 * b : 16 * b + 16, here] = small[16:32, width * b : width * (b + 1)]


def dispatch_grads(where, pieces, rows, capacity, tokens, experts_all, bias_shape, after):
    features = pieces[0].shape[1]
    shape = jax.ShapeDtypeStruct
    return pl.pallas_call(
        functools.partial(dispatch_grads_kernel, capacity),
        out_shape=[
            shape((rows, 2 * features + 128), jnp.bfloat16),
            shape((2, 4 * tokens), jnp.int32),
            shape((2, 4 * tokens), jnp.int32),
            shape((2, tokens), jnp.int32),
            shape((2, features), jnp.float32),
            shape(bias_shape, jnp.float32),
            shape((experts_all, features), jnp.float32),
        ],
        in_specs=[SCALARS] + [WHOLE] * 4 + [ANYWHERE],
        out_specs=[WHOLE] * 7,
        compiler_params=ROOM,
        cost_estimate=pl.CostEstimate(
            flops=30000000000, bytes_accessed=100000000, transcendentals=0
        ),
        name="dispatch_grads",
    )(where, *pieces, after)


def dispatch_kernel(places_ref, *refs):
    pieces, out_ref = refs[:4], refs[5]
    rows = out_ref.shape[0]
    features = pieces[0].shape[1]
    line = jnp.concatenate([p[...] for p in pieces], axis=0)
    for e in range(2):
        out_ref[:, e * features : (e + 1) * features] = jnp.dot(
            picks_of(places_ref[...], e, rows), line, preferred_element_type=jnp.float32
        ).astype(jnp.bfloat16)


def dispatch(places, pieces, rows, after):
    return pl.pallas_call(
        dispatch_kernel,
        out_shape=jax.ShapeDtypeStruct((rows, 2 * pieces[0].shape[1]), jnp.bfloat16),
        in_specs=[WHOLE] * 5 + [ANYWHERE],
        out_specs=WHOLE,
        compiler_params=ROOM,
        name="dispatch",
    )(places, *pieces, after)


def chosen_logit(logits, ids):
    lanes = lax.broadcasted_iota(jnp.int32, logits.shape, 1)
    return jnp.sum(jnp.where(lanes == ids, logits, 0.0), axis=1, keepdims=True)


def gate_pair(first, second):
    top = jnp.maximum(first, second)
    one, two = jnp.exp(first - top), jnp.exp(second - top)
    total = one + two
    return one / total, two / total


def expert_kernel(x_ref, in_ref, out_ref, ret_ref, act_ref, rise_ref):
    f32, bf16 = jnp.float32, jnp.bfloat16
    slope = math.sqrt(2.0 / math.pi)
    pre = jnp.dot(x_ref[...], in_ref[0], preferred_element_type=f32)
    tanh = jnp.tanh(slope * (pre + 0.044715 * (pre * pre * pre)))
    active = (0.5 * pre * (1.0 + tanh)).astype(bf16)
    act_ref[0] = active
    ret_ref[...] = jnp.dot(active, out_ref[0], preferred_element_type=f32).astype(bf16)
    rise_ref[0] = 0.5 * (1.0 + tanh) + 0.5 * pre * (1.0 - tanh * tanh) * (
        slope * (1.0 + 3.0 * 0.044715 * (pre * pre))
    )


STEP = 256


def lanes_of(n):
    return pl.BlockSpec((STEP, n), lambda e, i: (i, e))


def rows_of(n):
    return pl.BlockSpec((1, STEP, n), lambda e, i: (e, i, 0))


def one_of(a, b):
    return pl.BlockSpec((1, a, b), lambda e, i: (e, 0, 0))


def experts(arrived, w_in, w_out):
    rows = arrived.shape[0]
    features, hidden = w_in.shape[1:]
    return pl.pallas_call(
        expert_kernel,
        grid=(2, rows // STEP),
        out_shape=[
            jax.ShapeDtypeStruct((rows, 2 * features), jnp.bfloat16),
            jax.ShapeDtypeStruct((2, rows, hidden), jnp.bfloat16),
            jax.ShapeDtypeStruct((2, rows, hidden), jnp.float32),
        ],
        in_specs=[lanes_of(features), one_of(features, hidden), one_of(hidden, features)],
        out_specs=[lanes_of(features), rows_of(hidden), rows_of(hidden)],
        compiler_params=ROOM,
        name="experts",
    )(arrived, w_in, w_out)


def expert_back_kernel(
    capacity, e, own_ref, x_ref, g_ref, ids_ref, in_ref, out_ref, router_ref, rise_ref, *refs
):
    pre_ref, arr_ref, outs, held = refs[0], refs[1], refs[2:6], refs[6]
    f32, bf16, i32 = jnp.float32, jnp.bfloat16, jnp.int32
    own = own_ref[0] + e
    rows = x_ref.shape[0]
    step = 256

    def chunk(i, carry):
        at = pl.ds(pl.multiple_of(i * step, step), step)
        ids = ids_ref[at, :].astype(f32)
        lanes = lax.broadcasted_iota(i32, ids.shape, 1)
        other = jnp.sum(jnp.where(lanes == e, ids, 0.0), axis=1, keepdims=True).astype(i32) - own
        logits = lax.dot_general(
            x_ref[at, :], router_ref[...], LAST, preferred_element_type=f32
        )
        gate, _ = gate_pair(chosen_logit(logits, own), chosen_logit(logits, other))
        grown = (gate * g_ref[at, :].astype(f32)).astype(bf16)
        arr_ref[at, :] = grown
        back = lax.dot_general(grown, out_ref[0], LAST, preferred_element_type=f32)
        grad = (back * rise_ref[0, at, :]).astype(bf16)
        pre_ref[at, :] = grad
        held[at, :] = lax.dot_general(grad, in_ref[0], LAST, preferred_element_type=f32).astype(
            bf16
        )
        return carry

    lax.fori_loop(0, rows // step, chunk, 0)
    part = rows // 4
    here = lax.broadcasted_iota(i32, (part, rows), 0)
    there = lax.broadcasted_iota(i32, (part, rows), 1)
    block = (here * (65536 // capacity + 1)) >> 16
    for r, out in enumerate(outs):
        source = here + block * (3 * capacity) + r * capacity
        pick = (there == source).astype(f32).astype(bf16)
        out[...] = jnp.dot(pick, held[...], preferred_element_type=f32).astype(bf16)


def experts_back(own, e, arrived, grad_wide, w_in, w_out, router_w, rise, capacity, flops):
    rows = arrived.shape[0]
    features, hidden = w_in.shape[1:]
    bf16 = jnp.bfloat16
    shape = jax.ShapeDtypeStruct
    part = rows // 4
    lanes = lambda n: pl.BlockSpec((rows, n), lambda i: (0, e))
    one = lambda a, b: pl.BlockSpec((1, a, b), lambda i: (e, 0, 0))
    whole = lambda a, b: pl.BlockSpec((a, b), lambda i: (0, 0))
    return pl.pallas_call(
        functools.partial(expert_back_kernel, capacity, e),
        grid=(1,),
        out_shape=[shape((rows, hidden), bf16), shape((rows, features), bf16)]
        + [shape((part, features), bf16)] * 4,
        in_specs=[
            SCALARS,
            lanes(features),
            lanes(features),
            pl.BlockSpec((rows, 128), lambda i: (0, 2 * features // 128)),
            one(features, hidden),
            one(hidden, features),
            whole(*router_w.shape),
            one(rows, hidden),
        ],
        out_specs=[whole(rows, hidden), whole(rows, features)] + [whole(part, features)] * 4,
        scratch_shapes=[pltpu.VMEM((rows, features), bf16)],
        compiler_params=ROOM,
        cost_estimate=pl.CostEstimate(
            flops=flops, bytes_accessed=10_000_000, transcendentals=0
        ),
        name="experts_back",
    )(own[None], arrived, grad_wide, grad_wide, w_in, w_out, router_w, rise)


def weight_grads_kernel(x_ref, act_ref, pre_a, pre_b, arr_a, arr_b, in_ref, out_ref):
    def make(pre_ref, arr_ref):
        in_ref[0] = lax.dot_general(
            x_ref[...], pre_ref[...], FIRST, preferred_element_type=jnp.float32
        )
        out_ref[0] = lax.dot_general(
            act_ref[0], arr_ref[...], FIRST, preferred_element_type=jnp.float32
        )

    pl.when(pl.program_id(0) == 0)(lambda: make(pre_a, arr_a))
    pl.when(pl.program_id(0) == 1)(lambda: make(pre_b, arr_b))


def weight_grads(arrived, active, grad_pre, grad_arrived):
    rows = arrived.shape[0]
    hidden, features = grad_pre[0].shape[1], grad_arrived[0].shape[1]
    step = 256
    cuts = features // step
    whole = lambda n: pl.BlockSpec((rows, n), lambda e, j: (0, 0))
    out = lambda n: pl.BlockSpec((1, step, n), lambda e, j: (e, j, 0))
    return pl.pallas_call(
        weight_grads_kernel,
        grid=(2, cuts),
        out_shape=[
            jax.ShapeDtypeStruct((2, features, hidden), jnp.float32),
            jax.ShapeDtypeStruct((2, hidden, features), jnp.float32),
        ],
        in_specs=[
            pl.BlockSpec((rows, step), lambda e, j: (0, e * cuts + j)),
            pl.BlockSpec((1, rows, step), lambda e, j: (e, 0, j)),
        ]
        + [whole(hidden)] * 2
        + [whole(features)] * 2,
        out_specs=[out(hidden), out(features)],
        compiler_params=ROOM,
        cost_estimate=pl.CostEstimate(
            flops=8 * rows * features * hidden, bytes_accessed=20_000_000, transcendentals=0
        ),
        name="weight_grads",
    )(arrived, active, *grad_pre, *grad_arrived)


def sum_rows_kernel(capacity, *refs):
    out_ref = refs[-1]
    f32, bf16, i32 = jnp.float32, jnp.bfloat16, jnp.int32
    totals = []
    for pieces in (refs[:4], refs[4:8]):
        total = pieces[0][...].astype(f32)
        for piece in pieces[1:]:
            total = total + piece[...].astype(f32)
        totals.append(total)
    total = jnp.concatenate(totals, axis=0)
    rows = out_ref.shape[0]
    part = total.shape[0] // 2
    here = lax.broadcasted_iota(i32, (rows, 2 * part), 0)
    there = lax.broadcasted_iota(i32, (rows, 2 * part), 1)
    owner, q = here >> 4, here & 15
    second = q >= capacity
    source = owner * capacity + jnp.where(second, part + q - capacity, q)
    pick = ((there == source) & (q < 2 * capacity)).astype(f32).astype(bf16)
    out_ref[...] = jnp.dot(pick, total.astype(bf16), preferred_element_type=f32).astype(bf16)


def sum_rows(pieces, capacity, after):
    rows, features = 2 * pieces[0].shape[0], pieces[0].shape[1]
    return pl.pallas_call(
        functools.partial(sum_rows_kernel, capacity),
        out_shape=jax.ShapeDtypeStruct((rows // (2 * capacity) * 16, features), jnp.bfloat16),
        in_specs=[WHOLE] * 8 + [ANYWHERE] * len(after),
        out_specs=WHOLE,
        compiler_params=ROOM,
        cost_estimate=pl.CostEstimate(
            flops=20000000000, bytes_accessed=60000000, transcendentals=0
        ),
        name="sum_rows",
    )(*pieces, *after)


def combine_kernel(places_ref, ids_ref, router_ref, ret_ref, *refs):
    f32, bf16 = jnp.float32, jnp.bfloat16
    grads, moes, outs = refs[:4], refs[4:8], refs[9:13]
    tokens, features = moes[0].shape
    rows = ret_ref.shape[0]
    row = lax.broadcasted_iota(jnp.int32, (rows, tokens), 0)
    tail_lane = lax.broadcasted_iota(jnp.int32, (tokens, 128), 1)
    for r in range(4):
        here = slice(r * tokens, (r + 1) * tokens)
        logits = lax.dot_general(
            moes[r][...], router_ref[...], LAST, preferred_element_type=f32
        )
        ids = [to_column(ids_ref[k : k + 1, here]) for k in range(2)]
        gates = gate_pair(chosen_logit(logits, ids[0]), chosen_logit(logits, ids[1]))
        total = jnp.zeros((tokens, features), f32)
        tail = jnp.zeros((tokens, 128), f32)
        grad = grads[r][:tokens, :].astype(f32)
        for k in range(2):
            got = jnp.zeros((tokens, features), f32)
            for e in range(2):
                pick = (row + e * rows == places_ref[k : k + 1, here]).astype(f32).astype(bf16)
                got = got + lax.dot_general(
                    pick,
                    ret_ref[:, e * features : (e + 1) * features],
                    FIRST,
                    preferred_element_type=f32,
                )
            total = total + gates[k] * got
            dots = jnp.sum(grad * got, axis=1, keepdims=True)
            high = dots.astype(bf16).astype(f32)
            tail = jnp.where(tail_lane == k, high, tail)
            tail = jnp.where(tail_lane == 2 + k, dots - high, tail)
        outs[r][:, :features] = total.astype(bf16)
        outs[r][:, features:] = tail.astype(bf16)


def combine(places, ids, router_w, returned, grads, moes, after):
    tokens, features = moes[0].shape
    return pl.pallas_call(
        combine_kernel,
        out_shape=[jax.ShapeDtypeStruct((tokens, features + 128), jnp.bfloat16)] * 4,
        in_specs=[WHOLE] * 12 + [ANYWHERE],
        out_specs=[WHOLE] * 4,
        compiler_params=ROOM,
        name="combine",
    )(places, ids, router_w, returned, *grads, *moes, after)


def layer(
    tokens,
    seq_lengths,
    routes,
    gain_attn,
    w_query,
    w_key,
    w_value,
    w_output,
    rel_bias,
    gain_moe,
    w_router,
    w_in,
    w_out,
    cotangent,
):
    row_count, features = tokens.shape
    shard_rows = w_query.shape[0]
    expert_count = w_router.shape[1]
    bucket_count = rel_bias.shape[1]
    head_count = 4 * rel_bias.shape[0]
    capacity = 3 * row_count // expert_count
    f32 = jnp.float32
    bf16 = jnp.bfloat16

    shard = lax.axis_index("x").astype(jnp.int32)
    core = lax.axis_index("c").astype(jnp.int32)
    where = jnp.stack([shard, core])
    owners = expert_count // 2
    slot_rows = owners * 4 * capacity

    line = make_line(
        routes.T, jnp.stack([gain_attn, gain_moe]), rel_bias, w_router.T, cotangent
    )
    line_grads = along_x(line)
    sent = pack(core, (w_query, w_key, w_value), line)
    near = along_x(sent)[1:]
    def to_owners(outgoing):
        return lax.all_to_all(outgoing, ("y", "z", "c"), 0, 0, tiled=True)

    outgoing_grads, places, ids, spots, gains, bias_table, router_f = dispatch_grads(
        where,
        line_grads,
        slot_rows,
        capacity,
        row_count,
        expert_count,
        (head_count, bucket_count),
        line,
    )
    gain_one, gain_two = gains[0:1], gains[1:2]
    bias_table, router_w = bias_table.astype(bf16), router_f.astype(bf16)
    grad_wide = to_owners(outgoing_grads)
    near_out = along_x(hold_back(w_output, outgoing_grads))[1:]
    first_expert = 2 * lax.axis_index(("y", "z", "c")).astype(jnp.int32)

    segments = row_segments(seq_lengths[0], row_count)
    distance, onehot = position_tables(row_count, bucket_count)
    allowed = (segments[:, None] == segments[None, :]) & (distance >= 0)
    position_bias = jnp.einsum("ijb,hb->hij", onehot, bias_table, preferred_element_type=f32)
    masked_bias = jnp.where(allowed[None], position_bias, -1000000000.0)
    far = [swap_core(piece) for piece in near]
    hidden_one, queries, key_rows, value_rows, probs, attended = attend(
        where,
        tokens,
        gain_one,
        masked_bias,
        (w_query, w_key, w_value),
        near,
        far,
    )
    middle, moe_in = to_middle(
        where, tokens, gain_two, attended, w_output, near_out
    )

    line_moe = along_x(moe_in)
    arrived = to_owners(dispatch(places, line_moe, slot_rows, grad_wide))
    ret, active, rise = experts(arrived, w_in, w_out)
    returned = to_owners(ret)
    grad_pre, grad_arrived, summed = [], [], []
    for e, flops in enumerate((3_000_000_000, 60_000_000_000)):
        pre, grown, *blocks = experts_back(
            first_expert, e, arrived, grad_wide, w_in, w_out, router_w, rise, capacity, flops
        )
        grad_pre.append(pre)
        grad_arrived.append(grown)
        summed += [blocks[0]] + [shift_x(blocks[r], -r) for r in range(1, 4)]
    grad_w_in, grad_w_out = weight_grads(arrived, active, grad_pre, grad_arrived)
    bundle = combine(places, ids, router_w, returned, line_grads, line_moe, grad_w_in)
    back_rows = to_owners(sum_rows(summed, capacity, (grad_w_out, bundle[0])))
    homes = [bundle[0]] + [shift_x(bundle[r], -r) for r in range(1, 4)]
    result, grad_tokens, kept, given = backward(
        where,
        tokens,
        cotangent,
        gain_one,
        gain_two,
        ids,
        router_w,
        middle,
        moe_in,
        attended,
        hidden_one,
        queries,
        key_rows,
        value_rows,
        probs,
        spots,
        back_rows,
        *homes,
        w_query,
        w_key,
        w_value,
        w_output,
        *near,
        *far,
        *near_out,
    )
    piece = shard_rows // 8
    wide = features + 128
    paired = (kept.astype(f32) + swap_core(given).astype(f32)).astype(bf16)
    spread = lax.all_to_all(paired, ("y", "x", "z"), 0, 0, tiled=True)
    mine = jnp.sum(spread.reshape(64, piece, wide).astype(f32), axis=0).astype(bf16)
    half = lax.all_to_all(
        jnp.broadcast_to(mine[None], (16, piece, wide)).reshape(16 * piece, wide),
        ("y", "z"),
        0,
        0,
        tiled=True,
    )
    *totals, router_total, gain_totals, bias_total = finish(
        core[None], half, swap_core(half), shard_rows, expert_count, rel_bias.shape
    )
    router_total = router_total.T
    gain_one_total, gain_two_total = gain_totals[0], gain_totals[1]
    return (
        result,
        grad_tokens,
        gain_one_total,
        totals[0],
        totals[1],
        totals[2],
        totals[3],
        bias_total,
        gain_two_total,
        router_total,
        grad_w_in,
        grad_w_out,
    )


def solution(mesh):
    cube = Mesh(mesh.devices.reshape(4, 4, 2, 4), ("y", "z", "c", "x"))
    expert = ("y", "z", "c")
    everyone = ("y", "z", "c", "x")
    placed = (
        P(everyone, None),
        P(everyone, None),
        P(everyone, None),
        P("x"),
        P("x", None),
        P("x", None),
        P("x", None),
        P("x", None),
        P("x", None),
        P("x"),
        P("x", None),
        P(expert, None, "x"),
        P(expert, "x", None),
        P(everyone, None),
    )
    return jax.shard_map(
        layer,
        mesh=cube,
        in_specs=placed,
        out_specs=(
            P(everyone, None),
            P(everyone, None),
            P("x"),
            P("x", None),
            P("x", None),
            P("x", None),
            P("x", None),
            P("x", None),
            P("x"),
            P("x", None),
            P(expert, None, "x"),
            P(expert, "x", None),
        ),
        check_vma=False,
    )
```

```python
import functools
import math

import jax
import jax.numpy as jnp
from jax import lax
from jax.experimental import pallas as pl
from jax.experimental.pallas import tpu as pltpu
from jax.sharding import Mesh, PartitionSpec as P

epsilon = 1e-06
bucket_edges = list(range(1, 17)) + [
    int(math.ceil(16.0 * 8.0 ** ((bucket_level - 16) / 16.0))) for bucket_level in range(17, 32)
]


def row_segments(lengths, row_count):
    sequence_ends = jnp.cumsum(lengths)
    positions = jnp.arange(row_count, dtype=jnp.int32)
    return jnp.sum((positions[:, None] >= sequence_ends[None, :]).astype(jnp.int32), axis=1)


def position_tables(row_count, bucket_count):
    positions = jnp.arange(row_count, dtype=jnp.int32)
    distance = positions[:, None] - positions[None, :]
    edge_values = jnp.array(bucket_edges, dtype=jnp.int32)
    bucket = jnp.sum((distance[:, :, None] >= edge_values).astype(jnp.int32), axis=2)
    onehot = (bucket[:, :, None] == jnp.arange(bucket_count, dtype=jnp.int32)).astype(jnp.bfloat16)
    return (distance, onehot)


def shift(block, axis, step):
    ranks = lax.axis_size(axis)
    return lax.ppermute(block, axis, [(i, (i + step) % ranks) for i in range(ranks)])


def shift_x(block, step):
    return shift(block, "x", step)


def swap_core(block):
    return lax.ppermute(block, "c", [(0, 1), (1, 0)])


def along_x(block):
    return [block, shift_x(block, 1), shift_x(block, 2), shift_x(block, 3)]


def line_kernel(routes_ref, gains_ref, bias_ref, router_ref, cotangent_ref, line_ref, held, sem):
    f32 = jnp.float32
    tokens = cotangent_ref.shape[0]
    copy = pltpu.make_async_copy(cotangent_ref, line_ref.at[pl.ds(0, tokens)], sem)
    copy.start()
    held[...] = jnp.zeros_like(held)
    held[0:2, : gains_ref.shape[1]] = gains_ref[...].astype(f32)
    held[2:5, : bias_ref.shape[1]] = bias_ref[...].astype(f32)
    held[5:7, :tokens] = routes_ref[...].astype(f32)
    width = router_ref.shape[1]
    for b in range(router_ref.shape[0] // 16):
        part = router_ref[16 * b : 16 * b + 16, :].astype(f32)
        held[16:32, width * b : width * (b + 1)] = part
    line_ref[tokens:, :] = held[...].astype(jnp.bfloat16)
    copy.wait()


def pack_kernel(count, core_ref, *refs):
    mats, out_ref, sems = refs[:count], refs[count + 1], refs[count + 2]
    half = mats[0].shape[0] // 2
    start = pl.multiple_of(core_ref[0] * half, half)
    copies = start_copies(
        [
            (m.at[pl.ds(start, half)], out_ref.at[pl.ds(k * half, half)])
            for k, m in enumerate(mats)
        ],
        sems,
    )
    for c in copies:
        c.wait()


def start_copies(pairs, sems):
    copies = [pltpu.make_async_copy(s, d, sems.at[i]) for i, (s, d) in enumerate(pairs)]
    for c in copies:
        c.start()
    return copies


def block_copies(shard, core, mats, near, far, outs):
    rows = mats[0].shape[0]
    half = rows // 2
    pairs = []
    for k, (mat, out) in enumerate(zip(mats, outs)):
        begin = pl.multiple_of(shard * rows, rows)
        pairs.append((mat, out.at[pl.ds(begin, rows)]))
        part = pl.ds(k * half, half)
        for r in range(1, 4):
            begin = lax.rem(shard + (4 - r), 4) * rows
            mine = pl.multiple_of(begin + core * half, half)
            other = pl.multiple_of(begin + (1 - core) * half, half)
            pairs.append((near[r - 1].at[part], out.at[pl.ds(mine, half)]))
            pairs.append((far[r - 1].at[part], out.at[pl.ds(other, half)]))
    return pairs


def whole_copies(shard, mat, near, out):
    rows = mat.shape[0]
    pairs = []
    for r, piece in enumerate([mat, *near]):
        begin = pl.multiple_of(lax.rem(shard + (4 - r), 4) * rows, rows)
        pairs.append((piece, out.at[pl.ds(begin, rows)]))
    return pairs


def norm_scale(x):
    return lax.rsqrt(jnp.mean(x * x, axis=1, keepdims=True) + epsilon)


def head_half(block, side):
    lanes = lax.broadcasted_iota(jnp.int32, block.shape, 1)
    keep = (lanes < 64) if side == 0 else (lanes >= 64)
    return jnp.where(keep, block, jnp.zeros_like(block))


def to_column(row):
    n = row.shape[1]
    down = lax.broadcasted_iota(jnp.int32, (n, n), 0)
    across = lax.broadcasted_iota(jnp.int32, (n, n), 1)
    return jnp.sum(jnp.where(down == across, row, jnp.zeros_like(row)), axis=1, keepdims=True)


def diagonal_sums(scores):
    n = scores.shape[0]
    down = lax.broadcasted_iota(jnp.int32, (n, n), 0)
    step = 1
    while step < n:
        turned = pltpu.roll(scores, n - step, axis=1)
        scores = jnp.where((down & step) != 0, turned, scores)
        step *= 2
    return jnp.sum(scores, axis=0, keepdims=True)


def bucket_marks():
    shape = (128, 128)
    distance = (128 - lax.broadcasted_iota(jnp.int32, shape, 0)) & 127
    bucket = jnp.zeros(shape, jnp.int32)
    for edge in bucket_edges:
        bucket = bucket + (distance >= edge).astype(jnp.int32)
    mark = bucket == lax.broadcasted_iota(jnp.int32, shape, 1)
    return mark.astype(jnp.float32).astype(jnp.bfloat16)


LAST = (((1,), (1,)), ((), ()))
FIRST = (((0,), (0,)), ((), ()))


def attend_kernel(place_ref, tokens_ref, gain_ref, bias_ref, *refs):
    f32, bf16 = jnp.float32, jnp.bfloat16
    mats, near, far = refs[:3], refs[3:6], refs[6:9]
    hidden_ref, q_ref, k_ref, v_ref, probs_ref, attended_ref = refs[9:15]
    weights, sems = refs[15:18], refs[18]
    copies = start_copies(
        block_copies(place_ref[0], place_ref[1], mats, near, far, weights), sems
    )
    x = tokens_ref[...].astype(f32)
    hidden = (x * norm_scale(x) * gain_ref[...].astype(f32)).astype(bf16)
    hidden_ref[...] = hidden
    for n, (w, out) in enumerate(zip(weights, (q_ref, k_ref, v_ref))):
        for c in copies[7 * n : 7 * n + 7]:
            c.wait()
        out[...] = jnp.dot(hidden, w[...], preferred_element_type=f32).astype(bf16)
    heads = bias_ref.shape[0]
    for pair in range(heads // 2):
        lanes = slice(pair * 128, pair * 128 + 128)
        q, k, v = q_ref[:, lanes], k_ref[:, lanes], v_ref[:, lanes]
        total = jnp.zeros(q.shape, f32)
        for side in range(2):
            h = 2 * pair + side
            scores = lax.dot_general(q, head_half(k, side), LAST, preferred_element_type=f32)
            scores = scores * 0.125 + bias_ref[h]
            top = jnp.max(scores, axis=1, keepdims=True)
            grown = jnp.exp(scores - top)
            probs = grown / jnp.sum(grown, axis=1, keepdims=True)
            probs_ref[h] = probs
            total = total + jnp.dot(
                probs.astype(bf16), head_half(v, side), preferred_element_type=f32
            )
        attended_ref[:, lanes] = total.astype(bf16)


def middle_kernel(place_ref, tokens_ref, gain_ref, attended_ref, *refs):
    f32 = jnp.float32
    mat, near = refs[0], refs[1:4]
    middle_ref, moe_ref, weight, sems = refs[4:8]
    copies = start_copies(whole_copies(place_ref[0], mat, near, weight), sems)
    for c in copies:
        c.wait()
    middle = tokens_ref[...].astype(f32) + jnp.dot(
        attended_ref[...], weight[...], preferred_element_type=f32
    )
    middle_ref[...] = middle
    moe_ref[...] = (middle * norm_scale(middle) * gain_ref[...].astype(f32)).astype(jnp.bfloat16)


def backward_kernel(
    place_ref,
    tokens_ref,
    cotangent_ref,
    gain_one_ref,
    gain_two_ref,
    ids_ref,
    router_ref,
    middle_ref,
    moe_ref,
    attended_ref,
    hidden_ref,
    q_ref,
    k_ref,
    v_ref,
    probs_ref,
    spots_ref,
    rows_ref,
    *refs,
):
    f32, bf16 = jnp.float32, jnp.bfloat16
    homes, mats = refs[:4], refs[4:8]
    result_ref, tokens_out, kept_ref, given_ref = refs[8:12]
    held, grads_ref, small_ref, sems = refs[12:]
    copies = start_copies([(m, held.at[n]) for n, m in enumerate(mats)], sems)
    features = tokens_ref.shape[1]
    core = place_ref[1]
    width = features // 4
    small_ref[...] = jnp.zeros_like(small_ref)

    def leave(mat, left, right):
        grad = lax.dot_general(left, right, FIRST, preferred_element_type=f32).astype(bf16)
        grads_ref[...] = grad
        for x in range(4):
            low = grads_ref[x * 192 : x * 192 + 96, :]
            high = grads_ref[x * 192 + 96 : x * 192 + 192, :]
            at = (mat * 4 + x) * 96
            kept_ref[at : at + 96, :features] = jnp.where(core == 0, low, high)
            given_ref[at : at + 96, :features] = jnp.where(core == 0, high, low)

    def leave_wide(mats_rows, block):
        for x in range(4):
            for (mat, row), begin, size in zip(mats_rows, (0, 128), (128, 64)):
                at = (mat * 4 + x) * 96 + row
                small_ref[at : at + block.shape[0], :size] = block[
                    :, x * width + begin : x * width + begin + size
                ]

    home = homes[0][...].astype(f32)
    for piece in homes[1:]:
        home = home + piece[...].astype(f32)
    middle = middle_ref[...]
    result_ref[...] = (middle + home[:, :features]).astype(bf16)
    tail = home[:, features:]
    lane = lax.broadcasted_iota(jnp.int32, tail.shape, 1)
    grad_gates = [
        jnp.sum(jnp.where((lane == k) | (lane == 2 + k), tail, 0.0), axis=1, keepdims=True)
        for k in range(2)
    ]
    moe = moe_ref[...]
    logits = lax.dot_general(moe, router_ref[...], LAST, preferred_element_type=f32)
    ids = [to_column(ids_ref[k : k + 1, : tail.shape[0]]) for k in range(2)]
    gates = gate_pair(chosen_logit(logits, ids[0]), chosen_logit(logits, ids[1]))
    mix = gates[0] * grad_gates[0] + gates[1] * grad_gates[1]
    spots = lax.broadcasted_iota(jnp.int32, logits.shape, 1)
    grad_logits = jnp.zeros(logits.shape, f32)
    for k in range(2):
        grad_logits = jnp.where(spots == ids[k], gates[k] * (grad_gates[k] - mix), grad_logits)
    grad_logits = grad_logits.astype(bf16)
    slot = lax.broadcasted_iota(jnp.int32, (rows_ref.shape[0], tail.shape[0]), 0)
    pick = ((slot == spots_ref[0:1]) | (slot == spots_ref[1:2])).astype(f32).astype(bf16)
    grad_moe = lax.dot_general(pick, rows_ref[...], FIRST, preferred_element_type=f32)
    grad_moe = grad_moe + jnp.dot(grad_logits, router_ref[...], preferred_element_type=f32)
    leave_wide(
        ((0, 0), (1, 0)),
        lax.dot_general(grad_logits, moe, FIRST, preferred_element_type=f32),
    )
    scale = norm_scale(middle)
    normed = middle * scale
    leave_wide(((2, 2), (2, 3)), jnp.sum(grad_moe * normed, axis=0, keepdims=True))
    inner = grad_moe * gain_two_ref[...].astype(f32)
    grad_middle = cotangent_ref[...].astype(f32) + scale * (
        inner - normed * jnp.mean(inner * normed, axis=1, keepdims=True)
    )
    branch = grad_middle.astype(bf16)
    leave(3, attended_ref[...], branch)
    copies[3].wait()
    grad_attended = lax.dot_general(branch, held[3], LAST, preferred_element_type=f32).astype(bf16)
    grad_q, grad_k, grad_v, diagonals = [], [], [], []
    for pair in range(probs_ref.shape[0] // 2):
        lanes = slice(pair * 128, pair * 128 + 128)
        q, k, v = q_ref[:, lanes], k_ref[:, lanes], v_ref[:, lanes]
        grad = grad_attended[:, lanes]
        parts = [jnp.zeros(q.shape, f32) for _ in range(3)]
        for side in range(2):
            h = 2 * pair + side
            probs = probs_ref[h]
            grad_half = head_half(grad, side)
            parts[2] = parts[2] + lax.dot_general(
                probs.astype(bf16), grad_half, FIRST, preferred_element_type=f32
            )
            grad_probs = lax.dot_general(grad_half, v, LAST, preferred_element_type=f32)
            grad_scores = (
                probs * (grad_probs - jnp.sum(probs * grad_probs, axis=1, keepdims=True))
            ).astype(bf16)
            diagonals.append(diagonal_sums(grad_scores.astype(f32)))
            parts[0] = parts[0] + jnp.dot(
                grad_scores, head_half(k, side), preferred_element_type=f32
            )
            parts[1] = parts[1] + lax.dot_general(
                grad_scores, head_half(q, side), FIRST, preferred_element_type=f32
            )
        grad_q.append((parts[0] * 0.125).astype(bf16))
        grad_k.append((parts[1] * 0.125).astype(bf16))
        grad_v.append(parts[2].astype(bf16))
    left = jnp.concatenate(diagonals, axis=0)
    grad_bias = jnp.zeros((left.shape[0], 128), f32)
    for _ in range(3):
        part = left.astype(bf16)
        left = left - part.astype(f32)
        grad_bias = grad_bias + jnp.dot(part, bucket_marks(), preferred_element_type=f32)
    per = left.shape[0] // 4
    for a in range(4):
        at = (8 + a) * 96 + 4
        small_ref[at : at + per, :] = grad_bias[a * per : a * per + per, :]
    hidden = hidden_ref[...]
    grad_hidden = jnp.zeros(hidden.shape, f32)
    for n, parts in enumerate((grad_q, grad_k, grad_v)):
        grad = jnp.concatenate(parts, axis=1)
        leave(n, hidden, grad)
        copies[n].wait()
        grad_hidden = grad_hidden + lax.dot_general(
            grad, held[n], LAST, preferred_element_type=f32
        )
    x = tokens_ref[...].astype(f32)
    scale = norm_scale(x)
    normed = x * scale
    leave_wide(((2, 0), (2, 1)), jnp.sum(grad_hidden * normed, axis=0, keepdims=True))
    inner = grad_hidden * gain_one_ref[...].astype(f32)
    tokens_out[...] = grad_middle + scale * (
        inner - normed * jnp.mean(inner * normed, axis=1, keepdims=True)
    )
    small = small_ref[...].astype(bf16)
    none = jnp.zeros_like(small)
    kept_ref[:, features:] = jnp.where(core == 0, small, none)
    given_ref[:, features:] = jnp.where(core == 0, none, small)


ANYWHERE = pl.BlockSpec(memory_space=pl.ANY)
UNREAD = pl.BlockSpec(memory_space=pltpu.HBM)
SCALARS = pl.BlockSpec(memory_space=pltpu.SMEM)
WHOLE = pl.BlockSpec(memory_space=pltpu.VMEM)
ROOM = pltpu.CompilerParams(vmem_limit_bytes=38 * 1024 * 1024)
SOME = pltpu.CompilerParams(vmem_limit_bytes=20 * 1024 * 1024)


def make_line(routes, gains, bias, router, cotangent):
    tokens, cols = cotangent.shape
    return pl.pallas_call(
        line_kernel,
        out_shape=jax.ShapeDtypeStruct((tokens + 32, cols), jnp.bfloat16),
        in_specs=[WHOLE] * 4 + [ANYWHERE],
        out_specs=WHOLE,
        scratch_shapes=[pltpu.VMEM((32, cols), jnp.float32), pltpu.SemaphoreType.DMA],
        compiler_params=SOME,
        name="line",
    )(routes, gains, bias, router, cotangent)


def pack(core, mats, after):
    rows, cols = mats[0].shape
    count = len(mats)
    return pl.pallas_call(
        functools.partial(pack_kernel, count),
        out_shape=jax.ShapeDtypeStruct((count * rows // 2, cols), jnp.bfloat16),
        in_specs=[SCALARS] + [ANYWHERE] * (count + 1),
        out_specs=WHOLE,
        scratch_shapes=[pltpu.SemaphoreType.DMA((count,))],
        compiler_params=SOME,
        name="pack",
    )(core[None], *mats, after)


def hold_back_kernel(mat_ref, _, out_ref):
    out_ref[...] = mat_ref[...]


def hold_back(mat, after):
    return pl.pallas_call(
        hold_back_kernel,
        out_shape=jax.ShapeDtypeStruct(mat.shape, mat.dtype),
        in_specs=[WHOLE, ANYWHERE],
        out_specs=WHOLE,
        name="hold_back",
    )(mat, after)


def attend(where, tokens, gain, bias, mats, near, far):
    rows, cols = mats[0].shape
    state = jax.ShapeDtypeStruct(tokens.shape, jnp.bfloat16)
    full = jax.ShapeDtypeStruct((4 * rows, cols), jnp.bfloat16)
    return pl.pallas_call(
        attend_kernel,
        out_shape=[state] * 4
        + [jax.ShapeDtypeStruct(bias.shape, jnp.float32), state]
        + [full] * 3,
        in_specs=[SCALARS] + [WHOLE] * 3 + [ANYWHERE] * 9,
        out_specs=[WHOLE] * 9,
        scratch_shapes=[pltpu.SemaphoreType.DMA((21,))],
        compiler_params=SOME,
        cost_estimate=pl.CostEstimate(
            flops=80000000000, bytes_accessed=300000000, transcendentals=0
        ),
        name="attend",
    )(where, tokens, gain, bias, *mats, *near, *far)


def to_middle(where, tokens, gain, attended, mat, near):
    rows, cols = mat.shape
    return pl.pallas_call(
        middle_kernel,
        out_shape=[
            jax.ShapeDtypeStruct(tokens.shape, jnp.float32),
            jax.ShapeDtypeStruct(tokens.shape, jnp.bfloat16),
            jax.ShapeDtypeStruct((4 * rows, cols), jnp.bfloat16),
        ],
        in_specs=[SCALARS] + [WHOLE] * 3 + [ANYWHERE] * 4,
        out_specs=[WHOLE] * 3,
        scratch_shapes=[pltpu.SemaphoreType.DMA((4,))],
        compiler_params=SOME,
        name="middle",
    )(where, tokens, gain, attended, mat, *near)


def backward(where, *arrays):
    tokens = arrays[0]
    count, features = tokens.shape
    bf16, f32 = jnp.bfloat16, jnp.float32
    shape = jax.ShapeDtypeStruct
    return pl.pallas_call(
        backward_kernel,
        out_shape=[
            shape((count, features), bf16),
            shape((count, features), f32),
            shape((2 * features, features + 128), bf16),
            shape((2 * features, features + 128), bf16),
        ],
        in_specs=[SCALARS] + [WHOLE] * 20 + [ANYWHERE] * 4,
        out_specs=[WHOLE] * 4,
        scratch_shapes=[
            pltpu.VMEM((4, features, features), bf16),
            pltpu.VMEM((features, features), bf16),
            pltpu.VMEM((2 * features, 128), f32),
            pltpu.SemaphoreType.DMA((4,)),
        ],
        compiler_params=ROOM,
        name="backward",
    )(where, *arrays)


def finish_kernel(core_ref, own_ref, other_ref, *refs):
    mats, (router_out, gains_out, bias_out) = refs[:4], refs[4:]
    f32 = jnp.float32
    core = core_ref[0]
    half = own_ref.shape[0] // 4
    features = mats[0].shape[1]
    own, other = own_ref[...].astype(f32), other_ref[...].astype(f32)
    low, high = jnp.where(core == 0, own, other), jnp.where(core == 0, other, own)
    for k, out in enumerate(mats):
        here = slice(k * half, (k + 1) * half)
        out[:half, :] = low[here, :features]
        out[half:, :] = high[here, :features]
    small = low[:, features:]
    tall = router_out.shape[0]
    router_out[:, :128] = small[:tall, :]
    router_out[:, 128:] = small[half : half + tall, :64]
    for k in range(2):
        at = 2 * half + 2 * k
        gains_out[k : k + 1, :128] = small[at : at + 1, :]
        gains_out[k : k + 1, 128:] = small[at + 1 : at + 2, :64]
    at = 2 * half + 4
    bias_out[...] = small[at : at + bias_out.shape[0], : bias_out.shape[1]]


def finish(core, own, other, shard_rows, experts_all, bias_shape):
    features = own.shape[1] - 128
    shape = lambda *s: jax.ShapeDtypeStruct(s, jnp.float32)
    return pl.pallas_call(
        finish_kernel,
        out_shape=[shape(shard_rows, features)] * 4
        + [shape(experts_all, shard_rows), shape(2, shard_rows), shape(*bias_shape)],
        in_specs=[SCALARS] + [WHOLE] * 2,
        out_specs=[WHOLE] * 7,
        compiler_params=SOME,
        name="finish",
    )(core, own, other)


def picks_of(places, e, rows):
    row = lax.broadcasted_iota(jnp.int32, (rows, places.shape[1]), 0) + e * rows
    return ((row == places[0:1]) | (row == places[1:2])).astype(jnp.float32).astype(jnp.bfloat16)


def dispatch_grads_kernel(capacity, place_ref, *refs):
    pieces, (out_ref, places_ref, ids_ref, spots_ref) = refs[:4], refs[5:9]
    gains_ref, bias_ref, router_ref = refs[9:]
    f32, bf16, i32 = jnp.float32, jnp.bfloat16, jnp.int32
    rows = out_ref.shape[0]
    tokens = spots_ref.shape[1]
    features = pieces[0].shape[1]
    experts_all = 2 * rows // (4 * capacity)
    expert = lax.broadcasted_iota(i32, (experts_all, tokens), 0)
    down = lax.broadcasted_iota(i32, (tokens, tokens), 0)
    across = lax.broadcasted_iota(i32, (tokens, tokens), 1)
    earlier = (down < across).astype(f32).astype(bf16)
    sums = []
    for r in range(4):
        both = pieces[r][tokens : tokens + 16, :tokens].astype(f32)
        ids = [both[5 + k : 6 + k].astype(i32) for k in range(2)]
        match = [expert == i for i in ids]
        named = (match[0] | match[1]).astype(f32).astype(bf16)
        counts = jnp.dot(named, earlier, preferred_element_type=f32)
        here = slice(r * tokens, (r + 1) * tokens)
        for k in range(2):
            slot = jnp.sum(jnp.where(match[k], counts, 0.0), axis=0, keepdims=True).astype(i32)
            owner, local = ids[k] >> 1, ids[k] & 1
            places_ref[k : k + 1, here] = (
                local * rows + owner * (4 * capacity) + r * capacity + slot
            )
            ids_ref[k : k + 1, here] = ids[k]
            if r == 0:
                spots_ref[k : k + 1, :] = owner * 16 + local * capacity + slot
        sums.append(to_column(both[5:6] + both[6:7]))
    sums = jnp.concatenate(sums, axis=0)
    lanes = lax.broadcasted_iota(i32, (4 * tokens, 128), 1)
    line = jnp.concatenate([p[:tokens, :] for p in pieces], axis=0)
    places = places_ref[...]
    extra = jnp.zeros((rows, 128), f32)
    for e in range(2):
        pick = picks_of(places, e, rows)
        out_ref[:, e * features : (e + 1) * features] = jnp.dot(
            pick, line, preferred_element_type=f32
        ).astype(bf16)
        column = jnp.where(lanes == e, sums, 0.0).astype(bf16)
        extra = extra + jnp.dot(pick, column, preferred_element_type=f32)
    out_ref[:, 2 * features :] = extra.astype(bf16)
    smalls = [p[tokens:, :].astype(f32) for p in pieces]
    width = features // 4
    heads = bias_ref.shape[0] // 4
    for a in range(4):
        at = (place_ref[0] - a) & 3
        small = jnp.zeros_like(smalls[0])
        for k in range(4):
            small = jnp.where(at == k, smalls[k], small)
        here = slice(a * width, (a + 1) * width)
        gains_ref[:, here] = small[0:2, :width]
        bias_ref[a * heads : (a + 1) * heads, :] = small[2 : 2 + heads, : bias_ref.shape[1]]
        for b in range(router_ref.shape[0] // 16):
            router_ref[16 * b : 16 * b + 16, here] = small[16:32, width * b : width * (b + 1)]


def dispatch_grads(where, pieces, rows, capacity, tokens, experts_all, bias_shape, after):
    features = pieces[0].shape[1]
    shape = jax.ShapeDtypeStruct
    return pl.pallas_call(
        functools.partial(dispatch_grads_kernel, capacity),
        out_shape=[
            shape((rows, 2 * features + 128), jnp.bfloat16),
            shape((2, 4 * tokens), jnp.int32),
            shape((2, 4 * tokens), jnp.int32),
            shape((2, tokens), jnp.int32),
            shape((2, features), jnp.float32),
            shape(bias_shape, jnp.float32),
            shape((experts_all, features), jnp.float32),
        ],
        in_specs=[SCALARS] + [WHOLE] * 4 + [ANYWHERE],
        out_specs=[WHOLE] * 7,
        compiler_params=SOME,
        cost_estimate=pl.CostEstimate(
            flops=30000000000, bytes_accessed=100000000, transcendentals=0
        ),
        name="dispatch_grads",
    )(where, *pieces, after)


def dispatch_kernel(places_ref, *refs):
    pieces, out_ref = refs[:4], refs[5]
    rows = out_ref.shape[0]
    features = pieces[0].shape[1]
    line = jnp.concatenate([p[...] for p in pieces], axis=0)
    for e in range(2):
        out_ref[:, e * features : (e + 1) * features] = jnp.dot(
            picks_of(places_ref[...], e, rows), line, preferred_element_type=jnp.float32
        ).astype(jnp.bfloat16)


def dispatch(places, pieces, rows, after):
    return pl.pallas_call(
        dispatch_kernel,
        out_shape=jax.ShapeDtypeStruct((rows, 2 * pieces[0].shape[1]), jnp.bfloat16),
        in_specs=[WHOLE] * 5 + [UNREAD],
        out_specs=WHOLE,
        compiler_params=SOME,
        name="dispatch",
    )(places, *pieces, after)


def chosen_logit(logits, ids):
    lanes = lax.broadcasted_iota(jnp.int32, logits.shape, 1)
    return jnp.sum(jnp.where(lanes == ids, logits, 0.0), axis=1, keepdims=True)


def gate_pair(first, second):
    top = jnp.maximum(first, second)
    one, two = jnp.exp(first - top), jnp.exp(second - top)
    total = one + two
    return one / total, two / total


def expert_kernel(x_ref, in_ref, out_ref, ret_ref, act_ref, rise_ref):
    f32, bf16 = jnp.float32, jnp.bfloat16
    slope = math.sqrt(2.0 / math.pi)
    pre = jnp.dot(x_ref[...], in_ref[0], preferred_element_type=f32)
    tanh = jnp.tanh(slope * (pre + 0.044715 * (pre * pre * pre)))
    active = (0.5 * pre * (1.0 + tanh)).astype(bf16)
    act_ref[0] = active
    ret_ref[...] = jnp.dot(active, out_ref[0], preferred_element_type=f32).astype(bf16)
    rise_ref[0] = 0.5 * (1.0 + tanh) + 0.5 * pre * (1.0 - tanh * tanh) * (
        slope * (1.0 + 3.0 * 0.044715 * (pre * pre))
    )


STEP = 256


def lanes_of(n):
    return pl.BlockSpec((STEP, n), lambda e, i: (i, e))


def rows_of(n):
    return pl.BlockSpec((1, STEP, n), lambda e, i: (e, i, 0))


def one_of(a, b):
    return pl.BlockSpec((1, a, b), lambda e, i: (e, 0, 0))


def experts(arrived, w_in, w_out):
    rows = arrived.shape[0]
    features, hidden = w_in.shape[1:]
    return pl.pallas_call(
        expert_kernel,
        grid=(2, rows // STEP),
        out_shape=[
            jax.ShapeDtypeStruct((rows, 2 * features), jnp.bfloat16),
            jax.ShapeDtypeStruct((2, rows, hidden), jnp.bfloat16),
            jax.ShapeDtypeStruct((2, rows, hidden), jnp.float32),
        ],
        in_specs=[lanes_of(features), one_of(features, hidden), one_of(hidden, features)],
        out_specs=[lanes_of(features), rows_of(hidden), rows_of(hidden)],
        compiler_params=ROOM,
        name="experts",
    )(arrived, w_in, w_out)


def expert_back_kernel(
    capacity, own_ref, x_ref, g_ref, ids_ref, in_ref, out_ref, router_ref, rise_ref, *refs
):
    pre_ref, arr_ref, outs, held = refs[0], refs[1], refs[2:6], refs[6]
    f32, bf16, i32 = jnp.float32, jnp.bfloat16, jnp.int32
    e = pl.program_id(0)
    own = own_ref[0] + e
    rows = x_ref.shape[0]
    step = 256

    def chunk(i, carry):
        at = pl.ds(pl.multiple_of(i * step, step), step)
        ids = ids_ref[at, :].astype(f32)
        lanes = lax.broadcasted_iota(i32, ids.shape, 1)
        other = jnp.sum(jnp.where(lanes == e, ids, 0.0), axis=1, keepdims=True).astype(i32) - own
        logits = lax.dot_general(
            x_ref[at, :], router_ref[...], LAST, preferred_element_type=f32
        )
        gate, _ = gate_pair(chosen_logit(logits, own), chosen_logit(logits, other))
        grown = (gate * g_ref[at, :].astype(f32)).astype(bf16)
        arr_ref[0, at, :] = grown
        back = lax.dot_general(grown, out_ref[0], LAST, preferred_element_type=f32)
        grad = (back * rise_ref[0, at, :]).astype(bf16)
        pre_ref[0, at, :] = grad
        held[at, :] = lax.dot_general(grad, in_ref[0], LAST, preferred_element_type=f32).astype(
            bf16
        )
        return carry

    lax.fori_loop(0, rows // step, chunk, 0)
    part = rows // 4
    here = lax.broadcasted_iota(i32, (part, rows), 0)
    there = lax.broadcasted_iota(i32, (part, rows), 1)
    block = (here * (65536 // capacity + 1)) >> 16
    for r, out in enumerate(outs):
        source = here + block * (3 * capacity) + r * capacity
        pick = (there == source).astype(f32).astype(bf16)
        out[...] = jnp.dot(pick, held[...], preferred_element_type=f32).astype(bf16)


def experts_back(own, arrived, grad_wide, w_in, w_out, router_w, rise, capacity):
    rows = arrived.shape[0]
    features, hidden = w_in.shape[1:]
    bf16 = jnp.bfloat16
    shape = jax.ShapeDtypeStruct
    part = rows // 4
    lanes = lambda n: pl.BlockSpec((rows, n), lambda e: (0, e))
    one = lambda a, b: pl.BlockSpec((1, a, b), lambda e: (e, 0, 0))
    return pl.pallas_call(
        functools.partial(expert_back_kernel, capacity),
        grid=(2,),
        out_shape=[shape((2, rows, hidden), bf16), shape((2, rows, features), bf16)]
        + [shape((2 * part, features), bf16)] * 4,
        in_specs=[
            SCALARS,
            lanes(features),
            lanes(features),
            pl.BlockSpec((rows, 128), lambda e: (0, 2 * features // 128)),
            one(features, hidden),
            one(hidden, features),
            pl.BlockSpec(router_w.shape, lambda e: (0, 0)),
            one(rows, hidden),
        ],
        out_specs=[one(rows, hidden), one(rows, features)]
        + [pl.BlockSpec((part, features), lambda e: (e, 0))] * 4,
        scratch_shapes=[pltpu.VMEM((rows, features), bf16)],
        compiler_params=ROOM,
        name="experts_back",
    )(own[None], arrived, grad_wide, grad_wide, w_in, w_out, router_w, rise)


def weight_grads_kernel(x_ref, pre_ref, act_ref, arr_ref, in_ref, out_ref):
    in_ref[0] = lax.dot_general(x_ref[...], pre_ref[0], FIRST, preferred_element_type=jnp.float32)
    out_ref[0] = lax.dot_general(act_ref[0], arr_ref[0], FIRST, preferred_element_type=jnp.float32)


def weight_grads(arrived, grad_pre, active, grad_arrived):
    rows = arrived.shape[0]
    hidden, features = grad_pre.shape[2], grad_arrived.shape[2]
    step = 256
    cuts = features // step
    whole = lambda n: pl.BlockSpec((1, rows, n), lambda e, j: (e, 0, 0))
    out = lambda n: pl.BlockSpec((1, step, n), lambda e, j: (e, j, 0))
    return pl.pallas_call(
        weight_grads_kernel,
        grid=(2, cuts),
        out_shape=[
            jax.ShapeDtypeStruct((2, features, hidden), jnp.float32),
            jax.ShapeDtypeStruct((2, hidden, features), jnp.float32),
        ],
        in_specs=[
            pl.BlockSpec((rows, step), lambda e, j: (0, e * cuts + j)),
            whole(hidden),
            pl.BlockSpec((1, rows, step), lambda e, j: (e, 0, j)),
            whole(features),
        ],
        out_specs=[out(hidden), out(features)],
        compiler_params=ROOM,
        cost_estimate=pl.CostEstimate(
            flops=8 * rows * features * hidden, bytes_accessed=20_000_000, transcendentals=0
        ),
        name="weight_grads",
    )(arrived, grad_pre, active, grad_arrived)


def sum_rows_kernel(capacity, *refs):
    pieces, out_ref = refs[:4], refs[-1]
    f32, bf16, i32 = jnp.float32, jnp.bfloat16, jnp.int32
    total = pieces[0][...].astype(f32)
    for piece in pieces[1:]:
        total = total + piece[...].astype(f32)
    rows = out_ref.shape[0]
    part = total.shape[0] // 2
    here = lax.broadcasted_iota(i32, (rows, 2 * part), 0)
    there = lax.broadcasted_iota(i32, (rows, 2 * part), 1)
    owner, q = here >> 4, here & 15
    second = q >= capacity
    source = owner * capacity + jnp.where(second, part + q - capacity, q)
    pick = ((there == source) & (q < 2 * capacity)).astype(f32).astype(bf16)
    out_ref[...] = jnp.dot(pick, total.astype(bf16), preferred_element_type=f32).astype(bf16)


def sum_rows(pieces, capacity, after):
    rows, features = pieces[0].shape
    return pl.pallas_call(
        functools.partial(sum_rows_kernel, capacity),
        out_shape=jax.ShapeDtypeStruct((rows // (2 * capacity) * 16, features), jnp.bfloat16),
        in_specs=[WHOLE] * 4 + [ANYWHERE] * len(after),
        out_specs=WHOLE,
        compiler_params=SOME,
        cost_estimate=pl.CostEstimate(
            flops=20000000000, bytes_accessed=60000000, transcendentals=0
        ),
        name="sum_rows",
    )(*pieces, *after)


def combine_kernel(places_ref, ids_ref, router_ref, ret_ref, *refs):
    f32, bf16 = jnp.float32, jnp.bfloat16
    grads, moes, outs = refs[:4], refs[4:8], refs[9:13]
    tokens, features = moes[0].shape
    rows = ret_ref.shape[0]
    row = lax.broadcasted_iota(jnp.int32, (rows, tokens), 0)
    tail_lane = lax.broadcasted_iota(jnp.int32, (tokens, 128), 1)
    for r in range(4):
        here = slice(r * tokens, (r + 1) * tokens)
        logits = lax.dot_general(
            moes[r][...], router_ref[...], LAST, preferred_element_type=f32
        )
        ids = [to_column(ids_ref[k : k + 1, here]) for k in range(2)]
        gates = gate_pair(chosen_logit(logits, ids[0]), chosen_logit(logits, ids[1]))
        total = jnp.zeros((tokens, features), f32)
        tail = jnp.zeros((tokens, 128), f32)
        grad = grads[r][:tokens, :].astype(f32)
        for k in range(2):
            got = jnp.zeros((tokens, features), f32)
            for e in range(2):
                pick = (row + e * rows == places_ref[k : k + 1, here]).astype(f32).astype(bf16)
                got = got + lax.dot_general(
                    pick,
                    ret_ref[:, e * features : (e + 1) * features],
                    FIRST,
                    preferred_element_type=f32,
                )
            total = total + gates[k] * got
            dots = jnp.sum(grad * got, axis=1, keepdims=True)
            high = dots.astype(bf16).astype(f32)
            tail = jnp.where(tail_lane == k, high, tail)
            tail = jnp.where(tail_lane == 2 + k, dots - high, tail)
        outs[r][:, :features] = total.astype(bf16)
        outs[r][:, features:] = tail.astype(bf16)


def combine(places, ids, router_w, returned, grads, moes, after):
    tokens, features = moes[0].shape
    return pl.pallas_call(
        combine_kernel,
        out_shape=[jax.ShapeDtypeStruct((tokens, features + 128), jnp.bfloat16)] * 4,
        in_specs=[WHOLE] * 12 + [ANYWHERE],
        out_specs=[WHOLE] * 4,
        compiler_params=SOME,
        name="combine",
    )(places, ids, router_w, returned, *grads, *moes, after)


def layer(
    tokens,
    seq_lengths,
    routes,
    gain_attn,
    w_query,
    w_key,
    w_value,
    w_output,
    rel_bias,
    gain_moe,
    w_router,
    w_in,
    w_out,
    cotangent,
):
    row_count, features = tokens.shape
    shard_rows = w_query.shape[0]
    expert_count = w_router.shape[1]
    bucket_count = rel_bias.shape[1]
    head_count = 4 * rel_bias.shape[0]
    capacity = 3 * row_count // expert_count
    f32 = jnp.float32
    bf16 = jnp.bfloat16

    shard = lax.axis_index("x").astype(jnp.int32)
    core = lax.axis_index("c").astype(jnp.int32)
    where = jnp.stack([shard, core])
    owners = expert_count // 2
    slot_rows = owners * 4 * capacity

    line = make_line(
        routes.T, jnp.stack([gain_attn, gain_moe]), rel_bias, w_router.T, cotangent
    )
    line_grads = along_x(line)
    sent = pack(core, (w_query, w_key, w_value), line)
    near = along_x(sent)[1:]
    def to_owners(outgoing):
        return lax.all_to_all(outgoing, ("y", "z", "c"), 0, 0, tiled=True)

    outgoing_grads, places, ids, spots, gains, bias_table, router_f = dispatch_grads(
        where,
        line_grads,
        slot_rows,
        capacity,
        row_count,
        expert_count,
        (head_count, bucket_count),
        line,
    )
    gain_one, gain_two = gains[0:1], gains[1:2]
    bias_table, router_w = bias_table.astype(bf16), router_f.astype(bf16)
    grad_wide = to_owners(outgoing_grads)
    near_out = along_x(hold_back(w_output, outgoing_grads))[1:]
    first_expert = 2 * lax.axis_index(("y", "z", "c")).astype(jnp.int32)

    segments = row_segments(seq_lengths[0], row_count)
    distance, onehot = position_tables(row_count, bucket_count)
    allowed = (segments[:, None] == segments[None, :]) & (distance >= 0)
    position_bias = jnp.einsum("ijb,hb->hij", onehot, bias_table, preferred_element_type=f32)
    masked_bias = jnp.where(allowed[None], position_bias, -1000000000.0)
    far = [swap_core(piece) for piece in near]
    hidden_one, queries, key_rows, value_rows, probs, attended, *full_qkv = attend(
        where,
        tokens,
        gain_one,
        masked_bias,
        (w_query, w_key, w_value),
        near,
        far,
    )
    middle, moe_in, full_out = to_middle(
        where, tokens, gain_two, attended, w_output, near_out
    )

    line_moe = along_x(moe_in)
    arrived = to_owners(dispatch(places, line_moe, slot_rows, grad_wide))
    ret, active, rise = experts(arrived, w_in, w_out)
    returned = to_owners(ret)
    grad_pre, grad_arrived, *blocks = experts_back(
        first_expert, arrived, grad_wide, w_in, w_out, router_w, rise, capacity
    )
    summed = [blocks[0]] + [shift_x(blocks[r], -r) for r in range(1, 4)]
    grad_w_in, grad_w_out = weight_grads(arrived, grad_pre, active, grad_arrived)
    bundle = combine(places, ids, router_w, returned, line_grads, line_moe, grad_w_in)
    back_rows = to_owners(sum_rows(summed, capacity, (grad_w_out, bundle[0])))
    homes = [bundle[0]] + [shift_x(bundle[r], -r) for r in range(1, 4)]
    result, grad_tokens, kept, given = backward(
        where,
        tokens,
        cotangent,
        gain_one,
        gain_two,
        ids,
        router_w,
        middle,
        moe_in,
        attended,
        hidden_one,
        queries,
        key_rows,
        value_rows,
        probs,
        spots,
        back_rows,
        *homes,
        *full_qkv,
        full_out,
    )
    piece = shard_rows // 8
    wide = features + 128
    paired = (kept.astype(f32) + swap_core(given).astype(f32)).astype(bf16)
    spread = lax.all_to_all(paired, ("y", "x", "z"), 0, 0, tiled=True)
    mine = jnp.sum(spread.reshape(64, piece, wide).astype(f32), axis=0).astype(bf16)
    half = lax.all_to_all(
        jnp.broadcast_to(mine[None], (16, piece, wide)).reshape(16 * piece, wide),
        ("y", "z"),
        0,
        0,
        tiled=True,
    )
    *totals, router_total, gain_totals, bias_total = finish(
        core[None], half, swap_core(half), shard_rows, expert_count, rel_bias.shape
    )
    router_total = router_total.T
    gain_one_total, gain_two_total = gain_totals[0], gain_totals[1]
    return (
        result,
        grad_tokens,
        gain_one_total,
        totals[0],
        totals[1],
        totals[2],
        totals[3],
        bias_total,
        gain_two_total,
        router_total,
        grad_w_in,
        grad_w_out,
    )


def solution(mesh):
    cube = Mesh(mesh.devices.reshape(4, 4, 2, 4), ("y", "z", "c", "x"))
    expert = ("y", "z", "c")
    everyone = ("y", "z", "c", "x")
    placed = (
        P(everyone, None),
        P(everyone, None),
        P(everyone, None),
        P("x"),
        P("x", None),
        P("x", None),
        P("x", None),
        P("x", None),
        P("x", None),
        P("x"),
        P("x", None),
        P(expert, None, "x"),
        P(expert, "x", None),
        P(everyone, None),
    )
    return jax.shard_map(
        layer,
        mesh=cube,
        in_specs=placed,
        out_specs=(
            P(everyone, None),
            P(everyone, None),
            P("x"),
            P("x", None),
            P("x", None),
            P("x", None),
            P("x", None),
            P("x", None),
            P("x"),
            P("x", None),
            P(expert, None, "x"),
            P(expert, "x", None),
        ),
        check_vma=False,
    )
```
